256 devices in a mesh: pts: 64 (over y, z, core), cols: 4 (over x).
Axes of the slice: x: 4, y: 4, z: 8, core: 2. Of those that a mesh axis runs over, the one named last changes fastest.
Arguments:
- start: float32 [65536, 512], P('pts', 'cols'), may hold values from -6 to 6
- cov_blocks: float32 [512, 8, 128, 128], P('pts')
- col_index: int32 [512, 8], P('pts'), may hold values from 0 to 511, as said below
- order: int32 [4], replicated, may hold values from 0 to 3, each once
Outputs:
- basis: float32 [65536, 512], P('pts', 'cols')
The draws below stay inside these ranges and needn't reach their ends.
Inputs may be any that keep to these rules, and one draw needn't show every extreme that they name: col_index[i, 0] = i; every other entry lies within cycle distance 8 of i (taken modulo 512); repeats may occur.
All inputs are finite; a program needn't handle non-finite values.
Results may differ from the reference program's by a relative error of at most 0.0001.
Values sent between devices are 32-bit elements; how exact they have to be, the bound alone decides.
A program may use at most 64 MiB of HBM per device.

```python
import math
import jax
import jax.numpy as jnp
from jax import lax

PB = 128
NB_ROW = 8
K = 512
ITERS = 1
NBLK = 512
NPTS = 65536
BAND = 8
N_COLS = 4


def draw_cov_blocks(key, part):
    key = jax.random.fold_in(key, 11)
    first, second = jax.random.split(key, 2)
    shape = (NBLK, NB_ROW, PB, PB)
    off = jax.random.normal(first, shape, jnp.float32) * 0.025
    level = jnp.exp(jax.random.uniform(second, (NBLK, PB), jnp.float32, math.log(3.0), math.log(30.0)))
    slot_zero = (jnp.arange(NB_ROW) == 0).astype(jnp.float32)
    identity = jnp.eye(PB, dtype=jnp.float32)
    return off + slot_zero[None, :, None, None] * identity[None, None, :, :] * level[:, None, :, None]


def draw_col_index(key, part):
    key = jax.random.fold_in(key, 23)
    offset = jax.random.randint(key, (NBLK, NB_ROW), -BAND, BAND + 1)
    slots = jnp.arange(NB_ROW)[None, :]
    offset = jnp.where(slots == 0, 0, offset)
    row_block = jnp.arange(NBLK)[:, None]
    return jnp.mod(row_block + offset, NBLK).astype(jnp.int32)


def level_of(stream_key, dims, cuts, smallest, top_value):
    gain, own = 1.0, jax.random.fold_in(stream_key, 6)
    for position, parts in cuts:
        heights = jnp.exp(jax.random.uniform(jax.random.fold_in(own, position), (parts,), jnp.float32, smallest / len(cuts), top_value / len(cuts)))
        gain = gain * jnp.repeat(heights, dims[position] // parts).reshape([-1 if axis == position else 1 for axis in range(len(dims))])
    return gain


def centred(stream_key, shape, deviation, most, pieces=(), held_as=jnp.bfloat16):
    array = jax.random.normal(stream_key, shape, jnp.float32) * deviation
    if len(pieces) > 0:
        array = level_of(stream_key, shape, pieces, -0.22, 0.18) * array
    return jnp.clip(array, min=-most, max=most).astype(held_as)


def setup_inputs(seed: int = 0) -> dict:
    key_of = jax.random.split(jax.random.key(seed), 5)
    start = centred(key_of[0], (NPTS, K), 1.0, 6.0, ((0, 64), (1, 4)), jnp.float32)
    cov_blocks = draw_cov_blocks(jax.random.fold_in(key_of[4], 71), 0)
    col_index = draw_col_index(jax.random.fold_in(key_of[4], 71), 0)
    order = jax.random.permutation(key_of[3], N_COLS).astype(jnp.int32)
    return dict(start=start, cov_blocks=cov_blocks, col_index=col_index, order=order)


def inner(left, right):
    return lax.dot_general(left.astype(jnp.float32), right.astype(jnp.float32), (((0,), (0,)), ((), ())), precision=lax.Precision.HIGHEST, preferred_element_type=jnp.float32)

def schmidt(whole, order, groups, group_size):
    width = whole.shape[1]
    positions = jnp.arange(groups, dtype=jnp.int32)
    ranks = jnp.sum(positions[:, None] * (order[:, None] == positions[None, :]).astype(jnp.int32), axis=0)
    column_group = (jnp.arange(width, dtype=jnp.int32) // group_size).astype(jnp.int32)
    col_rank = jnp.sum(jnp.where(column_group[:, None] == positions[None, :], ranks[None, :], 0), axis=1)
    for step in range(groups):
        owner = order[step]
        current = lax.dynamic_slice_in_dim(whole, (owner * group_size).astype(jnp.int32), group_size, 1)
        gram = inner(current, current)
        lower = jnp.linalg.cholesky(gram)
        ortho = lax.linalg.triangular_solve(lower, current, left_side=False, lower=True, transpose_a=True)
        coef = inner(ortho, whole)
        updated = whole - jnp.dot(ortho.astype(jnp.float32), coef.astype(jnp.float32), precision=lax.Precision.HIGHEST, preferred_element_type=jnp.float32)
        tiled = jnp.tile(ortho, (1, groups))
        whole = jnp.where((col_rank > step)[None, :], updated, jnp.where((column_group == owner)[None, :], tiled, whole))
    return whole

def reference(start, cov_blocks, col_index, order):
    nblk = cov_blocks.shape[0]
    block = cov_blocks.shape[2]
    width = start.shape[1]
    groups = order.shape[0]
    group_size = width // groups
    basis = start
    for sweep in range(ITERS):
        tiles = basis.reshape(nblk, block, width)

        def one_row(pair):
            blocks, columns = pair
            picked = tiles[columns]
            return jnp.einsum('sab,sbk->ak', blocks, picked, precision=lax.Precision.HIGHEST)
        image = lax.map(one_row, (cov_blocks, col_index)).reshape(nblk * block, width)
        basis = schmidt(image, order, groups, group_size)
    return basis
```

```python
import jax
import jax.numpy as jnp
from jax import lax
from jax.experimental import pallas as pl
from jax.experimental.pallas import tpu as pltpu
from jax.sharding import PartitionSpec as P

MESH = pl.DeviceIdType.MESH
F32 = jnp.float32
BF16 = jnp.bfloat16
GROUPS = 4
WIDTH = 128
BLOCK = 128
ROW_BLOCKS = 8
SLOTS = 8
NBLK = 512
YS, ZS, CORES = 4, 8, 2
COLS = GROUPS * WIDTH
ROWS = ROW_BLOCKS * BLOCK
HALF = ROW_BLOCKS // 2
PIECE = 3 * WIDTH // CORES // ZS
TOLERANCE = 1e-4


def broadcast(value, axis, source):
    kept = jnp.where(lax.axis_index(axis) == source, value, 0).astype(value.dtype)
    return lax.psum(kept, axis)


def with_halo(cells, axis, width):
    count = lax.axis_size(axis)
    head = lax.slice_in_dim(cells, 0, width, axis=0)
    tail = lax.slice_in_dim(cells, cells.shape[0] - width, cells.shape[0], axis=0)
    return jnp.concatenate(
        [
            lax.ppermute(tail, axis, [(i, (i + 1) % count) for i in range(count)]),
            cells,
            lax.ppermute(head, axis, [((i + 1) % count, i) for i in range(count)]),
        ],
        axis=0,
    )


def inner(left, right):
    return lax.dot_general(
        left,
        right,
        (((0,), (0,)), ((), ())),
        precision=lax.Precision.HIGHEST,
        preferred_element_type=F32,
    )


def careful(start, cov_blocks, col_index, order):
    rows, group_size = start.shape
    blocks_dev = cov_blocks.shape[0]
    block = cov_blocks.shape[2]
    total_blocks = blocks_dev * lax.axis_size("pts")
    groups = lax.axis_size("cols")
    mine = lax.axis_index("cols")
    positions = jnp.arange(groups, dtype=jnp.int32)
    rank = jnp.sum(jnp.where(order == mine, positions, 0))
    first_block = lax.axis_index("pts") * blocks_dev - blocks_dev
    relative = jnp.mod(col_index - first_block, total_blocks)
    tiles = with_halo(start, "pts", rows).reshape(3 * blocks_dev, block, group_size)[relative]
    local = jnp.einsum(
        "rsab,rsbk->rak", cov_blocks, tiles, precision=lax.Precision.HIGHEST
    ).reshape(rows, group_size)

    def step(t, local):
        owner = order[t]
        gram = lax.psum(inner(local, local), "pts")
        lower = jnp.linalg.cholesky(gram)
        candidate = lax.linalg.triangular_solve(
            lower, local, left_side=False, lower=True, transpose_a=True
        )
        ortho = broadcast(candidate, "cols", owner)
        coef = lax.psum(inner(ortho, local), "pts")
        updated = local - jnp.dot(
            ortho, coef, precision=lax.Precision.HIGHEST, preferred_element_type=F32
        )
        return jnp.where(rank > t, updated, jnp.where(mine == owner, ortho, local))

    return lax.fori_loop(0, groups, step, local)


def split(x):
    high = x.astype(BF16)
    return high, (x - high.astype(F32)).astype(BF16)


def quarters(q, m, n):
    return (q[:m, :n] + q[m:, n:]) + (q[:m, n:] + q[m:, :n])


def dot(a, b):
    return jnp.dot(a, b, preferred_element_type=F32)


def dot_t(a, b):
    return lax.dot_general(a, b, (((0,), (0,)), ((), ())), preferred_element_type=F32)


def kernel(
    start, cov, col_index, order, out, residual,
    win, win_hl, covv, cov_hl, vall, vhl, tb, r1, s1, r2, r3, gb,
    e0, w, b, u, mk, e0_h, e0_l, w_h, w_l, b_h, b_l, u_h, x_hl, res, scol,
    c_sem, l_sem, o_sem, f_sem,
    halo_s, halo_r, left_s, right_s, fwdr_s, fwdl_s, next_r, prev_r, opp_r,
    p1_s, p1_r, p2_s, p2_r, p3_s, p3_r, p4_s, p4_r, p5_s, p5_r, p6_s, p6_r,
):
    p = lax.axis_index("pts")
    g = lax.axis_index("cols")
    npts = YS * ZS * CORES
    c = lax.rem(p, CORES)
    z = lax.rem(lax.div(p, CORES), ZS)
    y = lax.div(p, CORES * ZS)
    before, after = lax.rem(p + npts - 1, npts), lax.rem(p + 1, npts)
    sibling = p + 1 - 2 * c
    g_next, g_prev, g_opp = (lax.rem(g + k, GROUPS) for k in (1, 3, 2))

    def at_z(k):
        return p + (lax.rem(z + k, ZS) - z) * CORES

    def at_y(k):
        return p + (lax.rem(y + k, YS) - y) * (CORES * ZS)

    def remote(src, dst, send, recv, **where):
        return pltpu.make_async_remote_copy(
            src_ref=src, dst_ref=dst, send_sem=send, recv_sem=recv,
            device_id=where, device_id_type=MESH,
        )

    def cov_copy(r):
        return pltpu.make_async_copy(cov.at[r], covv.at[r], c_sem.at[r])

    own_copy = pltpu.make_async_copy(start, win.at[1], l_sem)
    own_copy.start()

    def start_cov(r, carry):
        cov_copy(r).start()
        return carry

    lax.fori_loop(0, ROW_BLOCKS, start_cov, 0)

    barrier = pltpu.get_barrier_semaphore()
    peers = [dict(pts=before), dict(pts=after)]
    peers += [dict(cols=h) for h in (g_next, g_prev, g_opp)]
    peers += [dict(pts=at_z(k)) for k in range(1, ZS)]
    peers += [dict(pts=at_y(k)) for k in range(1, YS)]
    for peer in peers:
        pl.semaphore_signal(barrier, inc=1, device_id=peer, device_id_type=MESH)
    pl.semaphore_wait(barrier, len(peers))

    to_after = remote(start, win.at[0], halo_s.at[0], halo_r.at[0], pts=after)
    to_before = remote(start, win.at[2], halo_s.at[1], halo_r.at[1], pts=before)
    to_after.start()
    to_before.start()

    ranks = []
    for a in range(GROUPS):
        rank = jnp.int32(0)
        for t in range(1, GROUPS):
            rank += jnp.where(order[t] == a, t, 0)
        ranks.append(rank)
    row_id = lax.broadcasted_iota(jnp.int32, (WIDTH, WIDTH), 0)
    col_id = lax.broadcasted_iota(jnp.int32, (WIDTH, WIDTH), 1)
    eye = (row_id == col_id).astype(F32)
    upper = (row_id < col_id).astype(F32) + 0.5 * eye
    for a in range(GROUPS):
        for h in range(GROUPS):
            rows, cols = slice(a * WIDTH, (a + 1) * WIDTH), slice(h * WIDTH, (h + 1) * WIDTH)
            if a == h:
                mk[rows, cols] = upper
            else:
                ahead = jnp.where(ranks[a] < ranks[h], 1.0, 0.0).astype(F32)
                mk[rows, cols] = jnp.full((WIDTH, WIDTH), ahead, F32)

    def split_cov(r, carry):
        cov_copy(r).wait()
        for s in range(SLOTS):
            high, low = split(covv[r, s])
            cov_hl[r, :BLOCK, s * BLOCK:(s + 1) * BLOCK] = high
            cov_hl[r, BLOCK:, s * BLOCK:(s + 1) * BLOCK] = low
        return carry

    lax.fori_loop(0, ROW_BLOCKS, split_cov, 0)

    def split_window(side):
        def one(k, carry):
            rows = pl.ds(pl.multiple_of(k * BLOCK, BLOCK), BLOCK)
            high, low = split(win[side, rows, :])
            win_hl[side * ROW_BLOCKS + k, :, :WIDTH] = high
            win_hl[side * ROW_BLOCKS + k, :, WIDTH:] = low
            return carry

        lax.fori_loop(0, ROW_BLOCKS, one, 0)

    own_copy.wait()
    split_window(1)
    to_after.wait_recv()
    split_window(0)
    to_before.wait_recv()
    split_window(2)

    base = p * ROW_BLOCKS - ROW_BLOCKS - NBLK

    def rows_of(src, i):
        r = lax.rem(i + HALF * (1 - lax.div(src, 2)), ROW_BLOCKS)
        return r, pl.ds(pl.multiple_of(r * BLOCK, BLOCK), BLOCK)

    def xcopy(src, i, send, recv, to):
        ref = vall.at[src, rows_of(src, i)[1], :]
        return remote(ref, ref, send.at[i], recv.at[i], cols=to)

    def own_left(i):
        return xcopy(g, i, left_s, next_r, g_prev)

    def own_right(i):
        return xcopy(g, i, right_s, prev_r, g_next)

    def forward_right(i):
        return xcopy(g_prev, i, fwdr_s, opp_r, g_next)

    def forward_left(i):
        return xcopy(g_next, i, fwdl_s, opp_r, g_prev)

    def from_opp(i):
        return xcopy(g_opp, i, fwdr_s, opp_r, g_next)

    def keep_split(src, i):
        rows = rows_of(src, i)[1]
        high, low = split(vall[src, rows, :])
        vhl[src, rows, :WIDTH] = high
        vhl[src, rows, WIDTH:] = low

    def image(i, carry):
        r, rows = rows_of(g, i)
        tiles = []
        for s in range(SLOTS):
            rel = lax.rem(col_index[r, s] - base, NBLK)
            tiles.append(win_hl[lax.min(rel, 3 * ROW_BLOCKS - 1)])
        quad = dot(cov_hl[r], jnp.concatenate(tiles, axis=0))
        vall[g, rows, :] = quarters(quad, BLOCK, WIDTH)
        own_left(i).start()

        @pl.when(i < HALF)
        def _():
            own_right(i).start()

        keep_split(g, i)
        return carry

    lax.fori_loop(0, ROW_BLOCKS, image, 0)

    def pass_right(i, carry):
        own_copy_in = xcopy(g_prev, i, right_s, prev_r, g_next)
        own_copy_in.wait_recv()
        forward_right(i).start()
        keep_split(g_prev, i)
        return carry

    lax.fori_loop(0, HALF, pass_right, 0)

    def rest_right(i, carry):
        own_right(i).start()
        return carry

    lax.fori_loop(HALF, ROW_BLOCKS, rest_right, 0)

    def half_of(src, k):
        return pl.ds(pl.multiple_of(lax.rem(k + 1 - lax.div(src, 2), 2) * (HALF * BLOCK), HALF * BLOCK), HALF * BLOCK)

    def gram_half(src, k):
        rows = half_of(src, k)
        return quarters(dot_t(vhl[g, rows, :], vhl[src, rows, :]), WIDTH, WIDTH)

    gram_own = gram_half(g, 0) + gram_half(g, 1)
    tb[0, :WIDTH, :] = gram_own

    def take_next(i, carry):
        xcopy(g_next, i, left_s, next_r, g_prev).wait_recv()

        @pl.when(i >= HALF)
        def _():
            forward_left(i).start()

        keep_split(g_next, i)
        return carry

    lax.fori_loop(0, HALF, take_next, 0)
    first = gram_half(g_next, 0)

    def take_opp(i, carry):
        from_opp(i).wait_recv()
        keep_split(g_opp, i)
        return carry

    lax.fori_loop(HALF, ROW_BLOCKS, take_next, 0)
    gram_next = first + gram_half(g_next, 1)
    lax.fori_loop(0, HALF, take_opp, 0)
    gram_opp = gram_half(g_opp, 0)
    edge = 3 * WIDTH // 2 - WIDTH
    tb[0, WIDTH:, :] = gram_next[:edge]
    tb[1, :WIDTH - edge, :] = gram_next[edge:]
    tb[1, WIDTH - edge:, :] = gram_opp

    to_core = remote(tb.at[1 - c], r1, p1_s, p1_r, pts=sibling)
    to_core.start()
    to_core.wait_recv()
    s1[...] = (tb[c] + r1[...]).reshape(ZS, PIECE, WIDTH)

    def z_send(k):
        to = lax.rem(z + k, ZS)
        return remote(s1.at[to], r2.at[z], p2_s.at[k], p2_r.at[z], pts=at_z(k))

    def z_recv(k):
        source = lax.rem(z + k, ZS)
        return remote(s1.at[source], r2.at[source], p2_s.at[k], p2_r.at[source], pts=at_z(k))

    for k in range(1, ZS):
        z_send(k).start()
    total = s1[z]
    for k in range(1, ZS):
        z_recv(k).wait_recv()
        total += r2[lax.rem(z + k, ZS)]
    r3[y] = total

    def y_send(k):
        return remote(r3.at[y], r3.at[y], p3_s.at[k], p3_r.at[y], pts=at_y(k))

    def y_recv(k):
        source = lax.rem(y + k, YS)
        return remote(r3.at[source], r3.at[source], p3_s.at[k], p3_r.at[source], pts=at_y(k))

    for k in range(1, YS):
        y_send(k).start()
    for k in range(1, YS):
        y_recv(k).wait_recv()
    gb[g, c, z] = (r3[0] + r3[1]) + (r3[2] + r3[3])

    def z_share(k):
        ref = gb.at[g, c, z]
        return remote(ref, ref, p4_s.at[k], p4_r.at[z], pts=at_z(k))

    def z_shared(k):
        source = lax.rem(z + k, ZS)
        ref = gb.at[g, c, source]
        return remote(ref, ref, p4_s.at[k], p4_r.at[source], pts=at_z(k))

    for k in range(1, ZS):
        z_share(k).start()

    def rest(i, carry):
        xcopy(g_prev, i, right_s, prev_r, g_next).wait_recv()
        keep_split(g_prev, i)
        return carry

    for k in range(1, ZS):
        z_shared(k).wait_recv()

    def x_share(k):
        ref = gb.at[g, c]
        return remote(ref, ref, p5_s.at[k], p5_r.at[g], cols=lax.rem(g + k, GROUPS))

    def x_shared(k):
        source = lax.rem(g + k, GROUPS)
        ref = gb.at[source, c]
        return remote(ref, ref, p5_s.at[k], p5_r.at[source], cols=source)

    def core_share(k):
        source = lax.rem(g + k, GROUPS)
        ref = gb.at[source, c]
        return remote(ref, ref, p6_s.at[source], p6_r.at[source], pts=sibling)

    def core_shared(k):
        source = lax.rem(g + k, GROUPS)
        ref = gb.at[source, 1 - c]
        return remote(ref, ref, p6_s.at[source], p6_r.at[source], pts=sibling)

    for k in range(1, GROUPS):
        x_share(k).start()
    core_share(0).start()
    lax.fori_loop(HALF, ROW_BLOCKS, rest, 0)
    lax.fori_loop(HALF, ROW_BLOCKS, take_opp, 0)
    for k in range(1, GROUPS):
        x_shared(k).wait_recv()
        core_share(k).start()
    for k in range(GROUPS):
        core_shared(k).wait_recv()

    parts = [gb[a].reshape(3 * WIDTH, WIDTH) for a in range(GROUPS)]
    diag = [parts[a][:WIDTH] for a in range(GROUPS)]
    down = [lax.rsqrt(jnp.sum(d * eye, axis=1, keepdims=True)) for d in diag]
    across = [lax.rsqrt(jnp.sum(d * eye, axis=0, keepdims=True)) for d in diag]

    def put(a, h, block):
        rows, cols = slice(a * WIDTH, (a + 1) * WIDTH), slice(h * WIDTH, (h + 1) * WIDTH)
        block = block * down[a] * across[h]
        if a == h:
            block = block - eye
        high, low = split(block)
        e0[rows, cols] = block
        e0_h[rows, cols] = high
        e0_l[rows, cols] = low
        block = -(mk[rows, cols] * block)
        w[rows, cols] = block
        high, low = split(block)
        w_h[rows, cols] = high
        w_l[rows, cols] = low

    for a in range(GROUPS):
        scol[a * WIDTH:(a + 1) * WIDTH, :] = jnp.broadcast_to(down[a], (WIDTH, WIDTH))
        put(a, a, diag[a])
        h = (a + 1) % GROUPS
        block = parts[a][WIDTH:2 * WIDTH]
        put(a, h, block)
        put(h, a, block.T)
    for a in range(GROUPS // 2):
        h = a + GROUPS // 2
        block = parts[a][2 * WIDTH:] + parts[h][2 * WIDTH:].T
        put(a, h, block)
        put(h, a, block.T)

    def tile(m):
        return pl.ds(pl.multiple_of(m * WIDTH, WIDTH), WIDTH)

    def newton(fine):
        def first(m, carry):
            rows = tile(m)
            prod = dot(e0_h[rows, :], w_h[...])
            if fine:
                prod += dot(e0_l[rows, :], w_h[...]) + dot(e0_h[rows, :], w_l[...])
            value = (e0[rows, :] + w[rows, :]) + prod
            b[rows, :] = value
            high, low = split(value)
            b_h[rows, :] = high
            if fine:
                b_l[rows, :] = low
            return carry

        def second(m, carry):
            rows = tile(m)
            prod = dot_t(w_h[:, rows], b_h[...])
            if fine:
                prod += dot_t(w_l[:, rows], b_h[...]) + dot_t(w_h[:, rows], b_l[...])
            here = lax.broadcasted_iota(jnp.int32, (WIDTH, COLS), 0) + m * WIDTH
            there = lax.broadcasted_iota(jnp.int32, (WIDTH, COLS), 1)
            own = jnp.where(here == there, w[rows, :], 0.0)
            value = mk[rows, :] * ((b[rows, :] + own) + prod)
            u[rows, :] = value
            u_h[rows, :] = value.astype(BF16)
            if fine:
                res[...] += jnp.sum((value * value).reshape(WIDTH // 8, 8, COLS), axis=0)
            return carry

        def third(m, carry):
            rows = tile(m)
            value = (w[rows, :] - u[rows, :]) - dot(w_h[rows, :], u_h[...])
            w[rows, :] = value
            high, low = split(value)
            w_h[rows, :] = high
            w_l[rows, :] = low
            return carry

        lax.fori_loop(0, GROUPS, first, 0)
        lax.fori_loop(0, GROUPS, second, 0)
        lax.fori_loop(0, GROUPS, third, 0)

    res[...] = jnp.zeros_like(res)
    newton(False)
    newton(False)
    newton(True)
    residual[...] = jnp.full(residual.shape, jnp.sum(res[...]), F32)

    mine = pl.ds(pl.multiple_of(g * WIDTH, WIDTH), WIDTH)
    for a in range(GROUPS):
        rows = slice(a * WIDTH, (a + 1) * WIDTH)
        same = jnp.where(g == a, 1.0, 0.0).astype(F32)
        high, low = split(scol[rows, :] * (w[rows, mine] + same * eye))
        x_hl[rows, :WIDTH] = high
        x_hl[rows, WIDTH:] = low

    outv = win

    def result(k):
        rows = pl.ds(pl.multiple_of(k * 2 * BLOCK, 2 * BLOCK), 2 * BLOCK)
        return pltpu.make_async_copy(outv.at[1, rows, :], out.at[rows, :], f_sem.at[k])

    def finish(k, carry):
        rows = pl.ds(pl.multiple_of(k * 2 * BLOCK, 2 * BLOCK), 2 * BLOCK)
        high = jnp.concatenate([vhl[h, rows, :WIDTH] for h in range(GROUPS)], axis=1)
        low = jnp.concatenate([vhl[h, rows, WIDTH:] for h in range(GROUPS)], axis=1)
        q = dot(jnp.concatenate([high, low], axis=0), x_hl[...])
        outv[1, rows, :] = quarters(q, 2 * BLOCK, WIDTH)
        result(k).start()
        return carry

    lax.fori_loop(0, ROW_BLOCKS // 2, finish, 0)

    to_after.wait_send()
    to_before.wait_send()

    def sent(i, carry):
        own_left(i).wait_send()
        own_right(i).wait_send()
        return carry

    def sent_on(i, carry):
        forward_right(i).wait_send()
        forward_left(i + HALF).wait_send()
        return carry

    lax.fori_loop(0, ROW_BLOCKS, sent, 0)
    lax.fori_loop(0, HALF, sent_on, 0)
    to_core.wait_send()
    for k in range(1, ZS):
        z_send(k).wait_send()
        z_share(k).wait_send()
    for k in range(1, YS):
        y_send(k).wait_send()
    for k in range(1, GROUPS):
        x_share(k).wait_send()
    for k in range(GROUPS):
        core_share(k).wait_send()

    def written(k, carry):
        result(k).wait()
        return carry

    lax.fori_loop(0, ROW_BLOCKS // 2, written, 0)


def fast(start, cov_blocks, col_index, order):
    dma = pltpu.SemaphoreType.DMA
    square = (COLS, COLS)
    hbm = pl.BlockSpec(memory_space=pl.ANY)
    smem = pl.BlockSpec(memory_space=pltpu.SMEM)
    return pl.pallas_call(
        kernel,
        out_shape=(
            jax.ShapeDtypeStruct((ROWS, WIDTH), F32),
            jax.ShapeDtypeStruct((8, 128), F32),
        ),
        in_specs=[hbm, hbm, smem, smem],
        out_specs=(hbm, pl.BlockSpec(memory_space=pltpu.VMEM)),
        scratch_shapes=[
            pltpu.VMEM((3, ROWS, WIDTH), F32),
            pltpu.VMEM((3 * ROW_BLOCKS, BLOCK, 2 * WIDTH), BF16),
            pltpu.VMEM((ROW_BLOCKS, SLOTS, BLOCK, BLOCK), F32),
            pltpu.VMEM((ROW_BLOCKS, 2 * BLOCK, SLOTS * BLOCK), BF16),
            pltpu.VMEM((GROUPS, ROWS, WIDTH), F32),
            pltpu.VMEM((GROUPS, ROWS, 2 * WIDTH), BF16),
            pltpu.VMEM((CORES, ZS * PIECE, WIDTH), F32),
            pltpu.VMEM((ZS * PIECE, WIDTH), F32),
            pltpu.VMEM((ZS, PIECE, WIDTH), F32),
            pltpu.VMEM((ZS, PIECE, WIDTH), F32),
            pltpu.VMEM((YS, PIECE, WIDTH), F32),
            pltpu.VMEM((GROUPS, CORES, ZS, PIECE, WIDTH), F32),
            pltpu.VMEM(square, F32),
            pltpu.VMEM(square, F32),
            pltpu.VMEM(square, F32),
            pltpu.VMEM(square, F32),
            pltpu.VMEM(square, F32),
            pltpu.VMEM(square, BF16),
            pltpu.VMEM(square, BF16),
            pltpu.VMEM(square, BF16),
            pltpu.VMEM(square, BF16),
            pltpu.VMEM(square, BF16),
            pltpu.VMEM(square, BF16),
            pltpu.VMEM(square, BF16),
            pltpu.VMEM((COLS, 2 * WIDTH), BF16),
            pltpu.VMEM((8, COLS), F32),
            pltpu.VMEM((COLS, WIDTH), F32),
            dma((ROW_BLOCKS,)),
            dma,
            dma,
            dma((ROW_BLOCKS // 2,)),
            dma((2,)), dma((2,)),
            dma((ROW_BLOCKS,)), dma((ROW_BLOCKS,)),
            dma((ROW_BLOCKS,)), dma((ROW_BLOCKS,)),
            dma((ROW_BLOCKS,)), dma((ROW_BLOCKS,)), dma((ROW_BLOCKS,)),
            dma, dma,
            dma((ZS,)), dma((ZS,)),
            dma((YS,)), dma((YS,)),
            dma((ZS,)), dma((ZS,)),
            dma((GROUPS,)), dma((GROUPS,)),
            dma((GROUPS,)), dma((GROUPS,)),
        ],
        compiler_params=pltpu.CompilerParams(
            collective_id=0, has_side_effects=True, vmem_limit_bytes=56 * 1024 * 1024
        ),
    )(start, cov_blocks, col_index, order)


def body(start, cov_blocks, col_index, order):
    result, residual = fast(start, cov_blocks, col_index, order)
    return lax.cond(
        residual[0, 0] < TOLERANCE,
        lambda: result,
        lambda: careful(start, cov_blocks, col_index, order),
    )


def solution(mesh):
    placed = (P("pts", "cols"), P("pts", None, None, None), P("pts", None), P())
    return jax.shard_map(
        body, mesh=mesh, in_specs=placed, out_specs=P("pts", "cols"), check_vma=False
    )
```

```python
import jax
import jax.numpy as jnp
from jax import lax
from jax.experimental import pallas as pl
from jax.experimental.pallas import tpu as pltpu
from jax.sharding import PartitionSpec as P

MESH = pl.DeviceIdType.MESH
F32 = jnp.float32
BF16 = jnp.bfloat16
GROUPS = 4
WIDTH = 128
BLOCK = 128
ROW_BLOCKS = 8
SLOTS = 8
NBLK = 512
YS, ZS, CORES = 4, 8, 2
COLS = GROUPS * WIDTH
ROWS = ROW_BLOCKS * BLOCK
HALF = ROW_BLOCKS // 2
PIECE = 3 * WIDTH // CORES // ZS
TOLERANCE = 1e-4


def total(value, axis):
    distance = 1
    while distance < lax.axis_size(axis):
        pairs = [(i, i ^ distance) for i in range(lax.axis_size(axis))]
        value = value + lax.ppermute(value, axis, pairs)
        distance *= 2
    return value


def broadcast(value, axis, source):
    kept = jnp.where(lax.axis_index(axis) == source, value, 0).astype(value.dtype)
    return total(kept, axis)


def with_halo(cells, axis, width):
    count = lax.axis_size(axis)
    head = lax.slice_in_dim(cells, 0, width, axis=0)
    tail = lax.slice_in_dim(cells, cells.shape[0] - width, cells.shape[0], axis=0)
    return jnp.concatenate(
        [
            lax.ppermute(tail, axis, [(i, (i + 1) % count) for i in range(count)]),
            cells,
            lax.ppermute(head, axis, [((i + 1) % count, i) for i in range(count)]),
        ],
        axis=0,
    )


def inner(left, right):
    return lax.dot_general(
        left,
        right,
        (((0,), (0,)), ((), ())),
        precision=lax.Precision.HIGHEST,
        preferred_element_type=F32,
    )


def careful(start, cov_blocks, col_index, order):
    rows, group_size = start.shape
    blocks_dev = cov_blocks.shape[0]
    block = cov_blocks.shape[2]
    total_blocks = blocks_dev * lax.axis_size("pts")
    groups = lax.axis_size("cols")
    mine = lax.axis_index("cols")
    positions = jnp.arange(groups, dtype=jnp.int32)
    rank = jnp.sum(jnp.where(order == mine, positions, 0))
    first_block = lax.axis_index("pts") * blocks_dev - blocks_dev
    relative = jnp.mod(col_index - first_block, total_blocks)
    tiles = with_halo(start, "pts", rows).reshape(3 * blocks_dev, block, group_size)[relative]
    local = jnp.einsum(
        "rsab,rsbk->rak", cov_blocks, tiles, precision=lax.Precision.HIGHEST
    ).reshape(rows, group_size)

    def step(t, local):
        owner = order[t]
        gram = total(inner(local, local), "pts")
        lower = jnp.linalg.cholesky(gram)
        candidate = lax.linalg.triangular_solve(
            lower, local, left_side=False, lower=True, transpose_a=True
        )
        ortho = broadcast(candidate, "cols", owner)
        coef = total(inner(ortho, local), "pts")
        updated = local - jnp.dot(
            ortho, coef, precision=lax.Precision.HIGHEST, preferred_element_type=F32
        )
        return jnp.where(rank > t, updated, jnp.where(mine == owner, ortho, local))

    return lax.fori_loop(0, groups, step, local)


def split(x):
    high = x.astype(BF16)
    return high, (x - high.astype(F32)).astype(BF16)


def quarters(q, m, n):
    return (q[:m, :n] + q[m:, n:]) + (q[:m, n:] + q[m:, :n])


def dot(a, b):
    return jnp.dot(a, b, preferred_element_type=F32)


def dot_t(a, b):
    return lax.dot_general(a, b, (((0,), (0,)), ((), ())), preferred_element_type=F32)


def kernel(
    start, cov, col_index, order, out, residual,
    win, win_hl, covv, cov_hl, vall, vhl, tb, r1, s1, r2, r3, gb,
    e0, w, b, u, mk, e0_h, e0_l, w_h, w_l, b_h, b_l, u_h, x_hl, res, scol,
    c_sem, l_sem, o_sem, f_sem,
    halo_s, halo_r, left_s, right_s, fwdr_s, fwdl_s, next_r, prev_r, opp_r,
    p1_s, p1_r, p2_s, p2_r, p3_s, p3_r, p4_s, p4_r, p5_s, p5_r, p6_s, p6_r,
):
    p = lax.axis_index("pts")
    g = lax.axis_index("cols")
    npts = YS * ZS * CORES
    c = lax.rem(p, CORES)
    z = lax.rem(lax.div(p, CORES), ZS)
    y = lax.div(p, CORES * ZS)
    before, after = lax.rem(p + npts - 1, npts), lax.rem(p + 1, npts)
    sibling = p + 1 - 2 * c
    g_next, g_prev, g_opp = (lax.rem(g + k, GROUPS) for k in (1, 3, 2))

    def at_z(k):
        return p + (lax.rem(z + k, ZS) - z) * CORES

    def at_y(k):
        return p + (lax.rem(y + k, YS) - y) * (CORES * ZS)

    def remote(src, dst, send, recv, **where):
        return pltpu.make_async_remote_copy(
            src_ref=src, dst_ref=dst, send_sem=send, recv_sem=recv,
            device_id=where, device_id_type=MESH,
        )

    def cov_copy(r):
        return pltpu.make_async_copy(cov.at[r], covv.at[r], c_sem.at[r])

    own_copy = pltpu.make_async_copy(start, win.at[1], l_sem)
    own_copy.start()

    def start_cov(r, carry):
        cov_copy(r).start()
        return carry

    lax.fori_loop(0, ROW_BLOCKS, start_cov, 0)

    barrier = pltpu.get_barrier_semaphore()
    peers = [dict(pts=before), dict(pts=after)]
    peers += [dict(cols=h) for h in (g_next, g_prev, g_opp)]
    peers += [dict(pts=at_z(k)) for k in range(1, ZS)]
    peers += [dict(pts=at_y(k)) for k in range(1, YS)]
    for peer in peers:
        pl.semaphore_signal(barrier, inc=1, device_id=peer, device_id_type=MESH)
    pl.semaphore_wait(barrier, len(peers))

    to_after = remote(start, win.at[0], halo_s.at[0], halo_r.at[0], pts=after)
    to_before = remote(start, win.at[2], halo_s.at[1], halo_r.at[1], pts=before)
    to_after.start()
    to_before.start()

    ranks = []
    for a in range(GROUPS):
        rank = jnp.int32(0)
        for t in range(1, GROUPS):
            rank += jnp.where(order[t] == a, t, 0)
        ranks.append(rank)
    row_id = lax.broadcasted_iota(jnp.int32, (WIDTH, WIDTH), 0)
    col_id = lax.broadcasted_iota(jnp.int32, (WIDTH, WIDTH), 1)
    eye = (row_id == col_id).astype(F32)
    upper = (row_id < col_id).astype(F32) + 0.5 * eye
    for a in range(GROUPS):
        for h in range(GROUPS):
            rows, cols = slice(a * WIDTH, (a + 1) * WIDTH), slice(h * WIDTH, (h + 1) * WIDTH)
            if a == h:
                mk[rows, cols] = upper
            else:
                ahead = jnp.where(ranks[a] < ranks[h], 1.0, 0.0).astype(F32)
                mk[rows, cols] = jnp.full((WIDTH, WIDTH), ahead, F32)

    def split_cov(r, carry):
        cov_copy(r).wait()
        for s in range(SLOTS):
            high, low = split(covv[r, s])
            cov_hl[r, :BLOCK, s * BLOCK:(s + 1) * BLOCK] = high
            cov_hl[r, BLOCK:, s * BLOCK:(s + 1) * BLOCK] = low
        return carry

    lax.fori_loop(0, ROW_BLOCKS, split_cov, 0)

    def split_window(side):
        def one(k, carry):
            rows = pl.ds(pl.multiple_of(k * BLOCK, BLOCK), BLOCK)
            high, low = split(win[side, rows, :])
            win_hl[side * ROW_BLOCKS + k, :, :WIDTH] = high
            win_hl[side * ROW_BLOCKS + k, :, WIDTH:] = low
            return carry

        lax.fori_loop(0, ROW_BLOCKS, one, 0)

    own_copy.wait()
    split_window(1)
    to_after.wait_recv()
    split_window(0)
    to_before.wait_recv()
    split_window(2)

    base = p * ROW_BLOCKS - ROW_BLOCKS - NBLK

    def rows_of(src, i):
        r = lax.rem(i + HALF * (1 - lax.div(src, 2)), ROW_BLOCKS)
        return r, pl.ds(pl.multiple_of(r * BLOCK, BLOCK), BLOCK)

    def xcopy(src, i, send, recv, to):
        ref = vall.at[src, rows_of(src, i)[1], :]
        return remote(ref, ref, send.at[i], recv.at[i], cols=to)

    def own_left(i):
        return xcopy(g, i, left_s, next_r, g_prev)

    def own_right(i):
        return xcopy(g, i, right_s, prev_r, g_next)

    def forward_right(i):
        return xcopy(g_prev, i, fwdr_s, opp_r, g_next)

    def forward_left(i):
        return xcopy(g_next, i, fwdl_s, opp_r, g_prev)

    def from_opp(i):
        return xcopy(g_opp, i, fwdr_s, opp_r, g_next)

    def keep_split(src, i):
        rows = rows_of(src, i)[1]
        high, low = split(vall[src, rows, :])
        vhl[src, rows, :WIDTH] = high
        vhl[src, rows, WIDTH:] = low

    def image(i, carry):
        r, rows = rows_of(g, i)
        tiles = []
        for s in range(SLOTS):
            rel = lax.rem(col_index[r, s] - base, NBLK)
            tiles.append(win_hl[lax.min(rel, 3 * ROW_BLOCKS - 1)])
        quad = dot(cov_hl[r], jnp.concatenate(tiles, axis=0))
        vall[g, rows, :] = quarters(quad, BLOCK, WIDTH)
        own_left(i).start()

        @pl.when(i < HALF)
        def _():
            own_right(i).start()

        keep_split(g, i)
        return carry

    lax.fori_loop(0, ROW_BLOCKS, image, 0)

    def pass_right(i, carry):
        own_copy_in = xcopy(g_prev, i, right_s, prev_r, g_next)
        own_copy_in.wait_recv()
        forward_right(i).start()
        keep_split(g_prev, i)
        return carry

    lax.fori_loop(0, HALF, pass_right, 0)

    def rest_right(i, carry):
        own_right(i).start()
        return carry

    lax.fori_loop(HALF, ROW_BLOCKS, rest_right, 0)

    def half_of(src, k):
        return pl.ds(pl.multiple_of(lax.rem(k + 1 - lax.div(src, 2), 2) * (HALF * BLOCK), HALF * BLOCK), HALF * BLOCK)

    def gram_half(src, k):
        rows = half_of(src, k)
        return quarters(dot_t(vhl[g, rows, :], vhl[src, rows, :]), WIDTH, WIDTH)

    gram_own = gram_half(g, 0) + gram_half(g, 1)
    tb[0, :WIDTH, :] = gram_own

    def take_next(i, carry):
        xcopy(g_next, i, left_s, next_r, g_prev).wait_recv()

        @pl.when(i >= HALF)
        def _():
            forward_left(i).start()

        keep_split(g_next, i)
        return carry

    lax.fori_loop(0, HALF, take_next, 0)
    first = gram_half(g_next, 0)

    def take_opp(i, carry):
        from_opp(i).wait_recv()
        keep_split(g_opp, i)
        return carry

    lax.fori_loop(HALF, ROW_BLOCKS, take_next, 0)
    gram_next = first + gram_half(g_next, 1)
    lax.fori_loop(0, HALF, take_opp, 0)
    gram_opp = gram_half(g_opp, 0)
    edge = 3 * WIDTH // 2 - WIDTH
    tb[0, WIDTH:, :] = gram_next[:edge]
    tb[1, :WIDTH - edge, :] = gram_next[edge:]
    tb[1, WIDTH - edge:, :] = gram_opp

    to_core = remote(tb.at[1 - c], r1, p1_s, p1_r, pts=sibling)
    to_core.start()
    to_core.wait_recv()
    s1[...] = (tb[c] + r1[...]).reshape(ZS, PIECE, WIDTH)

    def z_send(k):
        to = lax.rem(z + k, ZS)
        return remote(s1.at[to], r2.at[z], p2_s.at[k], p2_r.at[z], pts=at_z(k))

    def z_recv(k):
        source = lax.rem(z + k, ZS)
        return remote(s1.at[source], r2.at[source], p2_s.at[k], p2_r.at[source], pts=at_z(k))

    for k in range(1, ZS):
        z_send(k).start()
    summed = s1[z]
    for k in range(1, ZS):
        z_recv(k).wait_recv()
        summed += r2[lax.rem(z + k, ZS)]
    r3[y] = summed

    def y_send(k):
        return remote(r3.at[y], r3.at[y], p3_s.at[k], p3_r.at[y], pts=at_y(k))

    def y_recv(k):
        source = lax.rem(y + k, YS)
        return remote(r3.at[source], r3.at[source], p3_s.at[k], p3_r.at[source], pts=at_y(k))

    for k in range(1, YS):
        y_send(k).start()
    for k in range(1, YS):
        y_recv(k).wait_recv()
    gb[g, c, z] = (r3[0] + r3[1]) + (r3[2] + r3[3])

    def z_share(k):
        ref = gb.at[g, c, z]
        return remote(ref, ref, p4_s.at[k], p4_r.at[z], pts=at_z(k))

    def z_shared(k):
        source = lax.rem(z + k, ZS)
        ref = gb.at[g, c, source]
        return remote(ref, ref, p4_s.at[k], p4_r.at[source], pts=at_z(k))

    for k in range(1, ZS):
        z_share(k).start()

    def rest(i, carry):
        xcopy(g_prev, i, right_s, prev_r, g_next).wait_recv()
        keep_split(g_prev, i)
        return carry

    for k in range(1, ZS):
        z_shared(k).wait_recv()

    def x_share(k):
        ref = gb.at[g, c]
        return remote(ref, ref, p5_s.at[k], p5_r.at[g], cols=lax.rem(g + k, GROUPS))

    def x_shared(k):
        source = lax.rem(g + k, GROUPS)
        ref = gb.at[source, c]
        return remote(ref, ref, p5_s.at[k], p5_r.at[source], cols=source)

    def core_share(k):
        source = lax.rem(g + k, GROUPS)
        ref = gb.at[source, c]
        return remote(ref, ref, p6_s.at[source], p6_r.at[source], pts=sibling)

    def core_shared(k):
        source = lax.rem(g + k, GROUPS)
        ref = gb.at[source, 1 - c]
        return remote(ref, ref, p6_s.at[source], p6_r.at[source], pts=sibling)

    for k in range(1, GROUPS):
        x_share(k).start()
    core_share(0).start()
    lax.fori_loop(HALF, ROW_BLOCKS, rest, 0)
    lax.fori_loop(HALF, ROW_BLOCKS, take_opp, 0)
    for k in range(1, GROUPS):
        x_shared(k).wait_recv()
        core_share(k).start()
    for k in range(GROUPS):
        core_shared(k).wait_recv()

    parts = [gb[a].reshape(3 * WIDTH, WIDTH) for a in range(GROUPS)]
    diag = [parts[a][:WIDTH] for a in range(GROUPS)]
    down = [lax.rsqrt(jnp.sum(d * eye, axis=1, keepdims=True)) for d in diag]
    across = [lax.rsqrt(jnp.sum(d * eye, axis=0, keepdims=True)) for d in diag]

    def put(a, h, block):
        rows, cols = slice(a * WIDTH, (a + 1) * WIDTH), slice(h * WIDTH, (h + 1) * WIDTH)
        block = block * down[a] * across[h]
        if a == h:
            block = block - eye
        high, low = split(block)
        e0[rows, cols] = block
        e0_h[rows, cols] = high
        e0_l[rows, cols] = low
        block = -(mk[rows, cols] * block)
        w[rows, cols] = block
        high, low = split(block)
        w_h[rows, cols] = high
        w_l[rows, cols] = low

    for a in range(GROUPS):
        scol[a * WIDTH:(a + 1) * WIDTH, :] = jnp.broadcast_to(down[a], (WIDTH, WIDTH))
        put(a, a, diag[a])
        h = (a + 1) % GROUPS
        block = parts[a][WIDTH:2 * WIDTH]
        put(a, h, block)
        put(h, a, block.T)
    for a in range(GROUPS // 2):
        h = a + GROUPS // 2
        block = parts[a][2 * WIDTH:] + parts[h][2 * WIDTH:].T
        put(a, h, block)
        put(h, a, block.T)

    def tile(m):
        return pl.ds(pl.multiple_of(m * WIDTH, WIDTH), WIDTH)

    def newton(fine):
        def first(m, carry):
            rows = tile(m)
            prod = dot(e0_h[rows, :], w_h[...])
            if fine:
                prod += dot(e0_l[rows, :], w_h[...]) + dot(e0_h[rows, :], w_l[...])
            value = (e0[rows, :] + w[rows, :]) + prod
            b[rows, :] = value
            high, low = split(value)
            b_h[rows, :] = high
            if fine:
                b_l[rows, :] = low
            return carry

        def second(m, carry):
            rows = tile(m)
            prod = dot_t(w_h[:, rows], b_h[...])
            if fine:
                prod += dot_t(w_l[:, rows], b_h[...]) + dot_t(w_h[:, rows], b_l[...])
            here = lax.broadcasted_iota(jnp.int32, (WIDTH, COLS), 0) + m * WIDTH
            there = lax.broadcasted_iota(jnp.int32, (WIDTH, COLS), 1)
            own = jnp.where(here == there, w[rows, :], 0.0)
            value = mk[rows, :] * ((b[rows, :] + own) + prod)
            u[rows, :] = value
            u_h[rows, :] = value.astype(BF16)
            if fine:
                res[...] += jnp.sum((value * value).reshape(WIDTH // 8, 8, COLS), axis=0)
            return carry

        def third(m, carry):
            rows = tile(m)
            value = (w[rows, :] - u[rows, :]) - dot(w_h[rows, :], u_h[...])
            w[rows, :] = value
            high, low = split(value)
            w_h[rows, :] = high
            w_l[rows, :] = low
            return carry

        lax.fori_loop(0, GROUPS, first, 0)
        lax.fori_loop(0, GROUPS, second, 0)
        lax.fori_loop(0, GROUPS, third, 0)

    res[...] = jnp.zeros_like(res)
    newton(False)
    newton(False)
    newton(True)
    residual[...] = jnp.full(residual.shape, jnp.sum(res[...]), F32)

    mine = pl.ds(pl.multiple_of(g * WIDTH, WIDTH), WIDTH)
    for a in range(GROUPS):
        rows = slice(a * WIDTH, (a + 1) * WIDTH)
        same = jnp.where(g == a, 1.0, 0.0).astype(F32)
        high, low = split(scol[rows, :] * (w[rows, mine] + same * eye))
        x_hl[rows, :WIDTH] = high
        x_hl[rows, WIDTH:] = low

    outv = win

    def result(k):
        rows = pl.ds(pl.multiple_of(k * 2 * BLOCK, 2 * BLOCK), 2 * BLOCK)
        return pltpu.make_async_copy(outv.at[1, rows, :], out.at[rows, :], f_sem.at[k])

    def finish(k, carry):
        rows = pl.ds(pl.multiple_of(k * 2 * BLOCK, 2 * BLOCK), 2 * BLOCK)
        high = jnp.concatenate([vhl[h, rows, :WIDTH] for h in range(GROUPS)], axis=1)
        low = jnp.concatenate([vhl[h, rows, WIDTH:] for h in range(GROUPS)], axis=1)
        q = dot(jnp.concatenate([high, low], axis=0), x_hl[...])
        outv[1, rows, :] = quarters(q, 2 * BLOCK, WIDTH)
        result(k).start()
        return carry

    lax.fori_loop(0, ROW_BLOCKS // 2, finish, 0)

    to_after.wait_send()
    to_before.wait_send()

    def sent(i, carry):
        own_left(i).wait_send()
        own_right(i).wait_send()
        return carry

    def sent_on(i, carry):
        forward_right(i).wait_send()
        forward_left(i + HALF).wait_send()
        return carry

    lax.fori_loop(0, ROW_BLOCKS, sent, 0)
    lax.fori_loop(0, HALF, sent_on, 0)
    to_core.wait_send()
    for k in range(1, ZS):
        z_send(k).wait_send()
        z_share(k).wait_send()
    for k in range(1, YS):
        y_send(k).wait_send()
    for k in range(1, GROUPS):
        x_share(k).wait_send()
    for k in range(GROUPS):
        core_share(k).wait_send()

    def written(k, carry):
        result(k).wait()
        return carry

    lax.fori_loop(0, ROW_BLOCKS // 2, written, 0)


def fast(start, cov_blocks, col_index, order):
    dma = pltpu.SemaphoreType.DMA
    square = (COLS, COLS)
    hbm = pl.BlockSpec(memory_space=pl.ANY)
    smem = pl.BlockSpec(memory_space=pltpu.SMEM)
    return pl.pallas_call(
        kernel,
        out_shape=(
            jax.ShapeDtypeStruct((ROWS, WIDTH), F32),
            jax.ShapeDtypeStruct((8, 128), F32),
        ),
        in_specs=[hbm, hbm, smem, smem],
        out_specs=(hbm, pl.BlockSpec(memory_space=pltpu.VMEM)),
        scratch_shapes=[
            pltpu.VMEM((3, ROWS, WIDTH), F32),
            pltpu.VMEM((3 * ROW_BLOCKS, BLOCK, 2 * WIDTH), BF16),
            pltpu.VMEM((ROW_BLOCKS, SLOTS, BLOCK, BLOCK), F32),
            pltpu.VMEM((ROW_BLOCKS, 2 * BLOCK, SLOTS * BLOCK), BF16),
            pltpu.VMEM((GROUPS, ROWS, WIDTH), F32),
            pltpu.VMEM((GROUPS, ROWS, 2 * WIDTH), BF16),
            pltpu.VMEM((CORES, ZS * PIECE, WIDTH), F32),
            pltpu.VMEM((ZS * PIECE, WIDTH), F32),
            pltpu.VMEM((ZS, PIECE, WIDTH), F32),
            pltpu.VMEM((ZS, PIECE, WIDTH), F32),
            pltpu.VMEM((YS, PIECE, WIDTH), F32),
            pltpu.VMEM((GROUPS, CORES, ZS, PIECE, WIDTH), F32),
            pltpu.VMEM(square, F32),
            pltpu.VMEM(square, F32),
            pltpu.VMEM(square, F32),
            pltpu.VMEM(square, F32),
            pltpu.VMEM(square, F32),
            pltpu.VMEM(square, BF16),
            pltpu.VMEM(square, BF16),
            pltpu.VMEM(square, BF16),
            pltpu.VMEM(square, BF16),
            pltpu.VMEM(square, BF16),
            pltpu.VMEM(square, BF16),
            pltpu.VMEM(square, BF16),
            pltpu.VMEM((COLS, 2 * WIDTH), BF16),
            pltpu.VMEM((8, COLS), F32),
            pltpu.VMEM((COLS, WIDTH), F32),
            dma((ROW_BLOCKS,)),
            dma,
            dma,
            dma((ROW_BLOCKS // 2,)),
            dma((2,)), dma((2,)),
            dma((ROW_BLOCKS,)), dma((ROW_BLOCKS,)),
            dma((ROW_BLOCKS,)), dma((ROW_BLOCKS,)),
            dma((ROW_BLOCKS,)), dma((ROW_BLOCKS,)), dma((ROW_BLOCKS,)),
            dma, dma,
            dma((ZS,)), dma((ZS,)),
            dma((YS,)), dma((YS,)),
            dma((ZS,)), dma((ZS,)),
            dma((GROUPS,)), dma((GROUPS,)),
            dma((GROUPS,)), dma((GROUPS,)),
        ],
        compiler_params=pltpu.CompilerParams(
            collective_id=0, has_side_effects=True, vmem_limit_bytes=56 * 1024 * 1024
        ),
    )(start, cov_blocks, col_index, order)


def body(start, cov_blocks, col_index, order):
    result, residual = fast(start, cov_blocks, col_index, order)
    return lax.cond(
        residual[0, 0] < TOLERANCE,
        lambda: result,
        lambda: careful(start, cov_blocks, col_index, order),
    )


def solution(mesh):
    placed = (P("pts", "cols"), P("pts", None, None, None), P("pts", None), P())
    return jax.shard_map(
        body, mesh=mesh, in_specs=placed, out_specs=P("pts", "cols"), check_vma=False
    )
```

```python
import jax
import jax.numpy as jnp
from jax import lax
from jax.experimental import pallas as pl
from jax.experimental.pallas import tpu as pltpu
from jax.sharding import PartitionSpec as P

MESH = pl.DeviceIdType.MESH
F32 = jnp.float32
BF16 = jnp.bfloat16
GROUPS = 4
WIDTH = 128
BLOCK = 128
ROW_BLOCKS = 8
SLOTS = 8
NBLK = 512
YS, ZS, CORES = 4, 8, 2
COLS = GROUPS * WIDTH
ROWS = ROW_BLOCKS * BLOCK
HALF = ROW_BLOCKS // 2
TILES = 3 * WIDTH // CORES // 8
PLANE = YS * ZS
TILES_G = WIDTH // 8
SETS = TILES // ZS
TOLERANCE = 4e-4


def total(value, axis):
    distance = 1
    while distance < lax.axis_size(axis):
        pairs = [(i, i ^ distance) for i in range(lax.axis_size(axis))]
        value = value + lax.ppermute(value, axis, pairs)
        distance *= 2
    return value


def broadcast(value, axis, source):
    kept = jnp.where(lax.axis_index(axis) == source, value, 0).astype(value.dtype)
    return total(kept, axis)


def with_halo(cells, axis, width):
    count = lax.axis_size(axis)
    head = lax.slice_in_dim(cells, 0, width, axis=0)
    tail = lax.slice_in_dim(cells, cells.shape[0] - width, cells.shape[0], axis=0)
    return jnp.concatenate(
        [
            lax.ppermute(tail, axis, [(i, (i + 1) % count) for i in range(count)]),
            cells,
            lax.ppermute(head, axis, [((i + 1) % count, i) for i in range(count)]),
        ],
        axis=0,
    )


def inner(left, right):
    return lax.dot_general(
        left,
        right,
        (((0,), (0,)), ((), ())),
        precision=lax.Precision.HIGHEST,
        preferred_element_type=F32,
    )


def careful(start, cov_blocks, col_index, order):
    rows, group_size = start.shape
    blocks_dev = cov_blocks.shape[0]
    block = cov_blocks.shape[2]
    total_blocks = blocks_dev * lax.axis_size("pts")
    groups = lax.axis_size("cols")
    mine = lax.axis_index("cols")
    positions = jnp.arange(groups, dtype=jnp.int32)
    rank = jnp.sum(jnp.where(order == mine, positions, 0))
    first_block = lax.axis_index("pts") * blocks_dev - blocks_dev
    relative = jnp.mod(col_index - first_block, total_blocks)
    tiles = with_halo(start, "pts", rows).reshape(3 * blocks_dev, block, group_size)[relative]
    local = jnp.einsum(
        "rsab,rsbk->rak", cov_blocks, tiles, precision=lax.Precision.HIGHEST
    ).reshape(rows, group_size)

    def step(t, local):
        owner = order[t]
        gram = total(inner(local, local), "pts")
        lower = jnp.linalg.cholesky(gram)
        candidate = lax.linalg.triangular_solve(
            lower, local, left_side=False, lower=True, transpose_a=True
        )
        ortho = broadcast(candidate, "cols", owner)
        coef = total(inner(ortho, local), "pts")
        updated = local - jnp.dot(
            ortho, coef, precision=lax.Precision.HIGHEST, preferred_element_type=F32
        )
        return jnp.where(rank > t, updated, jnp.where(mine == owner, ortho, local))

    return lax.fori_loop(0, groups, step, local)


def split(x):
    high = x.astype(BF16)
    return high, (x - high.astype(F32)).astype(BF16)


def quarters(q, m, n):
    return (q[:m, :n] + q[m:, n:]) + (q[:m, n:] + q[m:, :n])


def dot(a, b):
    return jnp.dot(a, b, preferred_element_type=F32)


def dot_t(a, b):
    return lax.dot_general(a, b, (((0,), (0,)), ((), ())), preferred_element_type=F32)


def kernel(
    start, cov, col_index, order, out, small,
    win, win_hl, covv, cov_hl, vall, vhl, acc, tb, r1, s1, r2, gb,
    e0, w, b, u, mk, e0_h, e0_l, w_h, w2_h, w_l, b_h, b_l, u_h, x_hl, res, scol,
    c_sem, l_sem, f_sem,
    halo_s, halo_r, left_s, right_s, fwdr_s, fwdl_s, next_r, prev_r, opp_r,
    p1_s, p1_r, p2_s, p2_r, p4_s, p4_r, p5_s, p5_r, p6_s, p6_r,
):
    p = lax.axis_index("pts")
    g = lax.axis_index("cols")
    npts = YS * ZS * CORES
    c = lax.rem(p, CORES)
    z = lax.rem(lax.div(p, CORES), ZS)
    y = lax.div(p, CORES * ZS)
    before, after = lax.rem(p + npts - 1, npts), lax.rem(p + 1, npts)
    sibling = p + 1 - 2 * c
    g_next, g_prev, g_opp = (lax.rem(g + k, GROUPS) for k in (1, 3, 2))

    here = y * ZS + z

    def peer(k):
        y_to, z_to = lax.rem(y + lax.div(k, ZS), YS), lax.rem(z + lax.rem(k, ZS), ZS)
        return y_to * ZS + z_to

    def device(chip):
        return chip * CORES + c

    def remote(src, dst, send, recv, **where):
        return pltpu.make_async_remote_copy(
            src_ref=src, dst_ref=dst, send_sem=send, recv_sem=recv,
            device_id=where, device_id_type=MESH,
        )

    def cov_copy(r):
        return pltpu.make_async_copy(cov.at[r], covv.at[r], c_sem.at[r])

    own_copy = pltpu.make_async_copy(start, win.at[1], l_sem)
    own_copy.start()

    def start_cov(r, carry):
        cov_copy(r).start()
        return carry

    lax.fori_loop(0, ROW_BLOCKS, start_cov, 0)

    barrier = pltpu.get_barrier_semaphore()
    peers = [dict(pts=before), dict(pts=after)]
    peers += [dict(cols=h) for h in (g_next, g_prev, g_opp)]
    for one in peers:
        pl.semaphore_signal(barrier, inc=1, device_id=one, device_id_type=MESH)

    def greet(k, carry):
        pl.semaphore_signal(barrier, inc=1, device_id=dict(pts=device(peer(k))), device_id_type=MESH)
        return carry

    lax.fori_loop(1, PLANE, greet, 0)
    pl.semaphore_wait(barrier, len(peers) + PLANE - 1)

    def to_after(k):
        rows = pl.ds(pl.multiple_of(k * BLOCK, BLOCK), BLOCK)
        return remote(start.at[rows, :], win.at[0, rows, :], halo_s.at[0, k], halo_r.at[0, k], pts=after)

    def to_before(k):
        rows = pl.ds(pl.multiple_of(k * BLOCK, BLOCK), BLOCK)
        return remote(start.at[rows, :], win.at[2, rows, :], halo_s.at[1, k], halo_r.at[1, k], pts=before)

    def start_halo(k, carry):
        to_after(ROW_BLOCKS - 1 - k).start()
        to_before(k).start()
        return carry

    lax.fori_loop(0, ROW_BLOCKS, start_halo, 0)

    ranks = []
    for a in range(GROUPS):
        rank = jnp.int32(0)
        for t in range(1, GROUPS):
            rank += jnp.where(order[t] == a, t, 0)
        ranks.append(rank)
    row_id = lax.broadcasted_iota(jnp.int32, (WIDTH, WIDTH), 0)
    col_id = lax.broadcasted_iota(jnp.int32, (WIDTH, WIDTH), 1)
    eye = (row_id == col_id).astype(F32)
    upper = (row_id < col_id).astype(F32) + 0.5 * eye
    for a in range(GROUPS):
        for h in range(GROUPS):
            rows, cols = slice(a * WIDTH, (a + 1) * WIDTH), slice(h * WIDTH, (h + 1) * WIDTH)
            if a == h:
                mk[rows, cols] = upper
            else:
                ahead = jnp.where(ranks[a] < ranks[h], 1.0, 0.0).astype(F32)
                mk[rows, cols] = jnp.full((WIDTH, WIDTH), ahead, F32)

    def split_cov(r, carry):
        cov_copy(r).wait()
        for s in range(SLOTS):
            high, low = split(covv[r, s])
            cov_hl[r, :BLOCK, s * BLOCK:(s + 1) * BLOCK] = high
            cov_hl[r, BLOCK:, s * BLOCK:(s + 1) * BLOCK] = low
        return carry

    lax.fori_loop(0, ROW_BLOCKS, split_cov, 0)

    def split_window(side, k):
        rows = pl.ds(pl.multiple_of(k * BLOCK, BLOCK), BLOCK)
        high, low = split(win[side, rows, :])
        win_hl[side * ROW_BLOCKS + k, :, :WIDTH] = high
        win_hl[side * ROW_BLOCKS + k, :, WIDTH:] = low

    def split_own(k, carry):
        split_window(1, k)
        return carry

    def take_halo(k, carry):
        to_after(ROW_BLOCKS - 1 - k).wait_recv()
        split_window(0, ROW_BLOCKS - 1 - k)
        to_before(k).wait_recv()
        split_window(2, k)
        return carry

    own_copy.wait()
    lax.fori_loop(0, ROW_BLOCKS, split_own, 0)
    lax.fori_loop(0, HALF, take_halo, 0)

    base = p * ROW_BLOCKS - ROW_BLOCKS - NBLK

    def rows_of(src, i):
        step, late = lax.rem(i, HALF), lax.div(i, HALF)
        up = lax.rem(lax.div(src, 2) + late, 2)
        r = HALF + step - up * (2 * step + 1)
        return r, pl.ds(pl.multiple_of(r * BLOCK, BLOCK), BLOCK)

    def xcopy(src, i, send, recv, to):
        ref = vall.at[src, rows_of(src, i)[1], :]
        return remote(ref, ref, send.at[i], recv.at[i], cols=to)

    def own_left(i):
        return xcopy(g, i, left_s, next_r, g_prev)

    def own_right(i):
        return xcopy(g, i, right_s, prev_r, g_next)

    def forward_right(i):
        return xcopy(g_prev, i, fwdr_s, opp_r, g_next)

    def forward_left(i):
        return xcopy(g_next, i, fwdl_s, opp_r, g_prev)

    def from_opp(i):
        return xcopy(g_opp, i, fwdr_s, opp_r, g_next)

    def keep_split(src, i):
        rows = rows_of(src, i)[1]
        high, low = split(vall[src, rows, :])
        vhl[src, rows, :WIDTH] = high
        vhl[src, rows, WIDTH:] = low

    def image(i):
        r, rows = rows_of(g, i)
        tiles = []
        for s in range(SLOTS):
            rel = lax.rem(col_index[r, s] - base, NBLK)
            tiles.append(win_hl[lax.min(rel, 3 * ROW_BLOCKS - 1)])
        quad = dot(cov_hl[r], jnp.concatenate(tiles, axis=0))
        vall[g, rows, :] = quarters(quad, BLOCK, WIDTH)
        own_left(i).start()

    def images(j, carry):
        take_halo(j + HALF, 0)
        image(j)
        own_right(j).start()
        image(j + HALF)
        keep_split(g, j)
        keep_split(g, j + HALF)
        return carry

    lax.fori_loop(0, HALF, images, 0)

    def half_of(src, late):
        low = lax.rem(lax.div(src, 2) + 1 + late, 2)
        return pl.ds(pl.multiple_of(low * (HALF * BLOCK), HALF * BLOCK), HALF * BLOCK)

    def gram_half(src, late):
        rows = half_of(src, late)
        return quarters(dot_t(vhl[g, rows, :], vhl[src, rows, :]), WIDTH, WIDTH)

    tb[0, :TILES_G] = (gram_half(g, 0) + gram_half(g, 1)).reshape(TILES_G, 8, WIDTH)

    def pass_right(j, carry):
        xcopy(g_prev, j, right_s, prev_r, g_next).wait_recv()
        forward_right(j).start()
        return carry

    def rest_right(j, carry):
        own_right(j).start()
        return carry

    lax.fori_loop(0, HALF, pass_right, 0)
    lax.fori_loop(HALF, ROW_BLOCKS, rest_right, 0)

    acc[...] = jnp.zeros_like(acc)

    def take_next(j, carry):
        for i in (j, j + HALF):
            xcopy(g_next, i, left_s, next_r, g_prev).wait_recv()
            keep_split(g_next, i)
        forward_left(j + HALF).start()
        near, far = rows_of(g_next, j)[1], rows_of(g_next, j + HALF)[1]
        left = jnp.concatenate([vhl[g, near, :], vhl[g, far, :]], axis=0)
        right = jnp.concatenate([vhl[g_next, near, :], vhl[g_next, far, :]], axis=0)
        acc[...] += dot_t(left, right)
        return carry

    def take_opp(i, carry):
        from_opp(i).wait_recv()
        keep_split(g_opp, i)
        return carry

    lax.fori_loop(0, HALF, take_next, 0)
    gram_next = quarters(acc[...], WIDTH, WIDTH).reshape(TILES_G, 8, WIDTH)
    edge = TILES - TILES_G
    tb[0, TILES_G:] = gram_next[:edge]
    tb[1, :TILES_G - edge] = gram_next[edge:]
    lax.fori_loop(0, HALF, take_opp, 0)
    tb[1, TILES_G - edge:] = gram_half(g_opp, 0).reshape(TILES_G, 8, WIDTH)

    to_core = remote(tb.at[1 - c], r1, p1_s, p1_r, pts=sibling)
    to_core.start()
    to_core.wait_recv()
    s1[...] = tb[c] + r1[...]

    def scatter(k):
        to = lax.min(peer(k), TILES - 1)
        return remote(s1.at[to], r2.at[here], p2_s.at[k], p2_r.at[here], pts=device(to))

    def start_scatter(k, carry):
        @pl.when(peer(k) < TILES)
        def _():
            scatter(k).start()

        return carry

    lax.fori_loop(1, PLANE, start_scatter, 0)

    def share(k):
        ref = gb.at[g, c, lax.min(here, TILES - 1)]
        return remote(ref, ref, p4_s.at[k], p4_r.at[lax.min(here, TILES - 1)], pts=device(peer(k)))

    @pl.when(here < TILES)
    def _():
        def take(k, summed):
            source = peer(k)
            remote(r2.at[source], r2.at[source], p2_s.at[k], p2_r.at[source], pts=device(source)).wait_recv()
            return summed + r2[source]

        gb[g, c, lax.min(here, TILES - 1)] = lax.fori_loop(1, PLANE, take, s1[lax.min(here, TILES - 1)])

        def start_share(k, carry):
            share(k).start()
            return carry

        lax.fori_loop(1, PLANE, start_share, 0)


    def rows_of_set(n):
        return pl.ds(pl.multiple_of(n * ZS, ZS), ZS)

    def x_share(k, n):
        ref = gb.at[g, c, rows_of_set(n)]
        return remote(ref, ref, p5_s.at[k, n], p5_r.at[g, n], cols=lax.rem(g + k, GROUPS))

    def x_shared(k, n):
        source = lax.rem(g + k, GROUPS)
        ref = gb.at[source, c, rows_of_set(n)]
        return remote(ref, ref, p5_s.at[k, n], p5_r.at[source, n], cols=source)

    def core_share(k):
        source = lax.rem(g + k, GROUPS)
        ref = gb.at[source, c]
        return remote(ref, ref, p6_s.at[source], p6_r.at[source], pts=sibling)

    def core_shared(k):
        source = lax.rem(g + k, GROUPS)
        ref = gb.at[source, 1 - c]
        return remote(ref, ref, p6_s.at[source], p6_r.at[source], pts=sibling)

    def shared(t, carry):
        @pl.when(t != here)
        def _():
            ref = gb.at[g, c, t]
            remote(ref, ref, p4_s.at[0], p4_r.at[t], pts=device(t)).wait_recv()

        return carry

    for n in range(SETS):
        lax.fori_loop(n * ZS, (n + 1) * ZS, shared, 0)
        for k in range(1, GROUPS):
            x_share(k, n).start()
    core_share(0).start()

    def rest(j, carry):
        keep_split(g_prev, j)
        xcopy(g_prev, j + HALF, right_s, prev_r, g_next).wait_recv()
        keep_split(g_prev, j + HALF)
        take_opp(j + HALF, 0)
        return carry

    lax.fori_loop(0, HALF, rest, 0)
    for k in range(1, GROUPS):
        for n in range(SETS):
            x_shared(k, n).wait_recv()
        core_share(k).start()
    for k in range(GROUPS):
        core_shared(k).wait_recv()

    parts = [gb[a].reshape(3 * WIDTH, WIDTH) for a in range(GROUPS)]
    diag = [parts[a][:WIDTH] for a in range(GROUPS)]
    down = [lax.rsqrt(jnp.sum(d * eye, axis=1, keepdims=True)) for d in diag]
    across = [lax.rsqrt(jnp.sum(d * eye, axis=0, keepdims=True)) for d in diag]

    def put(a, h, block):
        rows, cols = slice(a * WIDTH, (a + 1) * WIDTH), slice(h * WIDTH, (h + 1) * WIDTH)
        block = block * down[a] * across[h]
        if a == h:
            block = block - eye
        high, low = split(block)
        e0[rows, cols] = block
        e0_h[rows, cols] = high
        e0_l[rows, cols] = low
        block = -(mk[rows, cols] * block)
        w[rows, cols] = block
        high, low = split(block)
        w_h[rows, cols] = high
        w_l[rows, cols] = low

    for a in range(GROUPS):
        scol[a * WIDTH:(a + 1) * WIDTH, :] = jnp.broadcast_to(down[a], (WIDTH, WIDTH))
        put(a, a, diag[a])
        h = (a + 1) % GROUPS
        block = parts[a][WIDTH:2 * WIDTH]
        put(a, h, block)
        put(h, a, block.T)
    for a in range(GROUPS // 2):
        h = a + GROUPS // 2
        block = parts[a][2 * WIDTH:] + parts[h][2 * WIDTH:].T
        put(a, h, block)
        put(h, a, block.T)

    def newton(w_h, next_h, fine):
        for n in range(2):
            cols = slice(n * COLS // 2, (n + 1) * COLS // 2)
            prod = dot(e0_h[...], w_h[:, cols])
            if fine:
                prod += dot(e0_l[...], w_h[:, cols]) + dot(e0_h[...], w_l[:, cols])
            value = (e0[:, cols] + w[:, cols]) + prod
            b[:, cols] = value
            high, low = split(value)
            b_h[:, cols] = high
            if fine:
                b_l[:, cols] = low
        for n in range(2):
            cols = slice(n * COLS // 2, (n + 1) * COLS // 2)
            prod = dot_t(w_h[...], b_h[:, cols])
            if fine:
                prod += dot_t(w_l[...], b_h[:, cols]) + dot_t(w_h[...], b_l[:, cols])
            down_id = lax.broadcasted_iota(jnp.int32, (COLS, COLS // 2), 0)
            across_id = lax.broadcasted_iota(jnp.int32, (COLS, COLS // 2), 1) + n * COLS // 2
            own = jnp.where(down_id == across_id, w[:, cols], 0.0)
            value = mk[:, cols] * ((b[:, cols] + own) + prod)
            u[:, cols] = value
            u_h[:, cols] = value.astype(BF16)
            if fine:
                res[...] += jnp.sum((value * value).reshape(COLS // 8, 8, COLS // 2), axis=0)
        for n in range(2):
            cols = slice(n * COLS // 2, (n + 1) * COLS // 2)
            value = (w[:, cols] - u[:, cols]) - dot(w_h[...], u_h[:, cols])
            w[:, cols] = value
            if not fine:
                high, low = split(value)
                next_h[:, cols] = high
                w_l[:, cols] = low

    res[...] = jnp.zeros_like(res)
    newton(w_h, w2_h, False)
    newton(w2_h, None, True)
    small[0, 0] = jnp.where(jnp.sum(res[...]) < TOLERANCE, 1, 0).astype(jnp.int32)

    mine = pl.ds(pl.multiple_of(g * WIDTH, WIDTH), WIDTH)
    for a in range(GROUPS):
        rows = slice(a * WIDTH, (a + 1) * WIDTH)
        same = jnp.where(g == a, 1.0, 0.0).astype(F32)
        high, low = split(scol[rows, :] * (w[rows, mine] + same * eye))
        x_hl[rows, :WIDTH] = high
        x_hl[rows, WIDTH:] = low

    outv = win

    def result(k):
        rows = pl.ds(pl.multiple_of(k * 2 * BLOCK, 2 * BLOCK), 2 * BLOCK)
        return pltpu.make_async_copy(outv.at[1, rows, :], out.at[rows, :], f_sem.at[k])

    def finish(k, carry):
        rows = pl.ds(pl.multiple_of(k * 2 * BLOCK, 2 * BLOCK), 2 * BLOCK)
        high = jnp.concatenate([vhl[h, rows, :WIDTH] for h in range(GROUPS)], axis=1)
        low = jnp.concatenate([vhl[h, rows, WIDTH:] for h in range(GROUPS)], axis=1)
        q = dot(jnp.concatenate([high, low], axis=0), x_hl[...])
        outv[1, rows, :] = quarters(q, 2 * BLOCK, WIDTH)
        result(k).start()
        return carry

    lax.fori_loop(0, ROW_BLOCKS // 2, finish, 0)

    def sent(i, carry):
        to_after(i).wait_send()
        to_before(i).wait_send()
        own_left(i).wait_send()
        own_right(i).wait_send()
        return carry

    def sent_on(i, carry):
        forward_right(i).wait_send()
        forward_left(i + HALF).wait_send()
        return carry

    def scattered(k, carry):
        @pl.when(peer(k) < TILES)
        def _():
            scatter(k).wait_send()

        @pl.when(here < TILES)
        def _():
            share(k).wait_send()

        return carry

    lax.fori_loop(0, ROW_BLOCKS, sent, 0)
    lax.fori_loop(0, HALF, sent_on, 0)
    to_core.wait_send()
    lax.fori_loop(1, PLANE, scattered, 0)
    for k in range(1, GROUPS):
        for n in range(SETS):
            x_share(k, n).wait_send()
    for k in range(GROUPS):
        core_share(k).wait_send()

    def written(k, carry):
        result(k).wait()
        return carry

    lax.fori_loop(0, ROW_BLOCKS // 2, written, 0)


def fast(start, cov_blocks, col_index, order):
    dma = pltpu.SemaphoreType.DMA
    square = (COLS, COLS)
    hbm = pl.BlockSpec(memory_space=pl.ANY)
    smem = pl.BlockSpec(memory_space=pltpu.SMEM)
    return pl.pallas_call(
        kernel,
        out_shape=(
            jax.ShapeDtypeStruct((ROWS, WIDTH), F32),
            jax.ShapeDtypeStruct((1, 1), jnp.int32),
        ),
        in_specs=[hbm, hbm, smem, smem],
        out_specs=(hbm, smem),
        scratch_shapes=[
            pltpu.VMEM((3, ROWS, WIDTH), F32),
            pltpu.VMEM((3 * ROW_BLOCKS, BLOCK, 2 * WIDTH), BF16),
            pltpu.VMEM((ROW_BLOCKS, SLOTS, BLOCK, BLOCK), F32),
            pltpu.VMEM((ROW_BLOCKS, 2 * BLOCK, SLOTS * BLOCK), BF16),
            pltpu.VMEM((GROUPS, ROWS, WIDTH), F32),
            pltpu.VMEM((GROUPS, ROWS, 2 * WIDTH), BF16),
            pltpu.VMEM((2 * WIDTH, 2 * WIDTH), F32),
            pltpu.VMEM((CORES, TILES, 8, WIDTH), F32),
            pltpu.VMEM((TILES, 8, WIDTH), F32),
            pltpu.VMEM((TILES, 8, WIDTH), F32),
            pltpu.VMEM((PLANE, 8, WIDTH), F32),
            pltpu.VMEM((GROUPS, CORES, TILES, 8, WIDTH), F32),
            pltpu.VMEM(square, F32),
            pltpu.VMEM(square, F32),
            pltpu.VMEM(square, F32),
            pltpu.VMEM(square, F32),
            pltpu.VMEM(square, F32),
            pltpu.VMEM(square, BF16),
            pltpu.VMEM(square, BF16),
            pltpu.VMEM(square, BF16),
            pltpu.VMEM(square, BF16),
            pltpu.VMEM(square, BF16),
            pltpu.VMEM(square, BF16),
            pltpu.VMEM(square, BF16),
            pltpu.VMEM(square, BF16),
            pltpu.VMEM((COLS, 2 * WIDTH), BF16),
            pltpu.VMEM((8, COLS // 2), F32),
            pltpu.VMEM((COLS, WIDTH), F32),
            dma((ROW_BLOCKS,)),
            dma,
            dma((ROW_BLOCKS // 2,)),
            dma((2, ROW_BLOCKS)), dma((2, ROW_BLOCKS)),
            dma((ROW_BLOCKS,)), dma((ROW_BLOCKS,)),
            dma((ROW_BLOCKS,)), dma((ROW_BLOCKS,)),
            dma((ROW_BLOCKS,)), dma((ROW_BLOCKS,)), dma((ROW_BLOCKS,)),
            dma, dma,
            dma((PLANE,)), dma((PLANE,)),
            dma((PLANE,)), dma((TILES,)),
            dma((GROUPS, SETS)), dma((GROUPS, SETS)),
            dma((GROUPS,)), dma((GROUPS,)),
        ],
        compiler_params=pltpu.CompilerParams(
            collective_id=0, has_side_effects=True, vmem_limit_bytes=56 * 1024 * 1024
        ),
    )(start, cov_blocks, col_index, order)


def body(start, cov_blocks, col_index, order):
    result, small = fast(start, cov_blocks, col_index, order)
    return lax.cond(
        small[0, 0] == 1,
        lambda: result,
        lambda: careful(start, cov_blocks, col_index, order),
    )


def solution(mesh):
    placed = (P("pts", "cols"), P("pts", None, None, None), P("pts", None), P())
    return jax.shard_map(
        body, mesh=mesh, in_specs=placed, out_specs=P("pts", "cols"), check_vma=False
    )
```

```python
import jax
import jax.numpy as jnp
from jax import lax
from jax.experimental import pallas as pl
from jax.experimental.pallas import tpu as pltpu
from jax.sharding import PartitionSpec as P

MESH = pl.DeviceIdType.MESH
F32 = jnp.float32
BF16 = jnp.bfloat16
GROUPS = 4
WIDTH = 128
BLOCK = 128
ROW_BLOCKS = 8
SLOTS = 8
NBLK = 512
YS, ZS, CORES = 4, 8, 2
COLS = GROUPS * WIDTH
ROWS = ROW_BLOCKS * BLOCK
HALF = ROW_BLOCKS // 2
TILES = 3 * WIDTH // CORES // 8
PLANE = YS * ZS
TILES_G = WIDTH // 8
SETS = TILES // ZS
TOLERANCE = 4e-4


def total(value, axis):
    distance = 1
    while distance < lax.axis_size(axis):
        pairs = [(i, i ^ distance) for i in range(lax.axis_size(axis))]
        value = value + lax.ppermute(value, axis, pairs)
        distance *= 2
    return value


def broadcast(value, axis, source):
    kept = jnp.where(lax.axis_index(axis) == source, value, 0).astype(value.dtype)
    return total(kept, axis)


def with_halo(cells, axis, width):
    count = lax.axis_size(axis)
    head = lax.slice_in_dim(cells, 0, width, axis=0)
    tail = lax.slice_in_dim(cells, cells.shape[0] - width, cells.shape[0], axis=0)
    return jnp.concatenate(
        [
            lax.ppermute(tail, axis, [(i, (i + 1) % count) for i in range(count)]),
            cells,
            lax.ppermute(head, axis, [((i + 1) % count, i) for i in range(count)]),
        ],
        axis=0,
    )


def inner(left, right):
    return lax.dot_general(
        left,
        right,
        (((0,), (0,)), ((), ())),
        precision=lax.Precision.HIGHEST,
        preferred_element_type=F32,
    )


def careful(start, cov_blocks, col_index, order):
    rows, group_size = start.shape
    blocks_dev = cov_blocks.shape[0]
    block = cov_blocks.shape[2]
    total_blocks = blocks_dev * lax.axis_size("pts")
    groups = lax.axis_size("cols")
    mine = lax.axis_index("cols")
    positions = jnp.arange(groups, dtype=jnp.int32)
    rank = jnp.sum(jnp.where(order == mine, positions, 0))
    first_block = lax.axis_index("pts") * blocks_dev - blocks_dev
    relative = jnp.mod(col_index - first_block, total_blocks)
    tiles = with_halo(start, "pts", rows).reshape(3 * blocks_dev, block, group_size)[relative]
    local = jnp.einsum(
        "rsab,rsbk->rak", cov_blocks, tiles, precision=lax.Precision.HIGHEST
    ).reshape(rows, group_size)

    def step(t, local):
        owner = order[t]
        gram = total(inner(local, local), "pts")
        lower = jnp.linalg.cholesky(gram)
        candidate = lax.linalg.triangular_solve(
            lower, local, left_side=False, lower=True, transpose_a=True
        )
        ortho = broadcast(candidate, "cols", owner)
        coef = total(inner(ortho, local), "pts")
        updated = local - jnp.dot(
            ortho, coef, precision=lax.Precision.HIGHEST, preferred_element_type=F32
        )
        return jnp.where(rank > t, updated, jnp.where(mine == owner, ortho, local))

    return lax.fori_loop(0, groups, step, local)


def split(x):
    high = x.astype(BF16)
    return high, (x - high.astype(F32)).astype(BF16)


def quarters(q, m, n):
    return (q[:m, :n] + q[m:, n:]) + (q[:m, n:] + q[m:, :n])


def dot(a, b):
    return jnp.dot(a, b, preferred_element_type=F32)


def dot_t(a, b):
    return lax.dot_general(a, b, (((0,), (0,)), ((), ())), preferred_element_type=F32)


def kernel(
    start, cov, col_index, order, out, small,
    win, win_hl, covv, cov_hl, vall, vhl, acc, tb, r1, s1, r2, gb,
    e0, w, b, u, mk, e0_h, e0_l, w_h, w2_h, w_l, b_h, b_l, u_h, x_hl, res, scol,
    word, c_sem, l_sem, f_sem,
    halo_s, halo_r, v_s, next_r, prev_r, opp_r,
    p1_s, p1_r, p2_s, p2_r, p4_s, p4_r, p5_s, p5_r, p6_s, p6_r,
):
    p = lax.axis_index("pts")
    g = lax.axis_index("cols")
    npts = YS * ZS * CORES
    c = lax.rem(p, CORES)
    z = lax.rem(lax.div(p, CORES), ZS)
    y = lax.div(p, CORES * ZS)
    before, after = lax.rem(p + npts - 1, npts), lax.rem(p + 1, npts)
    sibling = p + 1 - 2 * c
    g_next, g_prev, g_opp = (lax.rem(g + k, GROUPS) for k in (1, 3, 2))

    here = y * ZS + z

    def peer(k):
        y_to, z_to = lax.rem(y + lax.div(k, ZS), YS), lax.rem(z + lax.rem(k, ZS), ZS)
        return y_to * ZS + z_to

    def device(chip):
        return chip * CORES + c

    def remote(src, dst, send, recv, **where):
        return pltpu.make_async_remote_copy(
            src_ref=src, dst_ref=dst, send_sem=send, recv_sem=recv,
            device_id=where, device_id_type=MESH,
        )

    cov_copy = pltpu.make_async_copy(cov, covv, c_sem)
    own_copy = pltpu.make_async_copy(start, win.at[1], l_sem)
    own_copy.start()

    cov_copy.start()

    barrier = pltpu.get_barrier_semaphore()
    near_x = [dict(cols=h) for h in (g_next, g_prev)]
    near_z = [dict(pts=device(peer(k))) for k in (1, ZS - 1)]
    near_y = [dict(pts=device(peer(k))) for k in (ZS, (YS - 1) * ZS)]
    next_z = [dict(pts=device(peer(k))) for k in (2, ZS - 2)]
    neighbours = [dict(pts=before), dict(pts=after)] + near_x + near_z + near_y

    def tell(sem, devices):
        for one in devices:
            pl.semaphore_signal(sem, inc=1, device_id=one, device_id_type=MESH)

    tell(barrier, neighbours)
    pl.semaphore_wait(barrier, len(neighbours))
    tell(word.at[0], near_z)
    tell(word.at[1], near_x)

    def halo_rows(side, k):
        count = HALF + 1 if k == 0 else 1
        low = HALF - 1 - k if side == 0 else (0 if k == 0 else HALF + k)
        return slice(low * BLOCK, (low + count) * BLOCK)

    def to_after(k):
        rows = halo_rows(0, k)
        return remote(start.at[rows, :], win.at[0, rows, :], halo_s.at[0], halo_r.at[0, k], pts=after)

    def to_before(k):
        rows = halo_rows(2, k)
        return remote(start.at[rows, :], win.at[2, rows, :], halo_s.at[1], halo_r.at[1, k], pts=before)

    for k in range(HALF):
        to_after(k).start()
        to_before(k).start()

    ranks = []
    for a in range(GROUPS):
        rank = jnp.int32(0)
        for t in range(1, GROUPS):
            rank += jnp.where(order[t] == a, t, 0)
        ranks.append(rank)
    row_id = lax.broadcasted_iota(jnp.int32, (WIDTH, WIDTH), 0)
    col_id = lax.broadcasted_iota(jnp.int32, (WIDTH, WIDTH), 1)
    eye = (row_id == col_id).astype(F32)
    upper = (row_id < col_id).astype(F32) + 0.5 * eye
    for a in range(GROUPS):
        for h in range(GROUPS):
            rows, cols = slice(a * WIDTH, (a + 1) * WIDTH), slice(h * WIDTH, (h + 1) * WIDTH)
            if a == h:
                mk[rows, cols] = upper
            else:
                ahead = jnp.where(ranks[a] < ranks[h], 1.0, 0.0).astype(F32)
                mk[rows, cols] = jnp.full((WIDTH, WIDTH), ahead, F32)

    cov_copy.wait()

    def split_cov(r, carry):
        for s in range(SLOTS):
            high, low = split(covv[r, s])
            cov_hl[r, :BLOCK, s * BLOCK:(s + 1) * BLOCK] = high
            cov_hl[r, BLOCK:, s * BLOCK:(s + 1) * BLOCK] = low
        return carry

    lax.fori_loop(0, ROW_BLOCKS, split_cov, 0)

    pl.semaphore_wait(word.at[0], 2)
    tell(word.at[2], next_z)
    def split_window(side, k):
        rows = pl.ds(k * BLOCK if isinstance(k, int) else pl.multiple_of(k * BLOCK, BLOCK), BLOCK)
        high, low = split(win[side, rows, :])
        win_hl[side * ROW_BLOCKS + k, :, :WIDTH] = high
        win_hl[side * ROW_BLOCKS + k, :, WIDTH:] = low

    def split_own(k, carry):
        split_window(1, k)
        return carry

    own_copy.wait()
    lax.fori_loop(0, ROW_BLOCKS, split_own, 0)

    base = p * ROW_BLOCKS - ROW_BLOCKS - NBLK

    def rows_of(src, i):
        step, late = lax.rem(i, HALF), lax.div(i, HALF)
        up = lax.rem(lax.div(src, 2) + late, 2)
        r = HALF + step - up * (2 * step + 1)
        return r, pl.ds(pl.multiple_of(r * BLOCK, BLOCK), BLOCK)

    def xcopy(src, i, recv, to):
        ref = vall.at[src, rows_of(src, i)[1], :]
        return remote(ref, ref, v_s, recv, cols=to)

    def own_left(i):
        return xcopy(g, i, next_r.at[lax.rem(i, HALF)], g_prev)

    def own_right(i):
        return xcopy(g, i, prev_r.at[lax.min(i, HALF)], g_next)

    def forward_right(i):
        return xcopy(g_prev, i, opp_r.at[0], g_next)

    def forward_left(i):
        return xcopy(g_next, i, opp_r.at[1], g_prev)

    def arrived(sem, *like):
        for ref in like:
            pltpu.make_async_copy(ref, ref, sem).wait()

    def several(src, count):
        return vall.at[src, pl.ds(0, count * BLOCK), :]

    def keep_split(src, i):
        rows = rows_of(src, i)[1]
        high, low = split(vall[src, rows, :])
        vhl[src, rows, :WIDTH] = high
        vhl[src, rows, WIDTH:] = low

    def image(i):
        r, rows = rows_of(g, i)
        tiles = []
        for s in range(SLOTS):
            rel = lax.rem(col_index[r, s] - base, NBLK)
            tiles.append(win_hl[lax.min(rel, 3 * ROW_BLOCKS - 1)])
        quad = dot(cov_hl[r], jnp.concatenate(tiles, axis=0))
        vall[g, rows, :] = quarters(quad, BLOCK, WIDTH)
        own_left(i).start()

    for j in range(HALF):
        to_after(j).wait_recv()
        to_before(j).wait_recv()
        if j == 0:
            for k in range(HALF):
                split_window(0, ROW_BLOCKS - 1 - k)
                split_window(2, k)
        split_window(0, HALF - 1 - j)
        split_window(2, HALF + j)
        image(j)
        own_right(j).start()
        image(j + HALF)
        keep_split(g, j)
        keep_split(g, j + HALF)
        if j == 0:
            pl.semaphore_wait(word.at[2], 2)
            tell(word.at[3], near_y)

    pl.semaphore_wait(word.at[3], 2)
    tell(word.at[4], near_y)

    def half_of(src, late):
        low = lax.rem(lax.div(src, 2) + 1 + late, 2)
        return pl.ds(pl.multiple_of(low * (HALF * BLOCK), HALF * BLOCK), HALF * BLOCK)

    def gram_half(src, late):
        rows = half_of(src, late)
        return quarters(dot_t(vhl[g, rows, :], vhl[src, rows, :]), WIDTH, WIDTH)

    tb[0, :TILES_G] = (gram_half(g, 0) + gram_half(g, 1)).reshape(TILES_G, 8, WIDTH)

    def pass_right(j, carry):
        arrived(prev_r.at[j], several(g_prev, 1))
        forward_right(j).start()
        return carry

    def rest_right(j, carry):
        own_right(j).start()
        return carry

    lax.fori_loop(0, HALF, pass_right, 0)
    lax.fori_loop(HALF, ROW_BLOCKS, rest_right, 0)

    acc[...] = jnp.zeros_like(acc)

    def take_next(j, carry):
        arrived(next_r.at[j], several(g_next, 2))
        keep_split(g_next, j)
        keep_split(g_next, j + HALF)
        forward_left(j + HALF).start()
        near, far = rows_of(g_next, j)[1], rows_of(g_next, j + HALF)[1]
        left = jnp.concatenate([vhl[g, near, :], vhl[g, far, :]], axis=0)
        right = jnp.concatenate([vhl[g_next, near, :], vhl[g_next, far, :]], axis=0)
        acc[...] += dot_t(left, right)
        return carry

    def take_opp(i, carry):
        keep_split(g_opp, i)
        return carry

    lax.fori_loop(0, HALF, take_next, 0)
    gram_next = quarters(acc[...], WIDTH, WIDTH).reshape(TILES_G, 8, WIDTH)
    edge = TILES - TILES_G
    tb[0, TILES_G:] = gram_next[:edge]
    tb[1, :TILES_G - edge] = gram_next[edge:]
    arrived(opp_r.at[0], several(g_opp, HALF))
    lax.fori_loop(0, HALF, take_opp, 0, unroll=True)
    tb[1, TILES_G - edge:] = gram_half(g_opp, 0).reshape(TILES_G, 8, WIDTH)

    to_core = remote(tb.at[1 - c], r1, p1_s, p1_r, pts=sibling)
    to_core.start()
    to_core.wait_recv()
    s1[...] = tb[c] + r1[...]

    pl.semaphore_wait(word.at[4], 2)
    pl.semaphore_wait(word.at[1], 2)
    def scatter(k):
        to = lax.min(peer(k), TILES - 1)
        return remote(s1.at[to], r2.at[here], p2_s, p2_r, pts=device(to))

    def start_scatter(k, carry):
        @pl.when(peer(k) < TILES)
        def _():
            scatter(k).start()

        return carry

    lax.fori_loop(1, PLANE, start_scatter, 0)

    def share(k):
        ref = gb.at[g, c, lax.min(here, TILES - 1)]
        return remote(ref, ref, p4_s, p4_r.at[lax.div(lax.min(here, TILES - 1), ZS)], pts=device(peer(k)))

    @pl.when(here < TILES)
    def _():
        arrived(p2_r, r2.at[pl.ds(1, PLANE - 1)])
        r2[here] = s1[lax.min(here, TILES - 1)]
        gb[g, c, lax.min(here, TILES - 1)] = jnp.sum(r2[...], axis=0)

        def start_share(k, carry):
            share(k).start()
            return carry

        lax.fori_loop(1, PLANE, start_share, 0)


    def rows_of_set(n):
        return pl.ds(pl.multiple_of(n * ZS, ZS), ZS)

    def x_share(k, n):
        ref = gb.at[g, c, rows_of_set(n)]
        return remote(ref, ref, p5_s, p5_r.at[GROUPS - k, n], cols=lax.rem(g + k, GROUPS))

    def core_share(k, n):
        ref = gb.at[lax.rem(g + k, GROUPS), c, rows_of_set(n)]
        return remote(ref, ref, p6_s, p6_r, pts=sibling)

    for n in range(SETS):
        @pl.when(y == n)
        def _():
            arrived(p4_r.at[n], gb.at[g, c, pl.ds(0, ZS - 1)])

        @pl.when(y != n)
        def _():
            arrived(p4_r.at[n], gb.at[g, c, pl.ds(0, ZS)])

        for k in range(1, GROUPS):
            x_share(k, n).start()
        core_share(0, n).start()

    arrived(prev_r.at[HALF], several(g_prev, HALF))
    arrived(opp_r.at[1], several(g_opp, HALF))

    def rest(j, carry):
        keep_split(g_prev, j)
        keep_split(g_prev, j + HALF)
        take_opp(j + HALF, 0)
        return carry

    lax.fori_loop(0, HALF, rest, 0)
    for n in range(SETS):
        for k in (1, 3, 2):
            arrived(p5_r.at[k, n], gb.at[lax.rem(g + k, GROUPS), c, rows_of_set(n)])
            core_share(k, n).start()
    arrived(p6_r, gb.at[:, 1 - c])

    parts = [gb[a].reshape(3 * WIDTH, WIDTH) for a in range(GROUPS)]
    diag = [parts[a][:WIDTH] for a in range(GROUPS)]
    down = [lax.rsqrt(jnp.sum(d * eye, axis=1, keepdims=True)) for d in diag]
    across = [lax.rsqrt(jnp.sum(d * eye, axis=0, keepdims=True)) for d in diag]

    def put(a, h, block):
        rows, cols = slice(a * WIDTH, (a + 1) * WIDTH), slice(h * WIDTH, (h + 1) * WIDTH)
        block = block * down[a] * across[h]
        if a == h:
            block = block - eye
        high, low = split(block)
        e0[rows, cols] = block
        e0_h[rows, cols] = high
        e0_l[rows, cols] = low
        block = -(mk[rows, cols] * block)
        w[rows, cols] = block
        high, low = split(block)
        w_h[rows, cols] = high
        w_l[rows, cols] = low

    for a in range(GROUPS):
        scol[a * WIDTH:(a + 1) * WIDTH, :] = jnp.broadcast_to(down[a], (WIDTH, WIDTH))
        put(a, a, diag[a])
        h = (a + 1) % GROUPS
        block = parts[a][WIDTH:2 * WIDTH]
        put(a, h, block)
        put(h, a, block.T)
    for a in range(GROUPS // 2):
        h = a + GROUPS // 2
        block = parts[a][2 * WIDTH:] + parts[h][2 * WIDTH:].T
        put(a, h, block)
        put(h, a, block.T)

    def newton(w_h, next_h, fine):
        for n in range(2):
            cols = slice(n * COLS // 2, (n + 1) * COLS // 2)
            prod = dot(e0_h[...], w_h[:, cols])
            if fine:
                prod += dot(e0_l[...], w_h[:, cols]) + dot(e0_h[...], w_l[:, cols])
            value = (e0[:, cols] + w[:, cols]) + prod
            b[:, cols] = value
            high, low = split(value)
            b_h[:, cols] = high
            if fine:
                b_l[:, cols] = low
        for n in range(2):
            cols = slice(n * COLS // 2, (n + 1) * COLS // 2)
            prod = dot_t(w_h[...], b_h[:, cols])
            if fine:
                prod += dot_t(w_l[...], b_h[:, cols]) + dot_t(w_h[...], b_l[:, cols])
            down_id = lax.broadcasted_iota(jnp.int32, (COLS, COLS // 2), 0)
            across_id = lax.broadcasted_iota(jnp.int32, (COLS, COLS // 2), 1) + n * COLS // 2
            own = jnp.where(down_id == across_id, w[:, cols], 0.0)
            value = mk[:, cols] * ((b[:, cols] + own) + prod)
            u[:, cols] = value
            u_h[:, cols] = value.astype(BF16)
            if fine:
                res[...] += jnp.sum((value * value).reshape(COLS // 8, 8, COLS // 2), axis=0)
        for n in range(2):
            cols = slice(n * COLS // 2, (n + 1) * COLS // 2)
            value = (w[:, cols] - u[:, cols]) - dot(w_h[...], u_h[:, cols])
            w[:, cols] = value
            if not fine:
                high, low = split(value)
                next_h[:, cols] = high
                w_l[:, cols] = low

    res[...] = jnp.zeros_like(res)
    newton(w_h, w2_h, False)
    newton(w2_h, None, True)
    small[0, 0] = jnp.where(jnp.sum(res[...]) < TOLERANCE, 1, 0).astype(jnp.int32)

    mine = pl.ds(pl.multiple_of(g * WIDTH, WIDTH), WIDTH)
    for a in range(GROUPS):
        rows = slice(a * WIDTH, (a + 1) * WIDTH)
        same = jnp.where(g == a, 1.0, 0.0).astype(F32)
        high, low = split(scol[rows, :] * (w[rows, mine] + same * eye))
        x_hl[rows, :WIDTH] = high
        x_hl[rows, WIDTH:] = low

    outv = win

    def result(k):
        rows = slice(k * 2 * BLOCK, (k + 1) * 2 * BLOCK)
        return pltpu.make_async_copy(outv.at[1, rows, :], out.at[rows, :], f_sem)

    for k in range(ROW_BLOCKS // 2):
        rows = slice(k * 2 * BLOCK, (k + 1) * 2 * BLOCK)
        high = jnp.concatenate([vhl[h, rows, :WIDTH] for h in range(GROUPS)], axis=1)
        low = jnp.concatenate([vhl[h, rows, WIDTH:] for h in range(GROUPS)], axis=1)
        q = dot(jnp.concatenate([high, low], axis=0), x_hl[...])
        outv[1, rows, :] = quarters(q, 2 * BLOCK, WIDTH)
        result(k).start()

    arrived(halo_s.at[0], win.at[0])
    arrived(halo_s.at[1], win.at[2])
    arrived(v_s, vall.at[:3])
    to_core.wait_send()
    arrived(p5_s, gb.at[:3, 0])
    arrived(p6_s, gb.at[:, 0])

    @pl.when(here < TILES)
    def _():
        arrived(p2_s, s1.at[pl.ds(0, TILES - 1)])
        arrived(p4_s, r2.at[pl.ds(0, PLANE - 1)])

    @pl.when(here >= TILES)
    def _():
        arrived(p2_s, s1)

    arrived(f_sem, out)


def fast(start, cov_blocks, col_index, order):
    dma = pltpu.SemaphoreType.DMA
    square = (COLS, COLS)
    hbm = pl.BlockSpec(memory_space=pl.ANY)
    smem = pl.BlockSpec(memory_space=pltpu.SMEM)
    return pl.pallas_call(
        kernel,
        out_shape=(
            jax.ShapeDtypeStruct((ROWS, WIDTH), F32),
            jax.ShapeDtypeStruct((1, 1), jnp.int32),
        ),
        in_specs=[hbm, hbm, smem, smem],
        out_specs=(hbm, smem),
        scratch_shapes=[
            pltpu.VMEM((3, ROWS, WIDTH), F32),
            pltpu.VMEM((3 * ROW_BLOCKS, BLOCK, 2 * WIDTH), BF16),
            pltpu.VMEM((ROW_BLOCKS, SLOTS, BLOCK, BLOCK), F32),
            pltpu.VMEM((ROW_BLOCKS, 2 * BLOCK, SLOTS * BLOCK), BF16),
            pltpu.VMEM((GROUPS, ROWS, WIDTH), F32),
            pltpu.VMEM((GROUPS, ROWS, 2 * WIDTH), BF16),
            pltpu.VMEM((2 * WIDTH, 2 * WIDTH), F32),
            pltpu.VMEM((CORES, TILES, 8, WIDTH), F32),
            pltpu.VMEM((TILES, 8, WIDTH), F32),
            pltpu.VMEM((TILES, 8, WIDTH), F32),
            pltpu.VMEM((PLANE, 8, WIDTH), F32),
            pltpu.VMEM((GROUPS, CORES, TILES, 8, WIDTH), F32),
            pltpu.VMEM(square, F32),
            pltpu.VMEM(square, F32),
            pltpu.VMEM(square, F32),
            pltpu.VMEM(square, F32),
            pltpu.VMEM(square, F32),
            pltpu.VMEM(square, BF16),
            pltpu.VMEM(square, BF16),
            pltpu.VMEM(square, BF16),
            pltpu.VMEM(square, BF16),
            pltpu.VMEM(square, BF16),
            pltpu.VMEM(square, BF16),
            pltpu.VMEM(square, BF16),
            pltpu.VMEM(square, BF16),
            pltpu.VMEM((COLS, 2 * WIDTH), BF16),
            pltpu.VMEM((8, COLS // 2), F32),
            pltpu.VMEM((COLS, WIDTH), F32),
            pltpu.SemaphoreType.REGULAR((5,)),
            dma, dma, dma,
            dma((2,)), dma((2, HALF)),
            dma, dma((HALF,)), dma((HALF + 1,)), dma((2,)),
            dma, dma,
            dma, dma,
            dma, dma((SETS,)),
            dma, dma((GROUPS, SETS)),
            dma, dma,
        ],
        compiler_params=pltpu.CompilerParams(
            collective_id=0, has_side_effects=True, vmem_limit_bytes=56 * 1024 * 1024
        ),
    )(start, cov_blocks, col_index, order)


def body(start, cov_blocks, col_index, order):
    result, small = fast(start, cov_blocks, col_index, order)
    return lax.cond(
        small[0, 0] == 1,
        lambda: result,
        lambda: careful(start, cov_blocks, col_index, order),
    )


def solution(mesh):
    placed = (P("pts", "cols"), P("pts", None, None, None), P("pts", None), P())
    return jax.shard_map(
        body, mesh=mesh, in_specs=placed, out_specs=P("pts", "cols"), check_vma=False
    )
```

```python
import jax
import jax.numpy as jnp
from jax import lax
from jax.experimental import pallas as pl
from jax.experimental.pallas import tpu as pltpu
from jax.sharding import PartitionSpec as P

MESH = pl.DeviceIdType.MESH
F32 = jnp.float32
BF16 = jnp.bfloat16
GROUPS = 4
WIDTH = 128
BLOCK = 128
ROW_BLOCKS = 8
SLOTS = 8
NBLK = 512
YS, ZS, CORES = 4, 8, 2
COLS = GROUPS * WIDTH
ROWS = ROW_BLOCKS * BLOCK
HALF = ROW_BLOCKS // 2
PLANE = YS * ZS
TILES_G = WIDTH // CORES // 8
KINDS = 4
TILES = KINDS * TILES_G
LATE = TILES - TILES_G
NEAR_LAST = (4, 3, 5, 2, 6, 1, 7, 0)
TOLERANCE = 4e-4


def total(value, axis):
    distance = 1
    while distance < lax.axis_size(axis):
        pairs = [(i, i ^ distance) for i in range(lax.axis_size(axis))]
        value = value + lax.ppermute(value, axis, pairs)
        distance *= 2
    return value


def broadcast(value, axis, source):
    kept = jnp.where(lax.axis_index(axis) == source, value, 0).astype(value.dtype)
    return total(kept, axis)


def with_halo(cells, axis, width):
    count = lax.axis_size(axis)
    head = lax.slice_in_dim(cells, 0, width, axis=0)
    tail = lax.slice_in_dim(cells, cells.shape[0] - width, cells.shape[0], axis=0)
    return jnp.concatenate(
        [
            lax.ppermute(tail, axis, [(i, (i + 1) % count) for i in range(count)]),
            cells,
            lax.ppermute(head, axis, [((i + 1) % count, i) for i in range(count)]),
        ],
        axis=0,
    )


def inner(left, right):
    return lax.dot_general(
        left,
        right,
        (((0,), (0,)), ((), ())),
        precision=lax.Precision.HIGHEST,
        preferred_element_type=F32,
    )


def careful(start, cov_blocks, col_index, order):
    rows, group_size = start.shape
    blocks_dev = cov_blocks.shape[0]
    block = cov_blocks.shape[2]
    total_blocks = blocks_dev * lax.axis_size("pts")
    groups = lax.axis_size("cols")
    mine = lax.axis_index("cols")
    positions = jnp.arange(groups, dtype=jnp.int32)
    rank = jnp.sum(jnp.where(order == mine, positions, 0))
    first_block = lax.axis_index("pts") * blocks_dev - blocks_dev
    relative = jnp.mod(col_index - first_block, total_blocks)
    tiles = with_halo(start, "pts", rows).reshape(3 * blocks_dev, block, group_size)[relative]
    local = jnp.einsum(
        "rsab,rsbk->rak", cov_blocks, tiles, precision=lax.Precision.HIGHEST
    ).reshape(rows, group_size)

    def step(t, local):
        owner = order[t]
        gram = total(inner(local, local), "pts")
        lower = jnp.linalg.cholesky(gram)
        candidate = lax.linalg.triangular_solve(
            lower, local, left_side=False, lower=True, transpose_a=True
        )
        ortho = broadcast(candidate, "cols", owner)
        coef = total(inner(ortho, local), "pts")
        updated = local - jnp.dot(
            ortho, coef, precision=lax.Precision.HIGHEST, preferred_element_type=F32
        )
        return jnp.where(rank > t, updated, jnp.where(mine == owner, ortho, local))

    return lax.fori_loop(0, groups, step, local)


def split(x):
    high = x.astype(BF16)
    return high, (x - high.astype(F32)).astype(BF16)


def quarters(q, m, n):
    return (q[:m, :n] + q[m:, n:]) + (q[:m, n:] + q[m:, :n])


def dot(a, b):
    return jnp.dot(a, b, preferred_element_type=F32)


def dot_t(a, b):
    return lax.dot_general(a, b, (((0,), (0,)), ((), ())), preferred_element_type=F32)


def kernel(
    start, cov, col_index, order, out, small,
    win, win_hl, covv, cov_hl, vall, vhl, acc, acc2, tb, r1, s1, r2, gb,
    e0, w, b, u, mk, e0_h, e0_l, w_h, w2_h, w_l, b_h, b_l, u_h, x_hl, res, scol,
    word, c_sem, l_sem, f_sem,
    halo_s, halo_r, v_s, next_r, prev_r, rest_r,
    p1_s, p1_r, p2_s, p2_r, p4_s, p4_r, p5_s, p5_r, p6_s, p6_r,
):
    p = lax.axis_index("pts")
    g = lax.axis_index("cols")
    npts = YS * ZS * CORES
    c = lax.rem(p, CORES)
    z = lax.rem(lax.div(p, CORES), ZS)
    y = lax.div(p, CORES * ZS)
    before, after = lax.rem(p + npts - 1, npts), lax.rem(p + 1, npts)
    sibling = p + 1 - 2 * c
    g_next, g_prev, g_opp = (lax.rem(g + k, GROUPS) for k in (1, 3, 2))

    here = y * ZS + z

    def peer(k):
        y_to, z_to = lax.rem(y + lax.div(k, ZS), YS), lax.rem(z + lax.rem(k, ZS), ZS)
        return y_to * ZS + z_to

    def device(chip):
        return chip * CORES + c

    def remote(src, dst, send, recv, **where):
        return pltpu.make_async_remote_copy(
            src_ref=src, dst_ref=dst, send_sem=send, recv_sem=recv,
            device_id=where, device_id_type=MESH,
        )

    cov_copy = pltpu.make_async_copy(cov, covv, c_sem)
    own_copy = pltpu.make_async_copy(start, win.at[1], l_sem)
    own_copy.start()

    cov_copy.start()

    barrier = pltpu.get_barrier_semaphore()
    near_x = [dict(cols=h) for h in (g_next, g_prev)]
    near_z = [dict(pts=device(peer(k))) for k in (1, ZS - 1)]
    near_y = [dict(pts=device(peer(k))) for k in (ZS, (YS - 1) * ZS)]
    next_z = [dict(pts=device(peer(k))) for k in (2, ZS - 2)]
    neighbours = [dict(pts=before), dict(pts=after)] + near_x + near_z + near_y

    def tell(sem, devices):
        for one in devices:
            pl.semaphore_signal(sem, inc=1, device_id=one, device_id_type=MESH)

    tell(barrier, neighbours)
    pl.semaphore_wait(barrier, len(neighbours))
    tell(word.at[0], near_z)
    tell(word.at[1], near_x)

    def halo_rows(side, k):
        count = HALF + 1 if k == 0 else 1
        low = HALF - 1 - k if side == 0 else (0 if k == 0 else HALF + k)
        return slice(low * BLOCK, (low + count) * BLOCK)

    def to_after(k):
        rows = halo_rows(0, k)
        return remote(start.at[rows, :], win.at[0, rows, :], halo_s.at[0], halo_r.at[0, k], pts=after)

    def to_before(k):
        rows = halo_rows(2, k)
        return remote(start.at[rows, :], win.at[2, rows, :], halo_s.at[1], halo_r.at[1, k], pts=before)

    for k in range(HALF):
        to_after(k).start()
        to_before(k).start()

    ranks = []
    for a in range(GROUPS):
        rank = jnp.int32(0)
        for t in range(1, GROUPS):
            rank += jnp.where(order[t] == a, t, 0)
        ranks.append(rank)
    row_id = lax.broadcasted_iota(jnp.int32, (WIDTH, WIDTH), 0)
    col_id = lax.broadcasted_iota(jnp.int32, (WIDTH, WIDTH), 1)
    eye = (row_id == col_id).astype(F32)
    upper = (row_id < col_id).astype(F32) + 0.5 * eye
    for a in range(GROUPS):
        for h in range(GROUPS):
            rows, cols = slice(a * WIDTH, (a + 1) * WIDTH), slice(h * WIDTH, (h + 1) * WIDTH)
            if a == h:
                mk[rows, cols] = upper
            else:
                ahead = jnp.where(ranks[a] < ranks[h], 1.0, 0.0).astype(F32)
                mk[rows, cols] = jnp.full((WIDTH, WIDTH), ahead, F32)

    cov_copy.wait()

    def split_cov(r, carry):
        for s in range(SLOTS):
            high, low = split(covv[r, s])
            cov_hl[r, :BLOCK, s * BLOCK:(s + 1) * BLOCK] = high
            cov_hl[r, BLOCK:, s * BLOCK:(s + 1) * BLOCK] = low
        return carry

    lax.fori_loop(0, ROW_BLOCKS, split_cov, 0)

    pl.semaphore_wait(word.at[0], 2)
    tell(word.at[2], next_z)
    def split_window(side, k):
        rows = pl.ds(k * BLOCK if isinstance(k, int) else pl.multiple_of(k * BLOCK, BLOCK), BLOCK)
        high, low = split(win[side, rows, :])
        win_hl[side * ROW_BLOCKS + k, :, :WIDTH] = high
        win_hl[side * ROW_BLOCKS + k, :, WIDTH:] = low

    def split_own(k, carry):
        split_window(1, k)
        return carry

    own_copy.wait()
    lax.fori_loop(0, ROW_BLOCKS, split_own, 0)

    base = p * ROW_BLOCKS - ROW_BLOCKS - NBLK

    def rows(r):
        return slice(r * BLOCK, (r + 1) * BLOCK)

    def turn(r):
        return lax.rem(g + GROUPS - r % GROUPS, GROUPS)

    def goes_left(r):
        t = turn(r)
        return (t >= 2) | (t == 0) if r < HALF else t >= 2

    def goes_right(r):
        t = turn(r)
        return t <= 1 if r < HALF else (t <= 1) | (t == 3)

    def between(r):
        t = turn(r)
        return (t == 1) | (t == 2)

    def has_next(r):
        t = turn(r)
        return t >= 1 if r < HALF else (t == 1) | (t == 2)

    def has_prev(r):
        t = turn(r)
        return (t == 1) | (t == 2) if r < HALF else t <= 2

    def prev_pair(r):
        t = turn(r)
        return t == 1 if r < HALF else t <= 1

    def xcopy(src, r, recv, to):
        ref = vall.at[src, rows(r), :]
        return remote(ref, ref, v_s, recv, cols=to)

    def arrived(sem, ref):
        pltpu.make_async_copy(ref, ref, sem).wait()

    def several(count):
        return vall.at[0, :count * BLOCK, :]

    def keep_split(src, r):
        high, low = split(vall[src, rows(r), :])
        vhl[src, rows(r), :WIDTH] = high
        vhl[src, rows(r), WIDTH:] = low

    def image(r):
        tiles = []
        for s in range(SLOTS):
            rel = lax.rem(col_index[r, s] - base, NBLK)
            tiles.append(win_hl[lax.min(rel, 3 * ROW_BLOCKS - 1)])
        quad = dot(cov_hl[r], jnp.concatenate(tiles, axis=0))
        vall[g, rows(r), :] = quarters(quad, BLOCK, WIDTH)

        @pl.when(goes_left(r))
        def _():
            xcopy(g, r, next_r.at[r], g_prev).start()

        @pl.when(goes_right(r))
        def _():
            xcopy(g, r, prev_r.at[r], g_next).start()

    for j in range(HALF):
        to_after(j).wait_recv()
        to_before(j).wait_recv()
        if j == 0:
            for k in range(HALF):
                split_window(0, ROW_BLOCKS - 1 - k)
                split_window(2, k)
        split_window(0, HALF - 1 - j)
        split_window(2, HALF + j)
        for r in (HALF + j, HALF - 1 - j):
            image(r)
            keep_split(g, r)
        if j == 0:
            pl.semaphore_wait(word.at[2], 2)
            tell(word.at[3], near_y)

    pl.semaphore_wait(word.at[3], 2)
    tell(word.at[4], near_y)

    def place(kind, block):
        for core in range(CORES):
            part = block[core * WIDTH // CORES:(core + 1) * WIDTH // CORES]
            tb[core, kind * TILES_G:(kind + 1) * TILES_G] = part.reshape(TILES_G, 8, WIDTH)

    def core_sum(first, count, send, recv):
        part = pl.ds(first, count)
        copy = remote(tb.at[1 - c, part], r1.at[part], send, recv, pts=sibling)
        return copy, part

    def scatter(y_to, far):
        to = y_to * ZS + lax.rem(z + far, ZS)
        return remote(s1.at[to], r2.at[here], p2_s, p2_r, pts=device(to))

    def scatter_rows(y_to):
        for far in NEAR_LAST[:-1]:
            scatter(y_to, far).start()

        @pl.when(y != y_to)
        def _():
            scatter(y_to, 0).start()

    def sum_tile():
        arrived(p2_r, r2.at[pl.ds(1, PLANE - 1)])
        r2[here] = s1[here]
        gb[g, c, here] = jnp.sum(r2[...], axis=0)
        ref = gb.at[g, c, here]
        for over in (2, 1, 3, 0):
            for far in NEAR_LAST:
                if over or far:
                    to = lax.rem(y + over, YS) * ZS + lax.rem(z + far, ZS)
                    remote(ref, ref, p4_s, p4_r.at[y], pts=device(to)).start()

    acc[...] = jnp.zeros_like(acc)
    acc2[...] = jnp.zeros_like(acc2)
    place(3, quarters(dot_t(vhl[g], vhl[g]), WIDTH, WIDTH))
    own_core, own_part = core_sum(LATE, TILES_G, p1_s.at[0], p1_r.at[0])
    own_core.start()

    for j in range(HALF):
        for r in (HALF + j, HALF - 1 - j):
            @pl.when(has_next(r))
            def _():
                arrived(next_r.at[r], several(1))
                keep_split(g_next, r)

            @pl.when(has_prev(r))
            def _():
                arrived(prev_r.at[r], several(1))
                keep_split(g_prev, r)

            @pl.when(between(r))
            def _():
                left = jnp.concatenate([vhl[g, rows(r), :], vhl[g_prev, rows(r), :]], axis=1)
                acc[...] += dot_t(left, vhl[g_next, rows(r), :])

            if r < HALF:
                @pl.when(turn(r) == 3)
                def _():
                    acc[:2 * WIDTH] += dot_t(vhl[g, rows(r), :], vhl[g_next, rows(r), :])

            @pl.when(prev_pair(r))
            def _():
                acc2[...] += dot_t(vhl[g_prev, rows(r), :], vhl[g, rows(r), :])

        if j == 1:
            own_core.wait_recv()
            s1[own_part] = tb[c, own_part] + r1[own_part]
            pl.semaphore_wait(word.at[4], 2)
            scatter_rows(YS - 1)

    place(0, quarters(acc[:2 * WIDTH], WIDTH, WIDTH))
    place(1, quarters(acc2[...], WIDTH, WIDTH))
    place(2, quarters(acc[2 * WIDTH:], WIDTH, WIDTH))

    late_core, late_part = core_sum(0, LATE, p1_s.at[1], p1_r.at[1])
    late_core.start()
    late_core.wait_recv()
    s1[late_part] = tb[c, late_part] + r1[late_part]

    for y_to in range(YS - 1):
        scatter_rows(y_to)

    for r in range(ROW_BLOCKS):
        @pl.when(jnp.logical_not(goes_left(r)))
        def _():
            xcopy(g, r, rest_r.at[0], g_prev).start()

        @pl.when(jnp.logical_not(goes_right(r)))
        def _():
            xcopy(g, r, rest_r.at[1], g_next).start()

        @pl.when(between(r))
        def _():
            xcopy(g_prev, r, rest_r.at[2], g_next).start()
            xcopy(g_next, r, rest_r.at[3], g_prev).start()

    sum_tile()

    pl.semaphore_wait(word.at[1], 2)

    def of_set(n):
        return pl.ds(n * TILES_G, TILES_G)

    def x_share(k, n):
        ref = gb.at[g, c, of_set(n)]
        return remote(ref, ref, p5_s, p5_r.at[GROUPS - k, n], cols=lax.rem(g + k, GROUPS))

    def core_share(k, n):
        ref = gb.at[lax.rem(g + k, GROUPS), c, of_set(n)]
        return remote(ref, ref, p6_s, p6_r, pts=sibling)

    for n in (3, 0, 1, 2):
        @pl.when(y == n)
        def _():
            arrived(p4_r.at[n], gb.at[g, c, pl.ds(0, TILES_G - 1)])

        @pl.when(y != n)
        def _():
            arrived(p4_r.at[n], gb.at[g, c, pl.ds(0, TILES_G)])

        for k in (2, 1, 3):
            x_share(k, n).start()
        core_share(0, n).start()

    arrived(rest_r.at[0], several(3))
    arrived(rest_r.at[1], several(3))
    arrived(rest_r.at[2], several(4))
    arrived(rest_r.at[3], several(4))
    for r in range(ROW_BLOCKS):
        keep_split(g_opp, r)

        @pl.when(jnp.logical_not(has_next(r)))
        def _():
            keep_split(g_next, r)

        @pl.when(jnp.logical_not(has_prev(r)))
        def _():
            keep_split(g_prev, r)

    for n in (3, 0, 1, 2):
        for k in (1, 3, 2):
            arrived(p5_r.at[k, n], gb.at[g, c, of_set(n)])
            core_share(k, n).start()
    arrived(p6_r, gb.at[:, 1 - c])

    def part(a, kind):
        return jnp.concatenate(
            [gb[a, core, kind * TILES_G:(kind + 1) * TILES_G].reshape(WIDTH // CORES, WIDTH) for core in range(CORES)], axis=0
        )

    diag = [part(a, 3) for a in range(GROUPS)]
    down = [lax.rsqrt(jnp.sum(d * eye, axis=1, keepdims=True)) for d in diag]
    across = [lax.rsqrt(jnp.sum(d * eye, axis=0, keepdims=True)) for d in diag]

    def put(a, h, block):
        rows, cols = slice(a * WIDTH, (a + 1) * WIDTH), slice(h * WIDTH, (h + 1) * WIDTH)
        block = block * down[a] * across[h]
        if a == h:
            block = block - eye
        high, low = split(block)
        e0[rows, cols] = block
        e0_h[rows, cols] = high
        e0_l[rows, cols] = low
        block = -(mk[rows, cols] * block)
        w[rows, cols] = block
        high, low = split(block)
        w_h[rows, cols] = high
        w_l[rows, cols] = low

    for a in range(GROUPS):
        scol[a * WIDTH:(a + 1) * WIDTH, :] = jnp.broadcast_to(down[a], (WIDTH, WIDTH))
        put(a, a, diag[a])
        h = (a + 1) % GROUPS
        block = part(a, 0) + part(h, 1)
        put(a, h, block)
        put(h, a, block.T)
    for a in range(GROUPS // 2):
        h = a + GROUPS // 2
        block = part((a + 1) % GROUPS, 2) + part((a + 3) % GROUPS, 2).T
        put(a, h, block)
        put(h, a, block.T)

    def newton(w_h, next_h, fine):
        for n in range(2):
            cols = slice(n * COLS // 2, (n + 1) * COLS // 2)
            prod = dot(e0_h[...], w_h[:, cols])
            if fine:
                prod += dot(e0_l[...], w_h[:, cols]) + dot(e0_h[...], w_l[:, cols])
            value = (e0[:, cols] + w[:, cols]) + prod
            b[:, cols] = value
            high, low = split(value)
            b_h[:, cols] = high
            if fine:
                b_l[:, cols] = low
        for n in range(2):
            cols = slice(n * COLS // 2, (n + 1) * COLS // 2)
            prod = dot_t(w_h[...], b_h[:, cols])
            if fine:
                prod += dot_t(w_l[...], b_h[:, cols]) + dot_t(w_h[...], b_l[:, cols])
            down_id = lax.broadcasted_iota(jnp.int32, (COLS, COLS // 2), 0)
            across_id = lax.broadcasted_iota(jnp.int32, (COLS, COLS // 2), 1) + n * COLS // 2
            own = jnp.where(down_id == across_id, w[:, cols], 0.0)
            value = mk[:, cols] * ((b[:, cols] + own) + prod)
            u[:, cols] = value
            u_h[:, cols] = value.astype(BF16)
            if fine:
                res[...] += jnp.sum((value * value).reshape(COLS // 8, 8, COLS // 2), axis=0)
        for n in range(2):
            cols = slice(n * COLS // 2, (n + 1) * COLS // 2)
            value = (w[:, cols] - u[:, cols]) - dot(w_h[...], u_h[:, cols])
            w[:, cols] = value
            if not fine:
                high, low = split(value)
                next_h[:, cols] = high
                w_l[:, cols] = low

    res[...] = jnp.zeros_like(res)
    newton(w_h, w2_h, False)
    newton(w2_h, None, True)
    small[0, 0] = jnp.where(jnp.sum(res[...]) < TOLERANCE, 1, 0).astype(jnp.int32)

    mine = pl.ds(pl.multiple_of(g * WIDTH, WIDTH), WIDTH)
    for a in range(GROUPS):
        rows = slice(a * WIDTH, (a + 1) * WIDTH)
        same = jnp.where(g == a, 1.0, 0.0).astype(F32)
        high, low = split(scol[rows, :] * (w[rows, mine] + same * eye))
        x_hl[rows, :WIDTH] = high
        x_hl[rows, WIDTH:] = low

    outv = win

    def result(k):
        rows = slice(k * 2 * BLOCK, (k + 1) * 2 * BLOCK)
        return pltpu.make_async_copy(outv.at[1, rows, :], out.at[rows, :], f_sem)

    for k in range(ROW_BLOCKS // 2):
        rows = slice(k * 2 * BLOCK, (k + 1) * 2 * BLOCK)
        high = jnp.concatenate([vhl[h, rows, :WIDTH] for h in range(GROUPS)], axis=1)
        low = jnp.concatenate([vhl[h, rows, WIDTH:] for h in range(GROUPS)], axis=1)
        q = dot(jnp.concatenate([high, low], axis=0), x_hl[...])
        outv[1, rows, :] = quarters(q, 2 * BLOCK, WIDTH)
        result(k).start()

    arrived(halo_s.at[0], win.at[0])
    arrived(halo_s.at[1], win.at[2])
    arrived(v_s, vall.at[:3])
    own_core.wait_send()
    late_core.wait_send()
    arrived(p2_s, s1.at[pl.ds(0, TILES - 1)])
    arrived(p4_s, r2.at[pl.ds(0, PLANE - 1)])
    arrived(p5_s, gb.at[:3, 0])
    arrived(p6_s, gb.at[:, 0])
    arrived(f_sem, out)


def fast(start, cov_blocks, col_index, order):
    dma = pltpu.SemaphoreType.DMA
    square = (COLS, COLS)
    hbm = pl.BlockSpec(memory_space=pl.ANY)
    smem = pl.BlockSpec(memory_space=pltpu.SMEM)
    return pl.pallas_call(
        kernel,
        out_shape=(
            jax.ShapeDtypeStruct((ROWS, WIDTH), F32),
            jax.ShapeDtypeStruct((1, 1), jnp.int32),
        ),
        in_specs=[hbm, hbm, smem, smem],
        out_specs=(hbm, smem),
        scratch_shapes=[
            pltpu.VMEM((3, ROWS, WIDTH), F32),
            pltpu.VMEM((3 * ROW_BLOCKS, BLOCK, 2 * WIDTH), BF16),
            pltpu.VMEM((ROW_BLOCKS, SLOTS, BLOCK, BLOCK), F32),
            pltpu.VMEM((ROW_BLOCKS, 2 * BLOCK, SLOTS * BLOCK), BF16),
            pltpu.VMEM((GROUPS, ROWS, WIDTH), F32),
            pltpu.VMEM((GROUPS, ROWS, 2 * WIDTH), BF16),
            pltpu.VMEM((4 * WIDTH, 2 * WIDTH), F32),
            pltpu.VMEM((2 * WIDTH, 2 * WIDTH), F32),
            pltpu.VMEM((CORES, TILES, 8, WIDTH), F32),
            pltpu.VMEM((TILES, 8, WIDTH), F32),
            pltpu.VMEM((TILES, 8, WIDTH), F32),
            pltpu.VMEM((PLANE, 8, WIDTH), F32),
            pltpu.VMEM((GROUPS, CORES, TILES, 8, WIDTH), F32),
            pltpu.VMEM(square, F32),
            pltpu.VMEM(square, F32),
            pltpu.VMEM(square, F32),
            pltpu.VMEM(square, F32),
            pltpu.VMEM(square, F32),
            pltpu.VMEM(square, BF16),
            pltpu.VMEM(square, BF16),
            pltpu.VMEM(square, BF16),
            pltpu.VMEM(square, BF16),
            pltpu.VMEM(square, BF16),
            pltpu.VMEM(square, BF16),
            pltpu.VMEM(square, BF16),
            pltpu.VMEM(square, BF16),
            pltpu.VMEM((COLS, 2 * WIDTH), BF16),
            pltpu.VMEM((8, COLS // 2), F32),
            pltpu.VMEM((COLS, WIDTH), F32),
            pltpu.SemaphoreType.REGULAR((5,)),
            dma, dma, dma,
            dma((2,)), dma((2, HALF)),
            dma, dma((ROW_BLOCKS,)), dma((ROW_BLOCKS,)), dma((4,)),
            dma((2,)), dma((2,)),
            dma, dma,
            dma, dma((KINDS,)),
            dma, dma((GROUPS, KINDS)),
            dma, dma,
        ],
        compiler_params=pltpu.CompilerParams(
            collective_id=0, has_side_effects=True, vmem_limit_bytes=56 * 1024 * 1024
        ),
    )(start, cov_blocks, col_index, order)


def body(start, cov_blocks, col_index, order):
    result, small = fast(start, cov_blocks, col_index, order)
    return lax.cond(
        small[0, 0] == 1,
        lambda: result,
        lambda: careful(start, cov_blocks, col_index, order),
    )


def solution(mesh):
    placed = (P("pts", "cols"), P("pts", None, None, None), P("pts", None), P())
    return jax.shard_map(
        body, mesh=mesh, in_specs=placed, out_specs=P("pts", "cols"), check_vma=False
    )
```

```python
import jax
import jax.numpy as jnp
from jax import lax
from jax.experimental import pallas as pl
from jax.experimental.pallas import tpu as pltpu
from jax.sharding import PartitionSpec as P

MESH = pl.DeviceIdType.MESH
F32 = jnp.float32
BF16 = jnp.bfloat16
GROUPS = 4
WIDTH = 128
BLOCK = 128
ROW_BLOCKS = 8
SLOTS = 8
NBLK = 512
YS, ZS, CORES = 4, 8, 2
COLS = GROUPS * WIDTH
ROWS = ROW_BLOCKS * BLOCK
HALF = ROW_BLOCKS // 2
PLANE = YS * ZS
TILES_G = WIDTH // CORES // 8
KINDS = 4
TILES = KINDS * TILES_G
LATE = TILES - TILES_G
NEAR_LAST = (4, 3, 5, 2, 6, 1, 7, 0)
TOLERANCE = 4e-4


def total(value, axis):
    distance = 1
    while distance < lax.axis_size(axis):
        pairs = [(i, i ^ distance) for i in range(lax.axis_size(axis))]
        value = value + lax.ppermute(value, axis, pairs)
        distance *= 2
    return value


def broadcast(value, axis, source):
    kept = jnp.where(lax.axis_index(axis) == source, value, 0).astype(value.dtype)
    return total(kept, axis)


def with_halo(cells, axis, width):
    count = lax.axis_size(axis)
    head = lax.slice_in_dim(cells, 0, width, axis=0)
    tail = lax.slice_in_dim(cells, cells.shape[0] - width, cells.shape[0], axis=0)
    return jnp.concatenate(
        [
            lax.ppermute(tail, axis, [(i, (i + 1) % count) for i in range(count)]),
            cells,
            lax.ppermute(head, axis, [((i + 1) % count, i) for i in range(count)]),
        ],
        axis=0,
    )


def inner(left, right):
    return lax.dot_general(
        left,
        right,
        (((0,), (0,)), ((), ())),
        precision=lax.Precision.HIGHEST,
        preferred_element_type=F32,
    )


def careful(start, cov_blocks, col_index, order):
    rows, group_size = start.shape
    blocks_dev = cov_blocks.shape[0]
    block = cov_blocks.shape[2]
    total_blocks = blocks_dev * lax.axis_size("pts")
    groups = lax.axis_size("cols")
    mine = lax.axis_index("cols")
    positions = jnp.arange(groups, dtype=jnp.int32)
    rank = jnp.sum(jnp.where(order == mine, positions, 0))
    first_block = lax.axis_index("pts") * blocks_dev - blocks_dev
    relative = jnp.mod(col_index - first_block, total_blocks)
    tiles = with_halo(start, "pts", rows).reshape(3 * blocks_dev, block, group_size)[relative]
    local = jnp.einsum(
        "rsab,rsbk->rak", cov_blocks, tiles, precision=lax.Precision.HIGHEST
    ).reshape(rows, group_size)

    def step(t, local):
        owner = order[t]
        gram = total(inner(local, local), "pts")
        lower = jnp.linalg.cholesky(gram)
        candidate = lax.linalg.triangular_solve(
            lower, local, left_side=False, lower=True, transpose_a=True
        )
        ortho = broadcast(candidate, "cols", owner)
        coef = total(inner(ortho, local), "pts")
        updated = local - jnp.dot(
            ortho, coef, precision=lax.Precision.HIGHEST, preferred_element_type=F32
        )
        return jnp.where(rank > t, updated, jnp.where(mine == owner, ortho, local))

    return lax.fori_loop(0, groups, step, local)


def split(x):
    high = x.astype(BF16)
    return high, (x - high.astype(F32)).astype(BF16)


def quarters(q, m, n):
    return (q[:m, :n] + q[m:, n:]) + (q[:m, n:] + q[m:, :n])


def dot(a, b):
    return jnp.dot(a, b, preferred_element_type=F32)


def dot_t(a, b):
    return lax.dot_general(a, b, (((0,), (0,)), ((), ())), preferred_element_type=F32)


def kernel(
    start, cov, col_in, order_in, out, small,
    col_index, order,
    win, win_hl, covv, cov_hl, vall, vhl, acc, acc2, tb, r1, s1, r2, gb,
    e0, w, b, u, mk, e0_h, e0_l, w_h, w2_h, w_l, b_h, b_l, u_h, w_by, u_by, x_hl, res, scol,
    word, i_sem, c_sem, l_sem,
    halo_s, halo_r, v_s, next_r, prev_r, rest_r,
    p1_s, p1_r, p2_s, p2_r, p4_s, p4_r, p5_s, p5_r, p6_s, p6_r,
):
    p = lax.axis_index("pts")
    g = lax.axis_index("cols")
    npts = YS * ZS * CORES
    c = lax.rem(p, CORES)
    z = lax.rem(lax.div(p, CORES), ZS)
    y = lax.div(p, CORES * ZS)
    before, after = lax.rem(p + npts - 1, npts), lax.rem(p + 1, npts)
    sibling = p + 1 - 2 * c
    g_next, g_prev, g_opp = (lax.rem(g + k, GROUPS) for k in (1, 3, 2))

    here = y * ZS + z

    def peer(k):
        y_to, z_to = lax.rem(y + lax.div(k, ZS), YS), lax.rem(z + lax.rem(k, ZS), ZS)
        return y_to * ZS + z_to

    def device(chip):
        return chip * CORES + c

    def remote(src, dst, send, recv, **where):
        return pltpu.make_async_remote_copy(
            src_ref=src, dst_ref=dst, send_sem=send, recv_sem=recv,
            device_id=where, device_id_type=MESH,
        )

    cov_copy = pltpu.make_async_copy(cov, covv, c_sem)
    own_copy = pltpu.make_async_copy(start, win.at[1], l_sem)
    own_copy.start()
    col_copy = pltpu.make_async_copy(col_in, col_index, i_sem.at[0])
    col_copy.start()
    order_copy = pltpu.make_async_copy(order_in, order, i_sem.at[1])
    order_copy.start()

    cov_copy.start()

    barrier = pltpu.get_barrier_semaphore()
    near_x = [dict(cols=h) for h in (g_next, g_prev)]
    near_z = [dict(pts=device(peer(k))) for k in (1, ZS - 1)]
    near_y = [dict(pts=device(peer(k))) for k in (ZS, (YS - 1) * ZS)]
    next_z = [dict(pts=device(peer(k))) for k in (2, ZS - 2)]
    neighbours = [dict(pts=before), dict(pts=after)] + near_x + near_z + near_y

    def tell(sem, devices):
        for one in devices:
            pl.semaphore_signal(sem, inc=1, device_id=one, device_id_type=MESH)

    tell(barrier, neighbours)
    pl.semaphore_wait(barrier, len(neighbours))
    tell(word.at[0], near_z)
    tell(word.at[1], near_x)

    def halo_rows(side, k):
        count = HALF + 1 if k == 0 else 1
        low = HALF - 1 - k if side == 0 else (0 if k == 0 else HALF + k)
        return slice(low * BLOCK, (low + count) * BLOCK)

    def to_after(k):
        rows = halo_rows(0, k)
        return remote(start.at[rows, :], win.at[0, rows, :], halo_s.at[0], halo_r.at[0, k], pts=after)

    def to_before(k):
        rows = halo_rows(2, k)
        return remote(start.at[rows, :], win.at[2, rows, :], halo_s.at[1], halo_r.at[1, k], pts=before)

    for k in range(HALF):
        to_after(k).start()
        to_before(k).start()

    col_copy.wait()
    order_copy.wait()
    ranks = []
    for a in range(GROUPS):
        rank = jnp.int32(0)
        for t in range(1, GROUPS):
            rank += jnp.where(order[t] == a, t, 0)
        ranks.append(rank)
    row_id = lax.broadcasted_iota(jnp.int32, (WIDTH, WIDTH), 0)
    col_id = lax.broadcasted_iota(jnp.int32, (WIDTH, WIDTH), 1)
    eye = (row_id == col_id).astype(F32)
    upper = (row_id < col_id).astype(F32) + 0.5 * eye
    for a in range(GROUPS):
        for h in range(GROUPS):
            rows, cols = slice(a * WIDTH, (a + 1) * WIDTH), slice(h * WIDTH, (h + 1) * WIDTH)
            if a == h:
                mk[rows, cols] = upper
            else:
                ahead = jnp.where(ranks[a] < ranks[h], 1.0, 0.0).astype(F32)
                mk[rows, cols] = jnp.full((WIDTH, WIDTH), ahead, F32)

    cov_copy.wait()

    def split_cov(r, carry):
        for s in range(SLOTS):
            high, low = split(covv[r, s])
            cov_hl[r, :BLOCK, s * BLOCK:(s + 1) * BLOCK] = high
            cov_hl[r, BLOCK:, s * BLOCK:(s + 1) * BLOCK] = low
        return carry

    lax.fori_loop(0, ROW_BLOCKS, split_cov, 0)

    pl.semaphore_wait(word.at[0], 2)
    tell(word.at[2], next_z)
    def split_window(side, k):
        rows = pl.ds(k * BLOCK if isinstance(k, int) else pl.multiple_of(k * BLOCK, BLOCK), BLOCK)
        high, low = split(win[side, rows, :])
        win_hl[side * ROW_BLOCKS + k, :, :WIDTH] = high
        win_hl[side * ROW_BLOCKS + k, :, WIDTH:] = low

    def split_own(k, carry):
        split_window(1, k)
        return carry

    own_copy.wait()
    lax.fori_loop(0, ROW_BLOCKS, split_own, 0)

    base = p * ROW_BLOCKS - ROW_BLOCKS - NBLK

    def rows(r):
        return slice(r * BLOCK, (r + 1) * BLOCK)

    def turn(r):
        return lax.rem(g + GROUPS - r % GROUPS, GROUPS)

    def goes_left(r):
        t = turn(r)
        return (t >= 2) | (t == 0) if r < HALF else t >= 2

    def goes_right(r):
        t = turn(r)
        return t <= 1 if r < HALF else (t <= 1) | (t == 3)

    def between(r):
        t = turn(r)
        return (t == 1) | (t == 2)

    def has_next(r):
        t = turn(r)
        return t >= 1 if r < HALF else (t == 1) | (t == 2)

    def has_prev(r):
        t = turn(r)
        return (t == 1) | (t == 2) if r < HALF else t <= 2

    def prev_pair(r):
        t = turn(r)
        return t == 1 if r < HALF else t <= 1

    def xcopy(src, r, recv, to):
        ref = vall.at[src, rows(r), :]
        return remote(ref, ref, v_s, recv, cols=to)

    def arrived(sem, ref):
        pltpu.make_async_copy(ref, ref, sem).wait()

    def several(count):
        return vall.at[0, :count * BLOCK, :]

    def keep_split(src, r):
        high, low = split(vall[src, rows(r), :])
        vhl[src, rows(r), :WIDTH] = high
        vhl[src, rows(r), WIDTH:] = low

    def image(r):
        tiles = []
        for s in range(SLOTS):
            rel = lax.rem(col_index[r, s] - base, NBLK)
            tiles.append(win_hl[lax.min(rel, 3 * ROW_BLOCKS - 1)])
        quad = dot(cov_hl[r], jnp.concatenate(tiles, axis=0))
        vall[g, rows(r), :] = quarters(quad, BLOCK, WIDTH)

        @pl.when(goes_left(r))
        def _():
            xcopy(g, r, next_r.at[r], g_prev).start()

        @pl.when(goes_right(r))
        def _():
            xcopy(g, r, prev_r.at[r], g_next).start()

    for j in range(HALF):
        to_after(j).wait_recv()
        to_before(j).wait_recv()
        if j == 0:
            for k in range(HALF):
                split_window(0, ROW_BLOCKS - 1 - k)
                split_window(2, k)
        split_window(0, HALF - 1 - j)
        split_window(2, HALF + j)
        for r in (HALF + j, HALF - 1 - j):
            image(r)
            keep_split(g, r)
        if j == 0:
            pl.semaphore_wait(word.at[2], 2)
            tell(word.at[3], near_y)

    pl.semaphore_wait(word.at[3], 2)
    tell(word.at[4], near_y)

    def place(kind, block):
        for core in range(CORES):
            part = block[core * WIDTH // CORES:(core + 1) * WIDTH // CORES]
            tb[core, kind * TILES_G:(kind + 1) * TILES_G] = part.reshape(TILES_G, 8, WIDTH)

    def core_sum(first, count, send, recv):
        part = pl.ds(first, count)
        copy = remote(tb.at[1 - c, part], r1.at[part], send, recv, pts=sibling)
        return copy, part

    def scatter(y_to, far):
        to = y_to * ZS + lax.rem(z + far, ZS)
        return remote(s1.at[to], r2.at[here], p2_s, p2_r, pts=device(to))

    def scatter_rows(y_to):
        for far in NEAR_LAST[:-1]:
            scatter(y_to, far).start()

        @pl.when(y != y_to)
        def _():
            scatter(y_to, 0).start()

    def sum_tile():
        arrived(p2_r, r2.at[pl.ds(1, PLANE - 1)])
        r2[here] = s1[here]
        gb[g, c, here] = jnp.sum(r2[...], axis=0)
        ref = gb.at[g, c, here]
        for over in (2, 1, 3, 0):
            for far in NEAR_LAST:
                if over or far:
                    to = lax.rem(y + over, YS) * ZS + lax.rem(z + far, ZS)
                    remote(ref, ref, p4_s, p4_r.at[y], pts=device(to)).start()

    acc[...] = jnp.zeros_like(acc)
    acc2[...] = jnp.zeros_like(acc2)
    place(3, quarters(dot_t(vhl[g], vhl[g]), WIDTH, WIDTH))
    own_core, own_part = core_sum(LATE, TILES_G, p1_s.at[0], p1_r.at[0])
    own_core.start()

    for j in range(HALF):
        for r in (HALF + j, HALF - 1 - j):
            @pl.when(has_next(r))
            def _():
                arrived(next_r.at[r], several(1))
                keep_split(g_next, r)

            @pl.when(has_prev(r))
            def _():
                arrived(prev_r.at[r], several(1))
                keep_split(g_prev, r)

            @pl.when(between(r))
            def _():
                left = jnp.concatenate([vhl[g, rows(r), :], vhl[g_prev, rows(r), :]], axis=1)
                acc[...] += dot_t(left, vhl[g_next, rows(r), :])

            if r < HALF:
                @pl.when(turn(r) == 3)
                def _():
                    acc[:2 * WIDTH] += dot_t(vhl[g, rows(r), :], vhl[g_next, rows(r), :])

            @pl.when(prev_pair(r))
            def _():
                acc2[...] += dot_t(vhl[g_prev, rows(r), :], vhl[g, rows(r), :])

        if j == 1:
            own_core.wait_recv()
            s1[own_part] = tb[c, own_part] + r1[own_part]
            pl.semaphore_wait(word.at[4], 2)
            scatter_rows(YS - 1)

    place(0, quarters(acc[:2 * WIDTH], WIDTH, WIDTH))
    place(1, quarters(acc2[...], WIDTH, WIDTH))
    place(2, quarters(acc[2 * WIDTH:], WIDTH, WIDTH))

    late_core, late_part = core_sum(0, LATE, p1_s.at[1], p1_r.at[1])
    late_core.start()
    late_core.wait_recv()
    s1[late_part] = tb[c, late_part] + r1[late_part]

    for y_to in range(YS - 1):
        scatter_rows(y_to)

    for r in range(ROW_BLOCKS):
        @pl.when(jnp.logical_not(goes_left(r)))
        def _():
            xcopy(g, r, rest_r.at[0], g_prev).start()

        @pl.when(jnp.logical_not(goes_right(r)))
        def _():
            xcopy(g, r, rest_r.at[1], g_next).start()

        @pl.when(between(r))
        def _():
            xcopy(g_prev, r, rest_r.at[2], g_next).start()
            xcopy(g_next, r, rest_r.at[3], g_prev).start()

    sum_tile()

    pl.semaphore_wait(word.at[1], 2)

    def of_set(n):
        return pl.ds(n * TILES_G, TILES_G)

    def x_share(k, n):
        ref = gb.at[g, c, of_set(n)]
        return remote(ref, ref, p5_s, p5_r.at[GROUPS - k, n], cols=lax.rem(g + k, GROUPS))

    def core_share(k, n):
        ref = gb.at[lax.rem(g + k, GROUPS), c, of_set(n)]
        return remote(ref, ref, p6_s, p6_r, pts=sibling)

    for n in (3, 0, 1, 2):
        @pl.when(y == n)
        def _():
            arrived(p4_r.at[n], gb.at[g, c, pl.ds(0, TILES_G - 1)])

        @pl.when(y != n)
        def _():
            arrived(p4_r.at[n], gb.at[g, c, pl.ds(0, TILES_G)])

        for k in (2, 1, 3):
            x_share(k, n).start()
        core_share(0, n).start()

    for n in (3, 0, 1, 2):
        for k in (1, 3, 2):
            arrived(p5_r.at[k, n], gb.at[g, c, of_set(n)])
            core_share(k, n).start()
    arrived(rest_r.at[0], several(3))
    arrived(rest_r.at[1], several(3))
    arrived(rest_r.at[2], several(4))
    arrived(rest_r.at[3], several(4))
    for r in range(ROW_BLOCKS):
        keep_split(g_opp, r)

        @pl.when(jnp.logical_not(has_next(r)))
        def _():
            keep_split(g_next, r)

        @pl.when(jnp.logical_not(has_prev(r)))
        def _():
            keep_split(g_prev, r)

    arrived(p6_r, gb.at[:, 1 - c])

    def part(a, kind):
        return jnp.concatenate(
            [gb[a, core, kind * TILES_G:(kind + 1) * TILES_G].reshape(WIDTH // CORES, WIDTH) for core in range(CORES)], axis=0
        )

    diag = [part(a, 3) for a in range(GROUPS)]
    down = [lax.rsqrt(jnp.sum(d * eye, axis=1, keepdims=True)) for d in diag]
    across = [lax.rsqrt(jnp.sum(d * eye, axis=0, keepdims=True)) for d in diag]

    def put(a, h, block):
        rows, cols = slice(a * WIDTH, (a + 1) * WIDTH), slice(h * WIDTH, (h + 1) * WIDTH)
        block = block * down[a] * across[h]
        if a == h:
            block = block - eye
        high, low = split(block)
        e0[rows, cols] = block
        e0_h[rows, cols] = high
        e0_l[rows, cols] = low
        block = -(mk[rows, cols] * block)
        w[rows, cols] = block
        high, low = split(block)
        w_h[rows, cols] = high
        w_l[rows, cols] = low

    for a in range(GROUPS):
        scol[a * WIDTH:(a + 1) * WIDTH, :] = jnp.broadcast_to(down[a], (WIDTH, WIDTH))
        put(a, a, diag[a])
        h = (a + 1) % GROUPS
        block = part(a, 0) + part(h, 1)
        put(a, h, block)
        put(h, a, block.T)
    for a in range(GROUPS // 2):
        h = a + GROUPS // 2
        block = part((a + 1) % GROUPS, 2) + part((a + 3) % GROUPS, 2).T
        put(a, h, block)
        put(h, a, block.T)

    def newton(w_h, next_h, fine):
        for n in range(2):
            cols = slice(n * COLS // 2, (n + 1) * COLS // 2)
            prod = dot(e0_h[...], w_h[:, cols])
            if fine:
                prod += dot(e0_l[...], w_h[:, cols]) + dot(e0_h[...], w_l[:, cols])
            value = (e0[:, cols] + w[:, cols]) + prod
            b[:, cols] = value
            high, low = split(value)
            b_h[:, cols] = high
            if fine:
                b_l[:, cols] = low
        for n in range(2):
            cols = slice(n * COLS // 2, (n + 1) * COLS // 2)
            prod = dot_t(w_h[...], b_h[:, cols])
            if fine:
                prod += dot_t(w_l[...], b_h[:, cols]) + dot_t(w_h[...], b_l[:, cols])
            down_id = lax.broadcasted_iota(jnp.int32, (COLS, COLS // 2), 0)
            across_id = lax.broadcasted_iota(jnp.int32, (COLS, COLS // 2), 1) + n * COLS // 2
            own = jnp.where(down_id == across_id, w[:, cols], 0.0)
            value = mk[:, cols] * ((b[:, cols] + own) + prod)
            if fine:
                for k in range(2):
                    u_by[2 * n + k] = value[:, k * WIDTH:(k + 1) * WIDTH]
            else:
                u[:, cols] = value
                u_h[:, cols] = value.astype(BF16)
            if fine:
                res[...] += jnp.sum((value * value).reshape(COLS // 8, 8, COLS // 2), axis=0)
        if fine:
            return
        for n in range(2):
            cols = slice(n * COLS // 2, (n + 1) * COLS // 2)
            value = (w[:, cols] - u[:, cols]) - dot(w_h[...], u_h[:, cols])
            w[:, cols] = value
            for k in range(2):
                w_by[2 * n + k] = value[:, k * WIDTH:(k + 1) * WIDTH]
            high, low = split(value)
            next_h[:, cols] = high
            w_l[:, cols] = low

    res[...] = jnp.zeros_like(res)
    newton(w_h, w2_h, False)
    newton(w2_h, None, True)
    small[0, 0] = jnp.where(jnp.sum(res[...]) < TOLERANCE, 1, 0).astype(jnp.int32)

    step = u_by[g]
    inverse = (w_by[g] - step) - dot(w2_h[...], step.astype(BF16))
    for a in range(GROUPS):
        rows_a = slice(a * WIDTH, (a + 1) * WIDTH)
        same = jnp.where(g == a, 1.0, 0.0).astype(F32)
        high, low = split(scol[rows_a, :] * (inverse[rows_a] + same * eye))
        x_hl[rows_a, :WIDTH] = high
        x_hl[rows_a, WIDTH:] = low

    for k in range(ROW_BLOCKS // 2):
        rows_k = slice(k * 2 * BLOCK, (k + 1) * 2 * BLOCK)
        high = jnp.concatenate([vhl[h, rows_k, :WIDTH] for h in range(GROUPS)], axis=1)
        low = jnp.concatenate([vhl[h, rows_k, WIDTH:] for h in range(GROUPS)], axis=1)
        q = dot(jnp.concatenate([high, low], axis=0), x_hl[...])
        out[rows_k, :] = quarters(q, 2 * BLOCK, WIDTH)

    arrived(halo_s.at[0], win.at[0])
    arrived(halo_s.at[1], win.at[2])
    arrived(v_s, vall.at[:3])
    own_core.wait_send()
    late_core.wait_send()
    arrived(p2_s, s1.at[pl.ds(0, TILES - 1)])
    arrived(p4_s, r2.at[pl.ds(0, PLANE - 1)])
    arrived(p5_s, gb.at[:3, 0])
    arrived(p6_s, gb.at[:, 0])


def fast(start, cov_blocks, col_index, order):
    dma = pltpu.SemaphoreType.DMA
    square = (COLS, COLS)
    hbm = pl.BlockSpec(memory_space=pl.ANY)
    smem = pl.BlockSpec(memory_space=pltpu.SMEM)
    return pl.pallas_call(
        kernel,
        out_shape=(
            pltpu.VMEM((ROWS, WIDTH), F32),
            pltpu.SMEM((1, 1), jnp.int32),
        ),
        in_specs=[hbm, hbm, hbm, hbm],
        out_specs=(pl.BlockSpec(memory_space=pltpu.VMEM), smem),
        scratch_shapes=[
            pltpu.SMEM((ROW_BLOCKS, SLOTS), jnp.int32),
            pltpu.SMEM((GROUPS,), jnp.int32),
            pltpu.VMEM((3, ROWS, WIDTH), F32),
            pltpu.VMEM((3 * ROW_BLOCKS, BLOCK, 2 * WIDTH), BF16),
            pltpu.VMEM((ROW_BLOCKS, SLOTS, BLOCK, BLOCK), F32),
            pltpu.VMEM((ROW_BLOCKS, 2 * BLOCK, SLOTS * BLOCK), BF16),
            pltpu.VMEM((GROUPS, ROWS, WIDTH), F32),
            pltpu.VMEM((GROUPS, ROWS, 2 * WIDTH), BF16),
            pltpu.VMEM((4 * WIDTH, 2 * WIDTH), F32),
            pltpu.VMEM((2 * WIDTH, 2 * WIDTH), F32),
            pltpu.VMEM((CORES, TILES, 8, WIDTH), F32),
            pltpu.VMEM((TILES, 8, WIDTH), F32),
            pltpu.VMEM((TILES, 8, WIDTH), F32),
            pltpu.VMEM((PLANE, 8, WIDTH), F32),
            pltpu.VMEM((GROUPS, CORES, TILES, 8, WIDTH), F32),
            pltpu.VMEM(square, F32),
            pltpu.VMEM(square, F32),
            pltpu.VMEM(square, F32),
            pltpu.VMEM(square, F32),
            pltpu.VMEM(square, F32),
            pltpu.VMEM(square, BF16),
            pltpu.VMEM(square, BF16),
            pltpu.VMEM(square, BF16),
            pltpu.VMEM(square, BF16),
            pltpu.VMEM(square, BF16),
            pltpu.VMEM(square, BF16),
            pltpu.VMEM(square, BF16),
            pltpu.VMEM(square, BF16),
            pltpu.VMEM((GROUPS, COLS, WIDTH), F32),
            pltpu.VMEM((GROUPS, COLS, WIDTH), F32),
            pltpu.VMEM((COLS, 2 * WIDTH), BF16),
            pltpu.VMEM((8, COLS // 2), F32),
            pltpu.VMEM((COLS, WIDTH), F32),
            pltpu.SemaphoreType.REGULAR((5,)),
            dma((2,)),
            dma, dma,
            dma((2,)), dma((2, HALF)),
            dma, dma((ROW_BLOCKS,)), dma((ROW_BLOCKS,)), dma((4,)),
            dma((2,)), dma((2,)),
            dma, dma,
            dma, dma((KINDS,)),
            dma, dma((GROUPS, KINDS)),
            dma, dma,
        ],
        compiler_params=pltpu.CompilerParams(
            collective_id=0, has_side_effects=True, vmem_limit_bytes=56 * 1024 * 1024
        ),
    )(start, cov_blocks, col_index, order)


def body(start, cov_blocks, col_index, order):
    result, small = fast(start, cov_blocks, col_index, order)
    return lax.cond(
        small[0, 0] == 1,
        lambda: result,
        lambda: careful(start, cov_blocks, col_index, order),
    )


def solution(mesh):
    placed = (P("pts", "cols"), P("pts", None, None, None), P("pts", None), P())
    return jax.shard_map(
        body, mesh=mesh, in_specs=placed, out_specs=P("pts", "cols"), check_vma=False
    )
```

```python
import jax
import jax.numpy as jnp
from jax import lax
from jax.experimental import pallas as pl
from jax.experimental.pallas import tpu as pltpu
from jax.sharding import PartitionSpec as P

MESH = pl.DeviceIdType.MESH
F32 = jnp.float32
BF16 = jnp.bfloat16
GROUPS = 4
WIDTH = 128
BLOCK = 128
ROW_BLOCKS = 8
SLOTS = 8
NBLK = 512
YS, ZS, CORES = 4, 8, 2
COLS = GROUPS * WIDTH
ROWS = ROW_BLOCKS * BLOCK
HALF = ROW_BLOCKS // 2
PLANE = YS * ZS
TILES_G = WIDTH // CORES // 8
KINDS = 4
TILES = KINDS * TILES_G
LATE = TILES - TILES_G
NEAR_LAST = (4, 3, 5, 2, 6, 1, 7, 0)
TOLERANCE = 4e-4


def total(value, axis):
    distance = 1
    while distance < lax.axis_size(axis):
        pairs = [(i, i ^ distance) for i in range(lax.axis_size(axis))]
        value = value + lax.ppermute(value, axis, pairs)
        distance *= 2
    return value


def broadcast(value, axis, source):
    kept = jnp.where(lax.axis_index(axis) == source, value, 0).astype(value.dtype)
    return total(kept, axis)


def with_halo(cells, axis, width):
    count = lax.axis_size(axis)
    head = lax.slice_in_dim(cells, 0, width, axis=0)
    tail = lax.slice_in_dim(cells, cells.shape[0] - width, cells.shape[0], axis=0)
    return jnp.concatenate(
        [
            lax.ppermute(tail, axis, [(i, (i + 1) % count) for i in range(count)]),
            cells,
            lax.ppermute(head, axis, [((i + 1) % count, i) for i in range(count)]),
        ],
        axis=0,
    )


def inner(left, right):
    return lax.dot_general(
        left,
        right,
        (((0,), (0,)), ((), ())),
        precision=lax.Precision.HIGHEST,
        preferred_element_type=F32,
    )


def careful(start, cov_blocks, col_index, order):
    rows, group_size = start.shape
    blocks_dev = cov_blocks.shape[0]
    block = cov_blocks.shape[2]
    total_blocks = blocks_dev * lax.axis_size("pts")
    groups = lax.axis_size("cols")
    mine = lax.axis_index("cols")
    positions = jnp.arange(groups, dtype=jnp.int32)
    rank = jnp.sum(jnp.where(order == mine, positions, 0))
    first_block = lax.axis_index("pts") * blocks_dev - blocks_dev
    relative = jnp.mod(col_index - first_block, total_blocks)
    tiles = with_halo(start, "pts", rows).reshape(3 * blocks_dev, block, group_size)[relative]
    local = jnp.einsum(
        "rsab,rsbk->rak", cov_blocks, tiles, precision=lax.Precision.HIGHEST
    ).reshape(rows, group_size)

    def step(t, local):
        owner = order[t]
        gram = total(inner(local, local), "pts")
        lower = jnp.linalg.cholesky(gram)
        candidate = lax.linalg.triangular_solve(
            lower, local, left_side=False, lower=True, transpose_a=True
        )
        ortho = broadcast(candidate, "cols", owner)
        coef = total(inner(ortho, local), "pts")
        updated = local - jnp.dot(
            ortho, coef, precision=lax.Precision.HIGHEST, preferred_element_type=F32
        )
        return jnp.where(rank > t, updated, jnp.where(mine == owner, ortho, local))

    return lax.fori_loop(0, groups, step, local)


def split(x):
    high = x.astype(BF16)
    return high, (x - high.astype(F32)).astype(BF16)


def quarters(q, m, n):
    return (q[:m, :n] + q[m:, n:]) + (q[:m, n:] + q[m:, :n])


def dot(a, b):
    return jnp.dot(a, b, preferred_element_type=F32)


def dot_t(a, b):
    return lax.dot_general(a, b, (((0,), (0,)), ((), ())), preferred_element_type=F32)


def kernel(
    start, cov, col_in, order_in, out, small,
    col_index, order,
    win, win_hl, covv, cov_hl, vall, vhl, acc, acc2, tb, r1, s1, r2, gb,
    nat, e0, b, u, e0_h, e0_l, w_h, w2_h, b_h, b_l, u_h, w_by, u_by, inv, x_hl, res,
    word, i_sem, c_sem, l_sem,
    halo_s, halo_r, v_s, next_r, prev_r, rest_r,
    p1_s, p1_r, p2_s, p2_r, p4_s, p4_r, p5_s, p5_r, p6_s, p6_r,
):
    p = lax.axis_index("pts")
    g = lax.axis_index("cols")
    npts = YS * ZS * CORES
    c = lax.rem(p, CORES)
    z = lax.rem(lax.div(p, CORES), ZS)
    y = lax.div(p, CORES * ZS)
    before, after = lax.rem(p + npts - 1, npts), lax.rem(p + 1, npts)
    sibling = p + 1 - 2 * c
    g_next, g_prev, g_opp = (lax.rem(g + k, GROUPS) for k in (1, 3, 2))

    here = y * ZS + z

    def peer(k):
        y_to, z_to = lax.rem(y + lax.div(k, ZS), YS), lax.rem(z + lax.rem(k, ZS), ZS)
        return y_to * ZS + z_to

    def device(chip):
        return chip * CORES + c

    def remote(src, dst, send, recv, **where):
        return pltpu.make_async_remote_copy(
            src_ref=src, dst_ref=dst, send_sem=send, recv_sem=recv,
            device_id=where, device_id_type=MESH,
        )

    cov_copy = pltpu.make_async_copy(cov, covv, c_sem)
    own_copy = pltpu.make_async_copy(start, win.at[1], l_sem)
    own_copy.start()
    col_copy = pltpu.make_async_copy(col_in, col_index, i_sem.at[0])
    col_copy.start()
    order_copy = pltpu.make_async_copy(order_in, order, i_sem.at[1])
    order_copy.start()

    cov_copy.start()

    barrier = pltpu.get_barrier_semaphore()
    near_x = [dict(cols=h) for h in (g_next, g_prev)]
    near_z = [dict(pts=device(peer(k))) for k in (1, ZS - 1)]
    near_y = [dict(pts=device(peer(k))) for k in (ZS, (YS - 1) * ZS)]
    next_z = [dict(pts=device(peer(k))) for k in (2, ZS - 2)]
    neighbours = [dict(pts=before), dict(pts=after)] + near_x + near_z + near_y

    def tell(sem, devices):
        for one in devices:
            pl.semaphore_signal(sem, inc=1, device_id=one, device_id_type=MESH)

    tell(barrier, neighbours)
    pl.semaphore_wait(barrier, len(neighbours))
    tell(word.at[0], near_z)
    tell(word.at[1], near_x)

    def halo_rows(side, k):
        count = HALF + 1 if k == 0 else 1
        low = HALF - 1 - k if side == 0 else (0 if k == 0 else HALF + k)
        return slice(low * BLOCK, (low + count) * BLOCK)

    def to_after(k):
        rows = halo_rows(0, k)
        return remote(start.at[rows, :], win.at[0, rows, :], halo_s.at[0], halo_r.at[0, k], pts=after)

    def to_before(k):
        rows = halo_rows(2, k)
        return remote(start.at[rows, :], win.at[2, rows, :], halo_s.at[1], halo_r.at[1, k], pts=before)

    for k in range(HALF):
        to_after(k).start()
        to_before(k).start()

    col_copy.wait()
    order_copy.wait()
    ranks = []
    for a in range(GROUPS):
        rank = jnp.int32(0)
        for t in range(1, GROUPS):
            rank += jnp.where(order[t] == a, t, 0)
        ranks.append(lax.min(rank, GROUPS - 1))
    row_id = lax.broadcasted_iota(jnp.int32, (WIDTH, WIDTH), 0)
    col_id = lax.broadcasted_iota(jnp.int32, (WIDTH, WIDTH), 1)
    eye = (row_id == col_id).astype(F32)

    cov_copy.wait()

    def split_cov(r, carry):
        for s in range(SLOTS):
            high, low = split(covv[r, s])
            cov_hl[r, :BLOCK, s * BLOCK:(s + 1) * BLOCK] = high
            cov_hl[r, BLOCK:, s * BLOCK:(s + 1) * BLOCK] = low
        return carry

    lax.fori_loop(0, ROW_BLOCKS, split_cov, 0)

    pl.semaphore_wait(word.at[0], 2)
    tell(word.at[2], next_z)
    def split_window(side, k):
        rows = pl.ds(k * BLOCK if isinstance(k, int) else pl.multiple_of(k * BLOCK, BLOCK), BLOCK)
        high, low = split(win[side, rows, :])
        win_hl[side * ROW_BLOCKS + k, :, :WIDTH] = high
        win_hl[side * ROW_BLOCKS + k, :, WIDTH:] = low

    def split_own(k, carry):
        split_window(1, k)
        return carry

    own_copy.wait()
    lax.fori_loop(0, ROW_BLOCKS, split_own, 0)

    base = p * ROW_BLOCKS - ROW_BLOCKS - NBLK

    def rows(r):
        return slice(r * BLOCK, (r + 1) * BLOCK)

    def turn(r):
        return lax.rem(g + GROUPS - r % GROUPS, GROUPS)

    def goes_left(r):
        t = turn(r)
        return (t >= 2) | (t == 0) if r < HALF else t >= 2

    def goes_right(r):
        t = turn(r)
        return t <= 1 if r < HALF else (t <= 1) | (t == 3)

    def between(r):
        t = turn(r)
        return (t == 1) | (t == 2)

    def has_next(r):
        t = turn(r)
        return t >= 1 if r < HALF else (t == 1) | (t == 2)

    def has_prev(r):
        t = turn(r)
        return (t == 1) | (t == 2) if r < HALF else t <= 2

    def prev_pair(r):
        t = turn(r)
        return t == 1 if r < HALF else t <= 1

    def xcopy(src, r, recv, to):
        ref = vall.at[src, rows(r), :]
        return remote(ref, ref, v_s, recv, cols=to)

    def arrived(sem, ref):
        pltpu.make_async_copy(ref, ref, sem).wait()

    def several(count):
        return vall.at[0, :count * BLOCK, :]

    def keep_split(src, r):
        high, low = split(vall[src, rows(r), :])
        vhl[src, rows(r), :WIDTH] = high
        vhl[src, rows(r), WIDTH:] = low

    def image(r):
        tiles = []
        for s in range(SLOTS):
            rel = lax.rem(col_index[r, s] - base, NBLK)
            tiles.append(win_hl[lax.min(rel, 3 * ROW_BLOCKS - 1)])
        quad = dot(cov_hl[r], jnp.concatenate(tiles, axis=0))
        vall[g, rows(r), :] = quarters(quad, BLOCK, WIDTH)

        @pl.when(goes_left(r))
        def _():
            xcopy(g, r, next_r.at[r], g_prev).start()

        @pl.when(goes_right(r))
        def _():
            xcopy(g, r, prev_r.at[r], g_next).start()

    for j in range(HALF):
        to_after(j).wait_recv()
        to_before(j).wait_recv()
        if j == 0:
            for k in range(HALF):
                split_window(0, ROW_BLOCKS - 1 - k)
                split_window(2, k)
        split_window(0, HALF - 1 - j)
        split_window(2, HALF + j)
        for r in (HALF + j, HALF - 1 - j):
            image(r)
            keep_split(g, r)
        if j == 0:
            pl.semaphore_wait(word.at[2], 2)
            tell(word.at[3], near_y)

    pl.semaphore_wait(word.at[3], 2)
    tell(word.at[4], near_y)

    def place(kind, block):
        for core in range(CORES):
            part = block[core * WIDTH // CORES:(core + 1) * WIDTH // CORES]
            tb[core, kind * TILES_G:(kind + 1) * TILES_G] = part.reshape(TILES_G, 8, WIDTH)

    def core_sum(first, count, send, recv):
        part = pl.ds(first, count)
        copy = remote(tb.at[1 - c, part], r1.at[part], send, recv, pts=sibling)
        return copy, part

    def scatter(y_to, far):
        to = y_to * ZS + lax.rem(z + far, ZS)
        return remote(s1.at[to], r2.at[here], p2_s, p2_r, pts=device(to))

    def scatter_rows(y_to):
        for far in NEAR_LAST[:-1]:
            scatter(y_to, far).start()

        @pl.when(y != y_to)
        def _():
            scatter(y_to, 0).start()

    def sum_tile():
        arrived(p2_r, r2.at[pl.ds(1, PLANE - 1)])
        r2[here] = s1[here]
        gb[g, c, here] = jnp.sum(r2[...], axis=0)
        ref = gb.at[g, c, here]
        for over in (2, 1, 3, 0):
            for far in NEAR_LAST:
                if over or far:
                    to = lax.rem(y + over, YS) * ZS + lax.rem(z + far, ZS)
                    remote(ref, ref, p4_s, p4_r.at[y], pts=device(to)).start()

    acc[...] = jnp.zeros_like(acc)
    acc2[...] = jnp.zeros_like(acc2)
    place(3, quarters(dot_t(vhl[g], vhl[g]), WIDTH, WIDTH))
    own_core, own_part = core_sum(LATE, TILES_G, p1_s.at[0], p1_r.at[0])
    own_core.start()

    for j in range(HALF):
        for r in (HALF + j, HALF - 1 - j):
            @pl.when(has_next(r))
            def _():
                arrived(next_r.at[r], several(1))
                keep_split(g_next, r)

            @pl.when(has_prev(r))
            def _():
                arrived(prev_r.at[r], several(1))
                keep_split(g_prev, r)

            @pl.when(between(r))
            def _():
                left = jnp.concatenate([vhl[g, rows(r), :], vhl[g_prev, rows(r), :]], axis=1)
                acc[...] += dot_t(left, vhl[g_next, rows(r), :])

            if r < HALF:
                @pl.when(turn(r) == 3)
                def _():
                    acc[:2 * WIDTH] += dot_t(vhl[g, rows(r), :], vhl[g_next, rows(r), :])

            @pl.when(prev_pair(r))
            def _():
                acc2[...] += dot_t(vhl[g_prev, rows(r), :], vhl[g, rows(r), :])

        if j == 1:
            own_core.wait_recv()
            s1[own_part] = tb[c, own_part] + r1[own_part]
            pl.semaphore_wait(word.at[4], 2)
            scatter_rows(YS - 1)

    place(0, quarters(acc[:2 * WIDTH], WIDTH, WIDTH))
    place(1, quarters(acc2[...], WIDTH, WIDTH))
    place(2, quarters(acc[2 * WIDTH:], WIDTH, WIDTH))

    late_core, late_part = core_sum(0, LATE, p1_s.at[1], p1_r.at[1])
    late_core.start()
    late_core.wait_recv()
    s1[late_part] = tb[c, late_part] + r1[late_part]

    for y_to in range(YS - 1):
        scatter_rows(y_to)

    for r in range(ROW_BLOCKS):
        @pl.when(jnp.logical_not(goes_left(r)))
        def _():
            xcopy(g, r, rest_r.at[0], g_prev).start()

        @pl.when(jnp.logical_not(goes_right(r)))
        def _():
            xcopy(g, r, rest_r.at[1], g_next).start()

        @pl.when(between(r))
        def _():
            xcopy(g_prev, r, rest_r.at[2], g_next).start()
            xcopy(g_next, r, rest_r.at[3], g_prev).start()

    sum_tile()

    pl.semaphore_wait(word.at[1], 2)

    def of_set(n):
        return pl.ds(n * TILES_G, TILES_G)

    def x_share(k, n):
        ref = gb.at[g, c, of_set(n)]
        return remote(ref, ref, p5_s, p5_r.at[GROUPS - k, n], cols=lax.rem(g + k, GROUPS))

    def core_share(k, n):
        ref = gb.at[lax.rem(g + k, GROUPS), c, of_set(n)]
        return remote(ref, ref, p6_s, p6_r, pts=sibling)

    for n in (3, 0, 1, 2):
        @pl.when(y == n)
        def _():
            arrived(p4_r.at[n], gb.at[g, c, pl.ds(0, TILES_G - 1)])

        @pl.when(y != n)
        def _():
            arrived(p4_r.at[n], gb.at[g, c, pl.ds(0, TILES_G)])

        for k in (2, 1, 3):
            x_share(k, n).start()
        core_share(0, n).start()

    for n in (3, 0, 1, 2):
        for k in (1, 3, 2):
            arrived(p5_r.at[k, n], gb.at[g, c, of_set(n)])
            core_share(k, n).start()
    arrived(rest_r.at[0], several(3))
    arrived(rest_r.at[1], several(3))
    arrived(rest_r.at[2], several(4))
    arrived(rest_r.at[3], several(4))
    for r in range(ROW_BLOCKS):
        keep_split(g_opp, r)

        @pl.when(jnp.logical_not(has_next(r)))
        def _():
            keep_split(g_next, r)

        @pl.when(jnp.logical_not(has_prev(r)))
        def _():
            keep_split(g_prev, r)

    arrived(p6_r, gb.at[:, 1 - c])

    def part(a, kind):
        return jnp.concatenate(
            [gb[a, core, kind * TILES_G:(kind + 1) * TILES_G].reshape(WIDTH // CORES, WIDTH) for core in range(CORES)], axis=0
        )

    diag = [part(a, 3) for a in range(GROUPS)]
    down = [lax.rsqrt(jnp.sum(d * eye, axis=1, keepdims=True)) for d in diag]
    across = [lax.rsqrt(jnp.sum(d * eye, axis=0, keepdims=True)) for d in diag]

    def put(a, h, block):
        block = block * down[a] * across[h]
        nat[a, h] = block - eye if a == h else block

    for a in range(GROUPS):
        put(a, a, diag[a])
        h = (a + 1) % GROUPS
        block = part(a, 0) + part(h, 1)
        put(a, h, block)
        put(h, a, block.T)
    for a in range(GROUPS // 2):
        h = a + GROUPS // 2
        block = part((a + 1) % GROUPS, 2) + part((a + 3) % GROUPS, 2).T
        put(a, h, block)
        put(h, a, block.T)

    side = COLS // 2
    first, second = slice(0, side), slice(side, COLS)
    parts = ((first, first), (first, second), (second, second))
    down_id = lax.broadcasted_iota(jnp.int32, (side, side), 0)
    across_id = lax.broadcasted_iota(jnp.int32, (side, side), 1)
    half_eye = jnp.where(down_id == across_id, 0.5, 0.0).astype(F32)
    upper = jnp.where(down_id < across_id, 1.0, 0.0).astype(F32) + half_eye
    w_h[second, first] = jnp.zeros((side, side), BF16)
    for t in range(GROUPS):
        for v in range(GROUPS):
            block = nat[order[t], order[v]]
            at = (slice(t * WIDTH, (t + 1) * WIDTH), slice(v * WIDTH, (v + 1) * WIDTH))
            high, low = split(block)
            e0_h[at] = high
            e0_l[at] = low
            e0[at] = block
    for m, n in parts:
        block = e0[m, n] if m != n else upper * e0[m, n]
        w_h[m, n] = (-block).astype(BF16)

    def newton(w_h, next_h, fine):
        for m, n in parts:
            depth = first if n == first else slice(0, COLS)
            prod = dot(e0_h[m, depth], w_h[depth, n])
            if fine:
                prod += dot(e0_l[m, depth], w_h[depth, n])
            value = (e0[m, n] + w_h[m, n].astype(F32)) + prod
            b[m, n] = value
            high, low = split(value)
            b_h[m, n] = high
            if fine:
                b_l[m, n] = low
        for m, n in parts:
            depth = first if m == first else slice(0, COLS)
            prod = dot_t(w_h[depth, m], b_h[depth, n])
            if fine:
                prod += dot_t(w_h[depth, m], b_l[depth, n])
            value = b[m, n] + prod
            if m == n:
                value = upper * value + half_eye * w_h[m, n].astype(F32)
            if fine:
                for k in range(2):
                    u_by[(2 if n == second else 0) + k, m] = value[:, k * WIDTH:(k + 1) * WIDTH]
                res[...] += jnp.sum((value * value).reshape(side // 8, 8, side), axis=0)
            else:
                u[m, n] = value
                u_h[m, n] = value.astype(BF16)
        if fine:
            return
        next_h[second, first] = jnp.zeros((side, side), BF16)
        for m, n in parts:
            depth = slice(m.start, n.stop)
            value = (w_h[m, n].astype(F32) - u[m, n]) - dot(w_h[m, depth], u_h[depth, n])
            high = value.astype(BF16)
            next_h[m, n] = high
            for k in range(2):
                w_by[(2 if n == second else 0) + k, m] = high[:, k * WIDTH:(k + 1) * WIDTH]

    res[...] = jnp.zeros_like(res)
    for k in range(2):
        u_by[k, second] = jnp.zeros((side, WIDTH), F32)
        w_by[k, second] = jnp.zeros((side, WIDTH), BF16)
    newton(w_h, w2_h, False)
    newton(w2_h, None, True)
    small[0, 0] = jnp.where(jnp.sum(res[...]) < TOLERANCE, 1, 0).astype(jnp.int32)

    rank = jnp.int32(0)
    for t in range(1, GROUPS):
        rank += jnp.where(order[t] == g, t, 0)
    rank = lax.min(rank, GROUPS - 1)
    step = u_by[rank]
    inverse = (w_by[rank].astype(F32) - step) - dot(w2_h[...], step.astype(BF16))
    for t in range(GROUPS):
        inv[t] = inverse[t * WIDTH:(t + 1) * WIDTH]
    for a in range(GROUPS):
        rows_a = slice(a * WIDTH, (a + 1) * WIDTH)
        same = jnp.where(g == a, 1.0, 0.0).astype(F32)
        high, low = split(down[a] * (inv[ranks[a]] + same * eye))
        x_hl[rows_a, :WIDTH] = high
        x_hl[rows_a, WIDTH:] = low

    for k in range(ROW_BLOCKS // 2):
        rows_k = slice(k * 2 * BLOCK, (k + 1) * 2 * BLOCK)
        high = jnp.concatenate([vhl[h, rows_k, :WIDTH] for h in range(GROUPS)], axis=1)
        low = jnp.concatenate([vhl[h, rows_k, WIDTH:] for h in range(GROUPS)], axis=1)
        q = dot(jnp.concatenate([high, low], axis=0), x_hl[...])
        out[rows_k, :] = quarters(q, 2 * BLOCK, WIDTH)

    arrived(halo_s.at[0], win.at[0])
    arrived(halo_s.at[1], win.at[2])
    arrived(v_s, vall.at[:3])
    own_core.wait_send()
    late_core.wait_send()
    arrived(p2_s, s1.at[pl.ds(0, TILES - 1)])
    arrived(p4_s, r2.at[pl.ds(0, PLANE - 1)])
    arrived(p5_s, gb.at[:3, 0])
    arrived(p6_s, gb.at[:, 0])


def fast(start, cov_blocks, col_index, order):
    dma = pltpu.SemaphoreType.DMA
    square = (COLS, COLS)
    hbm = pl.BlockSpec(memory_space=pl.ANY)
    smem = pl.BlockSpec(memory_space=pltpu.SMEM)
    return pl.pallas_call(
        kernel,
        out_shape=(
            pltpu.VMEM((ROWS, WIDTH), F32),
            pltpu.SMEM((1, 1), jnp.int32),
        ),
        in_specs=[hbm, hbm, hbm, hbm],
        out_specs=(pl.BlockSpec(memory_space=pltpu.VMEM), smem),
        scratch_shapes=[
            pltpu.SMEM((ROW_BLOCKS, SLOTS), jnp.int32),
            pltpu.SMEM((GROUPS,), jnp.int32),
            pltpu.VMEM((3, ROWS, WIDTH), F32),
            pltpu.VMEM((3 * ROW_BLOCKS, BLOCK, 2 * WIDTH), BF16),
            pltpu.VMEM((ROW_BLOCKS, SLOTS, BLOCK, BLOCK), F32),
            pltpu.VMEM((ROW_BLOCKS, 2 * BLOCK, SLOTS * BLOCK), BF16),
            pltpu.VMEM((GROUPS, ROWS, WIDTH), F32),
            pltpu.VMEM((GROUPS, ROWS, 2 * WIDTH), BF16),
            pltpu.VMEM((4 * WIDTH, 2 * WIDTH), F32),
            pltpu.VMEM((2 * WIDTH, 2 * WIDTH), F32),
            pltpu.VMEM((CORES, TILES, 8, WIDTH), F32),
            pltpu.VMEM((TILES, 8, WIDTH), F32),
            pltpu.VMEM((TILES, 8, WIDTH), F32),
            pltpu.VMEM((PLANE, 8, WIDTH), F32),
            pltpu.VMEM((GROUPS, CORES, TILES, 8, WIDTH), F32),
            pltpu.VMEM((GROUPS, GROUPS, WIDTH, WIDTH), F32),
            pltpu.VMEM(square, F32),
            pltpu.VMEM(square, F32),
            pltpu.VMEM(square, F32),
            pltpu.VMEM(square, BF16),
            pltpu.VMEM(square, BF16),
            pltpu.VMEM(square, BF16),
            pltpu.VMEM(square, BF16),
            pltpu.VMEM(square, BF16),
            pltpu.VMEM(square, BF16),
            pltpu.VMEM(square, BF16),
            pltpu.VMEM((GROUPS, COLS, WIDTH), BF16),
            pltpu.VMEM((GROUPS, COLS, WIDTH), F32),
            pltpu.VMEM((GROUPS, WIDTH, WIDTH), F32),
            pltpu.VMEM((COLS, 2 * WIDTH), BF16),
            pltpu.VMEM((8, COLS // 2), F32),
            pltpu.SemaphoreType.REGULAR((5,)),
            dma((2,)),
            dma, dma,
            dma((2,)), dma((2, HALF)),
            dma, dma((ROW_BLOCKS,)), dma((ROW_BLOCKS,)), dma((4,)),
            dma((2,)), dma((2,)),
            dma, dma,
            dma, dma((KINDS,)),
            dma, dma((GROUPS, KINDS)),
            dma, dma,
        ],
        compiler_params=pltpu.CompilerParams(
            collective_id=0, has_side_effects=True, vmem_limit_bytes=56 * 1024 * 1024
        ),
    )(start, cov_blocks, col_index, order)


def body(start, cov_blocks, col_index, order):
    result, small = fast(start, cov_blocks, col_index, order)
    return lax.cond(
        small[0, 0] == 1,
        lambda: result,
        lambda: careful(start, cov_blocks, col_index, order),
    )


def solution(mesh):
    placed = (P("pts", "cols"), P("pts", None, None, None), P("pts", None), P())
    return jax.shard_map(
        body, mesh=mesh, in_specs=placed, out_specs=P("pts", "cols"), check_vma=False
    )
```

```python
import jax
import jax.numpy as jnp
from jax import lax
from jax.experimental import pallas as pl
from jax.experimental.pallas import tpu as pltpu
from jax.sharding import PartitionSpec as P

MESH = pl.DeviceIdType.MESH
F32 = jnp.float32
BF16 = jnp.bfloat16
GROUPS = 4
WIDTH = 128
BLOCK = 128
ROW_BLOCKS = 8
SLOTS = 8
NBLK = 512
YS, ZS, CORES = 4, 8, 2
COLS = GROUPS * WIDTH
ROWS = ROW_BLOCKS * BLOCK
HALF = ROW_BLOCKS // 2
PLANE = YS * ZS
TILES_G = WIDTH // CORES // 8
KINDS = 4
TILES = KINDS * TILES_G
LATE = TILES - TILES_G
NEAR_LAST = (4, 3, 5, 2, 6, 1, 7, 0)
TOLERANCE = 4e-4


def total(value, axis):
    distance = 1
    while distance < lax.axis_size(axis):
        pairs = [(i, i ^ distance) for i in range(lax.axis_size(axis))]
        value = value + lax.ppermute(value, axis, pairs)
        distance *= 2
    return value


def broadcast(value, axis, source):
    kept = jnp.where(lax.axis_index(axis) == source, value, 0).astype(value.dtype)
    return total(kept, axis)


def with_halo(cells, axis, width):
    count = lax.axis_size(axis)
    head = lax.slice_in_dim(cells, 0, width, axis=0)
    tail = lax.slice_in_dim(cells, cells.shape[0] - width, cells.shape[0], axis=0)
    return jnp.concatenate(
        [
            lax.ppermute(tail, axis, [(i, (i + 1) % count) for i in range(count)]),
            cells,
            lax.ppermute(head, axis, [((i + 1) % count, i) for i in range(count)]),
        ],
        axis=0,
    )


def inner(left, right):
    return lax.dot_general(
        left,
        right,
        (((0,), (0,)), ((), ())),
        precision=lax.Precision.HIGHEST,
        preferred_element_type=F32,
    )


def careful(start, cov_blocks, col_index, order):
    rows, group_size = start.shape
    blocks_dev = cov_blocks.shape[0]
    block = cov_blocks.shape[2]
    total_blocks = blocks_dev * lax.axis_size("pts")
    groups = lax.axis_size("cols")
    mine = lax.axis_index("cols")
    positions = jnp.arange(groups, dtype=jnp.int32)
    rank = jnp.sum(jnp.where(order == mine, positions, 0))
    first_block = lax.axis_index("pts") * blocks_dev - blocks_dev
    relative = jnp.mod(col_index - first_block, total_blocks)
    tiles = with_halo(start, "pts", rows).reshape(3 * blocks_dev, block, group_size)[relative]
    local = jnp.einsum(
        "rsab,rsbk->rak", cov_blocks, tiles, precision=lax.Precision.HIGHEST
    ).reshape(rows, group_size)

    def step(t, local):
        owner = order[t]
        gram = total(inner(local, local), "pts")
        lower = jnp.linalg.cholesky(gram)
        candidate = lax.linalg.triangular_solve(
            lower, local, left_side=False, lower=True, transpose_a=True
        )
        ortho = broadcast(candidate, "cols", owner)
        coef = total(inner(ortho, local), "pts")
        updated = local - jnp.dot(
            ortho, coef, precision=lax.Precision.HIGHEST, preferred_element_type=F32
        )
        return jnp.where(rank > t, updated, jnp.where(mine == owner, ortho, local))

    return lax.fori_loop(0, groups, step, local)


def split(x):
    high = x.astype(BF16)
    return high, (x - high.astype(F32)).astype(BF16)


def quarters(q, m, n):
    return (q[:m, :n] + q[m:, n:]) + (q[:m, n:] + q[m:, :n])


def dot(a, b):
    return jnp.dot(a, b, preferred_element_type=F32)


def dot_t(a, b):
    return lax.dot_general(a, b, (((0,), (0,)), ((), ())), preferred_element_type=F32)


def kernel(
    start, cov, col_in, order_in, out, small,
    col_index, order,
    win, win_hl, covv, cov_hl, vall, vhl, acc, acc2, tb, r1, s1, r2, r3, gb,
    nat, e0, b, u, e0_h, e0_l, w_h, w2_h, b_h, b_l, u_h, w_by, u_by, inv, x_hl, res,
    word, i_sem, c_sem, l_sem,
    halo_s, halo_r, n_s, n_r, v_s, next_r, prev_r, rest_r,
    p1_s, p1_r, p2_s, p2_r, p3_r, p4_s, p4_r, p5_s, p5_r, p6_s, p6_r,
):
    p = lax.axis_index("pts")
    g = lax.axis_index("cols")
    npts = YS * ZS * CORES
    c = lax.rem(p, CORES)
    z = lax.rem(lax.div(p, CORES), ZS)
    y = lax.div(p, CORES * ZS)
    before, after = lax.rem(p + npts - 1, npts), lax.rem(p + 1, npts)
    sibling = p + 1 - 2 * c
    g_next, g_prev, g_opp = (lax.rem(g + k, GROUPS) for k in (1, 3, 2))

    here = y * ZS + z

    def peer(k):
        y_to, z_to = lax.rem(y + lax.div(k, ZS), YS), lax.rem(z + lax.rem(k, ZS), ZS)
        return y_to * ZS + z_to

    def device(chip):
        return chip * CORES + c

    def remote(src, dst, send, recv, **where):
        return pltpu.make_async_remote_copy(
            src_ref=src, dst_ref=dst, send_sem=send, recv_sem=recv,
            device_id=where, device_id_type=MESH,
        )

    cov_copy = pltpu.make_async_copy(cov, covv, c_sem)
    own_copy = pltpu.make_async_copy(start, win.at[1], l_sem)
    own_copy.start()
    col_copy = pltpu.make_async_copy(col_in, col_index, i_sem.at[0])
    col_copy.start()
    order_copy = pltpu.make_async_copy(order_in, order, i_sem.at[1])
    order_copy.start()

    cov_copy.start()

    barrier = pltpu.get_barrier_semaphore()
    near_x = [dict(cols=h) for h in (g_next, g_prev)]
    near_z = [dict(pts=device(peer(k))) for k in (1, ZS - 1)]
    near_y = [dict(pts=device(peer(k))) for k in (ZS, (YS - 1) * ZS)]
    next_z = [dict(pts=device(peer(k))) for k in (2, ZS - 2)]
    neighbours = [dict(pts=before), dict(pts=after)] + near_x + near_z + near_y

    def tell(sem, devices):
        for one in devices:
            pl.semaphore_signal(sem, inc=1, device_id=one, device_id_type=MESH)

    tell(barrier, neighbours)
    pl.semaphore_wait(barrier, len(neighbours))
    tell(word.at[0], near_z)
    tell(word.at[1], near_x)

    def turn_row(j):
        return ROW_BLOCKS - 1 - j + c * (2 * j - ROW_BLOCKS + 1)

    def rows(r):
        return pl.ds(pl.multiple_of(r * BLOCK, BLOCK), BLOCK)

    far_side, near_side = 2 * c, 2 - 2 * c
    far_device = before + c * (after - before)

    def to_far(j):
        block = rows(ROW_BLOCKS - 1 - turn_row(j))
        return remote(start.at[block, :], win.at[near_side, block, :], halo_s, halo_r.at[j], pts=far_device)

    to_near = remote(start, win.at[far_side], n_s, n_r, pts=sibling)
    to_far(0).start()
    to_near.start()
    for j in range(1, ROW_BLOCKS):
        to_far(j).start()

    col_copy.wait()
    order_copy.wait()
    ranks = []
    for a in range(GROUPS):
        rank = jnp.int32(0)
        for t in range(1, GROUPS):
            rank += jnp.where(order[t] == a, t, 0)
        ranks.append(lax.min(rank, GROUPS - 1))
    row_id = lax.broadcasted_iota(jnp.int32, (WIDTH, WIDTH), 0)
    col_id = lax.broadcasted_iota(jnp.int32, (WIDTH, WIDTH), 1)
    eye = (row_id == col_id).astype(F32)

    cov_copy.wait()

    def split_cov(r, carry):
        for s in range(SLOTS):
            high, low = split(covv[r, s])
            cov_hl[r, :BLOCK, s * BLOCK:(s + 1) * BLOCK] = high
            cov_hl[r, BLOCK:, s * BLOCK:(s + 1) * BLOCK] = low
        return carry

    lax.fori_loop(0, ROW_BLOCKS, split_cov, 0)

    def split_window(side, k):
        high, low = split(win[side, rows(k), :])
        win_hl[side * ROW_BLOCKS + k, :, :WIDTH] = high
        win_hl[side * ROW_BLOCKS + k, :, WIDTH:] = low

    def split_own(k, carry):
        split_window(1, k)
        return carry

    def split_near(k, carry):
        split_window(near_side, k)
        return carry

    own_copy.wait()
    lax.fori_loop(0, ROW_BLOCKS, split_own, 0)
    to_near.wait_recv()
    lax.fori_loop(0, ROW_BLOCKS, split_near, 0)

    base = p * ROW_BLOCKS - ROW_BLOCKS - NBLK

    def turn(r):
        return lax.rem(g + GROUPS - lax.rem(r, GROUPS), GROUPS)

    def goes_left(r):
        t = turn(r)
        return (t >= 2) | ((t == 0) & (r < HALF))

    def goes_right(r):
        t = turn(r)
        return (t <= 1) | ((t == 3) & (r >= HALF))

    def between(r):
        t = turn(r)
        return (t == 1) | (t == 2)

    def has_next(r):
        t = turn(r)
        return (t == 1) | (t == 2) | ((t == 3) & (r < HALF))

    def has_prev(r):
        t = turn(r)
        return (t == 1) | (t == 2) | ((t == 0) & (r >= HALF))

    def prev_pair(r):
        t = turn(r)
        return (t == 1) | ((t == 0) & (r >= HALF))

    def xcopy(src, r, recv, to):
        ref = vall.at[src, rows(r), :]
        return remote(ref, ref, v_s, recv, cols=to)

    def arrived(sem, ref):
        pltpu.make_async_copy(ref, ref, sem).wait()

    def several(count):
        return vall.at[0, :count * BLOCK, :]

    def keep_split(src, r):
        high, low = split(vall[src, rows(r), :])
        vhl[src, rows(r), :WIDTH] = high
        vhl[src, rows(r), WIDTH:] = low

    def image(r):
        tiles = []
        for s in range(SLOTS):
            rel = lax.rem(col_index[r, s] - base, NBLK)
            tiles.append(win_hl[lax.min(rel, 3 * ROW_BLOCKS - 1)])
        quad = dot(cov_hl[r], jnp.concatenate(tiles, axis=0))
        vall[g, rows(r), :] = quarters(quad, BLOCK, WIDTH)

        @pl.when(goes_left(r))
        def _():
            xcopy(g, r, next_r.at[r], g_prev).start()

        @pl.when(goes_right(r))
        def _():
            xcopy(g, r, prev_r.at[r], g_next).start()

    for j in range(ROW_BLOCKS):
        r = turn_row(j)
        arrived(halo_r.at[j], win.at[0, pl.ds(0, BLOCK), :])
        split_window(far_side, r)
        image(r)
        keep_split(g, r)
        if j == 0:
            pl.semaphore_wait(word.at[0], 2)
            tell(word.at[2], next_z)
        if j == 3:
            pl.semaphore_wait(word.at[2], 2)
            tell(word.at[3], near_y)

    pl.semaphore_wait(word.at[3], 2)
    tell(word.at[4], near_y)

    def place(kind, block):
        for core in range(CORES):
            part = block[core * WIDTH // CORES:(core + 1) * WIDTH // CORES]
            tb[core, kind * TILES_G:(kind + 1) * TILES_G] = part.reshape(TILES_G, 8, WIDTH)

    def core_sum(first, count, send, recv):
        part = pl.ds(first, count)
        copy = remote(tb.at[1 - c, part], r1.at[part], send, recv, pts=sibling)
        return copy, part

    def scatter(y_to, far):
        to = y_to * ZS + lax.rem(z + far, ZS)
        return remote(s1.at[to], r2.at[here], p2_s, p2_r, pts=device(to))

    def scatter_rows(y_to):
        for far in NEAR_LAST[:-1]:
            scatter(y_to, far).start()

        @pl.when(y != y_to)
        def _():
            scatter(y_to, 0).start()

    def scatter_prev(z_to):
        return remote(s1.at[TILES_G + z_to], r3.at[here], p2_s, p3_r, cols=g_prev, pts=device(z_to))

    def sum_tile():
        arrived(p2_r, r2.at[pl.ds(1, PLANE - 1)])
        r2[here] = s1[here]
        gb[g, c, here] = jnp.sum(r2[...], axis=0)

        @pl.when(y == 0)
        def _():
            arrived(p3_r, r3)
            gb[g, c, here] += jnp.sum(r3[...], axis=0)

        ref = gb.at[g, c, here]
        for over in (2, 1, 3, 0):
            for far in NEAR_LAST:
                if over or far:
                    to = lax.rem(y + over, YS) * ZS + lax.rem(z + far, ZS)
                    remote(ref, ref, p4_s, p4_r.at[y], pts=device(to)).start()

    acc[...] = jnp.zeros_like(acc)
    acc2[...] = jnp.zeros_like(acc2)
    place(3, quarters(dot_t(vhl[g], vhl[g]), WIDTH, WIDTH))
    own_core, own_part = core_sum(LATE, TILES_G, p1_s.at[0], p1_r.at[0])
    own_core.start()

    for j in range(ROW_BLOCKS):
        r = turn_row(j)

        @pl.when(has_next(r))
        def _():
            arrived(next_r.at[r], several(1))
            keep_split(g_next, r)

        @pl.when(has_prev(r))
        def _():
            arrived(prev_r.at[r], several(1))
            keep_split(g_prev, r)

        @pl.when(between(r))
        def _():
            left = jnp.concatenate([vhl[g, rows(r), :], vhl[g_prev, rows(r), :]], axis=1)
            acc[...] += dot_t(left, vhl[g_next, rows(r), :])

        @pl.when((turn(r) == 3) & (r < HALF))
        def _():
            acc[:2 * WIDTH] += dot_t(vhl[g, rows(r), :], vhl[g_next, rows(r), :])

        @pl.when(prev_pair(r))
        def _():
            acc2[...] += dot_t(vhl[g_prev, rows(r), :], vhl[g, rows(r), :])

        if j == 2:
            own_core.wait_recv()
            s1[own_part] = tb[c, own_part] + r1[own_part]
            pl.semaphore_wait(word.at[4], 2)
            tell(word.at[5], near_x)
            scatter_rows(YS - 1)

    place(0, quarters(acc[:2 * WIDTH], WIDTH, WIDTH))
    place(1, quarters(acc2[...], WIDTH, WIDTH))
    place(2, quarters(acc[2 * WIDTH:], WIDTH, WIDTH))

    late_core, late_part = core_sum(0, LATE, p1_s.at[1], p1_r.at[1])
    late_core.start()
    late_core.wait_recv()
    s1[late_part] = tb[c, late_part] + r1[late_part]

    pl.semaphore_wait(word.at[5], 2)
    for far in NEAR_LAST:
        scatter_prev(lax.rem(z + far, ZS)).start()
    scatter_rows(0)
    scatter_rows(2)

    for r in range(ROW_BLOCKS):
        @pl.when(jnp.logical_not(goes_left(r)))
        def _():
            xcopy(g, r, rest_r.at[0], g_prev).start()

        @pl.when(jnp.logical_not(goes_right(r)))
        def _():
            xcopy(g, r, rest_r.at[1], g_next).start()

        @pl.when(between(r))
        def _():
            xcopy(g_prev, r, rest_r.at[2], g_next).start()
            xcopy(g_next, r, rest_r.at[3], g_prev).start()

    @pl.when(y != 1)
    def _():
        sum_tile()

    pl.semaphore_wait(word.at[1], 2)

    def of_set(n):
        return pl.ds(n * TILES_G, TILES_G)

    def x_share(k, n):
        ref = gb.at[g, c, of_set(n)]
        return remote(ref, ref, p5_s, p5_r.at[GROUPS - k, n], cols=lax.rem(g + k, GROUPS))

    def core_share(k, n):
        ref = gb.at[lax.rem(g + k, GROUPS), c, of_set(n)]
        return remote(ref, ref, p6_s, p6_r, pts=sibling)

    for n in (3, 0, 2):
        @pl.when(y == n)
        def _():
            arrived(p4_r.at[n], gb.at[g, c, pl.ds(0, TILES_G - 1)])

        @pl.when(y != n)
        def _():
            arrived(p4_r.at[n], gb.at[g, c, pl.ds(0, TILES_G)])

        for k in (2, 1, 3):
            x_share(k, n).start()
        core_share(0, n).start()

    for n in (3, 0, 2):
        for k in (1, 3, 2):
            arrived(p5_r.at[k, n], gb.at[g, c, of_set(n)])
            core_share(k, n).start()
    arrived(rest_r.at[0], several(3))
    arrived(rest_r.at[1], several(3))
    arrived(rest_r.at[2], several(4))
    arrived(rest_r.at[3], several(4))
    for r in range(ROW_BLOCKS):
        keep_split(g_opp, r)

        @pl.when(jnp.logical_not(has_next(r)))
        def _():
            keep_split(g_next, r)

        @pl.when(jnp.logical_not(has_prev(r)))
        def _():
            keep_split(g_prev, r)

    arrived(p6_r, gb.at[:, 1 - c, pl.ds(0, TILES - TILES_G)])

    def part(a, kind):
        return jnp.concatenate(
            [gb[a, core, kind * TILES_G:(kind + 1) * TILES_G].reshape(WIDTH // CORES, WIDTH) for core in range(CORES)], axis=0
        )

    diag = [part(a, 3) for a in range(GROUPS)]
    down = [lax.rsqrt(jnp.sum(d * eye, axis=1, keepdims=True)) for d in diag]
    across = [lax.rsqrt(jnp.sum(d * eye, axis=0, keepdims=True)) for d in diag]

    def put(a, h, block):
        block = block * down[a] * across[h]
        nat[a, h] = block - eye if a == h else block

    for a in range(GROUPS):
        put(a, a, diag[a])
        h = (a + 1) % GROUPS
        block = part(a, 0)
        put(a, h, block)
        put(h, a, block.T)
    for a in range(GROUPS // 2):
        h = a + GROUPS // 2
        block = part((a + 1) % GROUPS, 2) + part((a + 3) % GROUPS, 2).T
        put(a, h, block)
        put(h, a, block.T)

    side = COLS // 2
    first, second = slice(0, side), slice(side, COLS)
    parts = ((first, first), (first, second), (second, second))
    down_id = lax.broadcasted_iota(jnp.int32, (side, side), 0)
    across_id = lax.broadcasted_iota(jnp.int32, (side, side), 1)
    half_eye = jnp.where(down_id == across_id, 0.5, 0.0).astype(F32)
    upper = jnp.where(down_id < across_id, 1.0, 0.0).astype(F32) + half_eye
    w_h[second, first] = jnp.zeros((side, side), BF16)
    for t in range(GROUPS):
        for v in range(GROUPS):
            block = nat[order[t], order[v]]
            at = (slice(t * WIDTH, (t + 1) * WIDTH), slice(v * WIDTH, (v + 1) * WIDTH))
            high, low = split(block)
            e0_h[at] = high
            e0_l[at] = low
            e0[at] = block
    for m, n in parts:
        block = e0[m, n] if m != n else upper * e0[m, n]
        w_h[m, n] = (-block).astype(BF16)

    def newton(w_h, next_h, fine):
        for m, n in parts:
            depth = first if n == first else slice(0, COLS)
            prod = dot(e0_h[m, depth], w_h[depth, n])
            if fine:
                prod += dot(e0_l[m, depth], w_h[depth, n])
            value = (e0[m, n] + w_h[m, n].astype(F32)) + prod
            b[m, n] = value
            high, low = split(value)
            b_h[m, n] = high
            if fine:
                b_l[m, n] = low
        for m, n in parts:
            depth = first if m == first else slice(0, COLS)
            prod = dot_t(w_h[depth, m], b_h[depth, n])
            if fine:
                prod += dot_t(w_h[depth, m], b_l[depth, n])
            value = b[m, n] + prod
            if m == n:
                value = upper * value + half_eye * w_h[m, n].astype(F32)
            if fine:
                for k in range(2):
                    u_by[(2 if n == second else 0) + k, m] = value[:, k * WIDTH:(k + 1) * WIDTH]
                res[...] += jnp.sum((value * value).reshape(side // 8, 8, side), axis=0)
            else:
                u[m, n] = value
                u_h[m, n] = value.astype(BF16)
        if fine:
            return
        next_h[second, first] = jnp.zeros((side, side), BF16)
        for m, n in parts:
            depth = slice(m.start, n.stop)
            value = (w_h[m, n].astype(F32) - u[m, n]) - dot(w_h[m, depth], u_h[depth, n])
            high = value.astype(BF16)
            next_h[m, n] = high
            for k in range(2):
                w_by[(2 if n == second else 0) + k, m] = high[:, k * WIDTH:(k + 1) * WIDTH]

    res[...] = jnp.zeros_like(res)
    for k in range(2):
        u_by[k, second] = jnp.zeros((side, WIDTH), F32)
        w_by[k, second] = jnp.zeros((side, WIDTH), BF16)
    newton(w_h, w2_h, False)
    newton(w2_h, None, True)
    small[0, 0] = jnp.where(jnp.sum(res[...]) < TOLERANCE, 1, 0).astype(jnp.int32)

    rank = jnp.int32(0)
    for t in range(1, GROUPS):
        rank += jnp.where(order[t] == g, t, 0)
    rank = lax.min(rank, GROUPS - 1)
    step = u_by[rank]
    inverse = (w_by[rank].astype(F32) - step) - dot(w2_h[...], step.astype(BF16))
    for t in range(GROUPS):
        inv[t] = inverse[t * WIDTH:(t + 1) * WIDTH]
    for a in range(GROUPS):
        rows_a = slice(a * WIDTH, (a + 1) * WIDTH)
        same = jnp.where(g == a, 1.0, 0.0).astype(F32)
        high, low = split(down[a] * (inv[ranks[a]] + same * eye))
        x_hl[rows_a, :WIDTH] = high
        x_hl[rows_a, WIDTH:] = low

    for k in range(ROW_BLOCKS // 2):
        rows_k = slice(k * 2 * BLOCK, (k + 1) * 2 * BLOCK)
        high = jnp.concatenate([vhl[h, rows_k, :WIDTH] for h in range(GROUPS)], axis=1)
        low = jnp.concatenate([vhl[h, rows_k, WIDTH:] for h in range(GROUPS)], axis=1)
        q = dot(jnp.concatenate([high, low], axis=0), x_hl[...])
        out[rows_k, :] = quarters(q, 2 * BLOCK, WIDTH)

    arrived(halo_s, win.at[0])
    to_near.wait_send()
    arrived(v_s, vall.at[:3])
    own_core.wait_send()
    late_core.wait_send()
    arrived(p2_s, s1.at[pl.ds(0, TILES - 1)])

    @pl.when(y == 1)
    def _():
        arrived(p2_s, s1.at[pl.ds(0, 1)])

    @pl.when(y != 1)
    def _():
        arrived(p4_s, r2.at[pl.ds(0, PLANE - 1)])

    arrived(p5_s, gb.at[:3, 0, pl.ds(0, TILES - TILES_G)])
    arrived(p6_s, gb.at[:, 0, pl.ds(0, TILES - TILES_G)])


def fast(start, cov_blocks, col_index, order):
    dma = pltpu.SemaphoreType.DMA
    square = (COLS, COLS)
    hbm = pl.BlockSpec(memory_space=pl.ANY)
    smem = pl.BlockSpec(memory_space=pltpu.SMEM)
    return pl.pallas_call(
        kernel,
        out_shape=(
            pltpu.VMEM((ROWS, WIDTH), F32),
            pltpu.SMEM((1, 1), jnp.int32),
        ),
        in_specs=[hbm, hbm, hbm, hbm],
        out_specs=(pl.BlockSpec(memory_space=pltpu.VMEM), smem),
        scratch_shapes=[
            pltpu.SMEM((ROW_BLOCKS, SLOTS), jnp.int32),
            pltpu.SMEM((GROUPS,), jnp.int32),
            pltpu.VMEM((3, ROWS, WIDTH), F32),
            pltpu.VMEM((3 * ROW_BLOCKS, BLOCK, 2 * WIDTH), BF16),
            pltpu.VMEM((ROW_BLOCKS, SLOTS, BLOCK, BLOCK), F32),
            pltpu.VMEM((ROW_BLOCKS, 2 * BLOCK, SLOTS * BLOCK), BF16),
            pltpu.VMEM((GROUPS, ROWS, WIDTH), F32),
            pltpu.VMEM((GROUPS, ROWS, 2 * WIDTH), BF16),
            pltpu.VMEM((4 * WIDTH, 2 * WIDTH), F32),
            pltpu.VMEM((2 * WIDTH, 2 * WIDTH), F32),
            pltpu.VMEM((CORES, TILES, 8, WIDTH), F32),
            pltpu.VMEM((TILES, 8, WIDTH), F32),
            pltpu.VMEM((TILES, 8, WIDTH), F32),
            pltpu.VMEM((PLANE, 8, WIDTH), F32),
            pltpu.VMEM((PLANE, 8, WIDTH), F32),
            pltpu.VMEM((GROUPS, CORES, TILES, 8, WIDTH), F32),
            pltpu.VMEM((GROUPS, GROUPS, WIDTH, WIDTH), F32),
            pltpu.VMEM(square, F32),
            pltpu.VMEM(square, F32),
            pltpu.VMEM(square, F32),
            pltpu.VMEM(square, BF16),
            pltpu.VMEM(square, BF16),
            pltpu.VMEM(square, BF16),
            pltpu.VMEM(square, BF16),
            pltpu.VMEM(square, BF16),
            pltpu.VMEM(square, BF16),
            pltpu.VMEM(square, BF16),
            pltpu.VMEM((GROUPS, COLS, WIDTH), BF16),
            pltpu.VMEM((GROUPS, COLS, WIDTH), F32),
            pltpu.VMEM((GROUPS, WIDTH, WIDTH), F32),
            pltpu.VMEM((COLS, 2 * WIDTH), BF16),
            pltpu.VMEM((8, COLS // 2), F32),
            pltpu.SemaphoreType.REGULAR((6,)),
            dma((2,)),
            dma, dma,
            dma, dma((ROW_BLOCKS,)), dma, dma,
            dma, dma((ROW_BLOCKS,)), dma((ROW_BLOCKS,)), dma((4,)),
            dma((2,)), dma((2,)),
            dma, dma, dma,
            dma, dma((KINDS,)),
            dma, dma((GROUPS, KINDS)),
            dma, dma,
        ],
        compiler_params=pltpu.CompilerParams(
            collective_id=0, has_side_effects=True, vmem_limit_bytes=56 * 1024 * 1024
        ),
    )(start, cov_blocks, col_index, order)


def body(start, cov_blocks, col_index, order):
    result, small = fast(start, cov_blocks, col_index, order)
    return lax.cond(
        small[0, 0] == 1,
        lambda: result,
        lambda: careful(start, cov_blocks, col_index, order),
    )


def solution(mesh):
    placed = (P("pts", "cols"), P("pts", None, None, None), P("pts", None), P())
    return jax.shard_map(
        body, mesh=mesh, in_specs=placed, out_specs=P("pts", "cols"), check_vma=False
    )
```

```python
import jax
import jax.numpy as jnp
from jax import lax
from jax.experimental import pallas as pl
from jax.experimental.pallas import tpu as pltpu
from jax.sharding import PartitionSpec as P

MESH = pl.DeviceIdType.MESH
F32 = jnp.float32
BF16 = jnp.bfloat16
GROUPS = 4
WIDTH = 128
BLOCK = 128
ROW_BLOCKS = 8
SLOTS = 8
NBLK = 512
YS, ZS, CORES = 4, 8, 2
COLS = GROUPS * WIDTH
ROWS = ROW_BLOCKS * BLOCK
HALF = ROW_BLOCKS // 2
PLANE = YS * ZS
TILES_G = WIDTH // CORES // 8
KINDS = 4
TILES = KINDS * TILES_G
NEAR_LAST = (4, 3, 5, 2, 6, 1, 7, 0)
TOLERANCE = 4e-4


def total(value, axis):
    distance = 1
    while distance < lax.axis_size(axis):
        pairs = [(i, i ^ distance) for i in range(lax.axis_size(axis))]
        value = value + lax.ppermute(value, axis, pairs)
        distance *= 2
    return value


def broadcast(value, axis, source):
    kept = jnp.where(lax.axis_index(axis) == source, value, 0).astype(value.dtype)
    return total(kept, axis)


def with_halo(cells, axis, width):
    count = lax.axis_size(axis)
    head = lax.slice_in_dim(cells, 0, width, axis=0)
    tail = lax.slice_in_dim(cells, cells.shape[0] - width, cells.shape[0], axis=0)
    return jnp.concatenate(
        [
            lax.ppermute(tail, axis, [(i, (i + 1) % count) for i in range(count)]),
            cells,
            lax.ppermute(head, axis, [((i + 1) % count, i) for i in range(count)]),
        ],
        axis=0,
    )


def inner(left, right):
    return lax.dot_general(
        left,
        right,
        (((0,), (0,)), ((), ())),
        precision=lax.Precision.HIGHEST,
        preferred_element_type=F32,
    )


def careful(start, cov_blocks, col_index, order):
    rows, group_size = start.shape
    blocks_dev = cov_blocks.shape[0]
    block = cov_blocks.shape[2]
    total_blocks = blocks_dev * lax.axis_size("pts")
    groups = lax.axis_size("cols")
    mine = lax.axis_index("cols")
    positions = jnp.arange(groups, dtype=jnp.int32)
    rank = jnp.sum(jnp.where(order == mine, positions, 0))
    first_block = lax.axis_index("pts") * blocks_dev - blocks_dev
    relative = jnp.mod(col_index - first_block, total_blocks)
    tiles = with_halo(start, "pts", rows).reshape(3 * blocks_dev, block, group_size)[relative]
    local = jnp.einsum(
        "rsab,rsbk->rak", cov_blocks, tiles, precision=lax.Precision.HIGHEST
    ).reshape(rows, group_size)

    def step(t, local):
        owner = order[t]
        gram = total(inner(local, local), "pts")
        lower = jnp.linalg.cholesky(gram)
        candidate = lax.linalg.triangular_solve(
            lower, local, left_side=False, lower=True, transpose_a=True
        )
        ortho = broadcast(candidate, "cols", owner)
        coef = total(inner(ortho, local), "pts")
        updated = local - jnp.dot(
            ortho, coef, precision=lax.Precision.HIGHEST, preferred_element_type=F32
        )
        return jnp.where(rank > t, updated, jnp.where(mine == owner, ortho, local))

    return lax.fori_loop(0, groups, step, local)


def split(x):
    high = x.astype(BF16)
    return high, (x - high.astype(F32)).astype(BF16)


def quarters(q, m, n):
    return (q[:m, :n] + q[m:, n:]) + (q[:m, n:] + q[m:, :n])


def dot(a, b):
    return jnp.dot(a, b, preferred_element_type=F32)


def dot_t(a, b):
    return lax.dot_general(a, b, (((0,), (0,)), ((), ())), preferred_element_type=F32)


def kernel(
    start, cov, col_in, order_in, out, small,
    col_index, order,
    win, win_hl, covv, cov_hl, vall, vhl, acc, acc2, tb, r1, s1, r2, r3, gb,
    nat, e0, b, u, e0_h, e0_l, w_h, w2_h, b_h, b_l, u_h, w_by, u_by, inv, x_hl, res,
    word, i_sem, c_sem, l_sem,
    halo_s, halo_r, n_s, n_r, v_s, next_r, prev_r, rest_r,
    p1_s, p1_r, p2_s, p2_r, p3_r, p4_s, p4_r, p5_s, p5_r, p6_s, p6_r,
):
    p = lax.axis_index("pts")
    g = lax.axis_index("cols")
    npts = YS * ZS * CORES
    c = lax.rem(p, CORES)
    z = lax.rem(lax.div(p, CORES), ZS)
    y = lax.div(p, CORES * ZS)
    before, after = lax.rem(p + npts - 1, npts), lax.rem(p + 1, npts)
    sibling = p + 1 - 2 * c
    g_next, g_prev, g_opp = (lax.rem(g + k, GROUPS) for k in (1, 3, 2))

    here = y * ZS + z

    def peer(k):
        y_to, z_to = lax.rem(y + lax.div(k, ZS), YS), lax.rem(z + lax.rem(k, ZS), ZS)
        return y_to * ZS + z_to

    def device(chip):
        return chip * CORES + c

    def remote(src, dst, send, recv, **where):
        return pltpu.make_async_remote_copy(
            src_ref=src, dst_ref=dst, send_sem=send, recv_sem=recv,
            device_id=where, device_id_type=MESH,
        )

    barrier = pltpu.get_barrier_semaphore()
    near_x = [dict(cols=h) for h in (g_next, g_prev)]
    near_z = [dict(pts=device(peer(k))) for k in (1, ZS - 1)]
    near_y = [dict(pts=device(peer(k))) for k in (ZS, (YS - 1) * ZS)]
    next_z = [dict(pts=device(peer(k))) for k in (2, ZS - 2)]
    neighbours = [dict(pts=before), dict(pts=after)] + near_x + near_z + near_y

    def tell(sem, devices):
        for one in devices:
            pl.semaphore_signal(sem, inc=1, device_id=one, device_id_type=MESH)

    tell(barrier, neighbours)

    cov_copy = pltpu.make_async_copy(cov, covv, c_sem)
    own_copy = pltpu.make_async_copy(start, win.at[1], l_sem)
    own_copy.start()
    col_copy = pltpu.make_async_copy(col_in, col_index, i_sem.at[0])
    col_copy.start()
    order_copy = pltpu.make_async_copy(order_in, order, i_sem.at[1])
    order_copy.start()

    cov_copy.start()

    pl.semaphore_wait(barrier, len(neighbours))
    tell(word.at[0], near_z)
    tell(word.at[1], near_x)

    def turn_row(j):
        return ROW_BLOCKS - 1 - j + c * (2 * j - ROW_BLOCKS + 1)

    def rows(r):
        return pl.ds(pl.multiple_of(r * BLOCK, BLOCK), BLOCK)

    far_side, near_side = 2 * c, 2 - 2 * c
    far_device = before + c * (after - before)

    def to_far(j):
        block = rows(ROW_BLOCKS - 1 - turn_row(j))
        return remote(start.at[block, :], win.at[near_side, block, :], halo_s, halo_r.at[j], pts=far_device)

    to_near = remote(start, win.at[far_side], n_s, n_r, pts=sibling)
    to_far(0).start()
    to_near.start()
    for j in range(1, ROW_BLOCKS):
        to_far(j).start()

    col_copy.wait()
    order_copy.wait()
    ranks = []
    for a in range(GROUPS):
        rank = jnp.int32(0)
        for t in range(1, GROUPS):
            rank += jnp.where(order[t] == a, t, 0)
        ranks.append(lax.min(rank, GROUPS - 1))
    row_id = lax.broadcasted_iota(jnp.int32, (WIDTH, WIDTH), 0)
    col_id = lax.broadcasted_iota(jnp.int32, (WIDTH, WIDTH), 1)
    eye = (row_id == col_id).astype(F32)

    cov_copy.wait()

    def split_cov(r, carry):
        for s in range(SLOTS):
            high, low = split(covv[r, s])
            cov_hl[r, :BLOCK, s * BLOCK:(s + 1) * BLOCK] = high
            cov_hl[r, BLOCK:, s * BLOCK:(s + 1) * BLOCK] = low
        return carry

    lax.fori_loop(0, ROW_BLOCKS, split_cov, 0)

    def split_window(side, k):
        high, low = split(win[side, rows(k), :])
        win_hl[side * ROW_BLOCKS + k, :, :WIDTH] = high
        win_hl[side * ROW_BLOCKS + k, :, WIDTH:] = low

    def split_own(k, carry):
        split_window(1, k)
        return carry

    def split_near(k, carry):
        split_window(near_side, k)
        return carry

    own_copy.wait()
    lax.fori_loop(0, ROW_BLOCKS, split_own, 0)
    to_near.wait_recv()
    lax.fori_loop(0, ROW_BLOCKS, split_near, 0)

    base = p * ROW_BLOCKS - ROW_BLOCKS - NBLK

    def turn(r):
        return lax.rem(g + GROUPS - lax.rem(r, GROUPS), GROUPS)

    def goes_left(r):
        t = turn(r)
        return (t >= 2) | ((t == 0) & (r < HALF))

    def goes_right(r):
        t = turn(r)
        return (t <= 1) | ((t == 3) & (r >= HALF))

    def between(r):
        t = turn(r)
        return (t == 1) | (t == 2)

    def has_next(r):
        t = turn(r)
        return (t == 1) | (t == 2) | ((t == 3) & (r < HALF))

    def has_prev(r):
        t = turn(r)
        return (t == 1) | (t == 2) | ((t == 0) & (r >= HALF))

    def prev_pair(r):
        t = turn(r)
        return (t == 1) | ((t == 0) & (r >= HALF))

    def xcopy(src, r, recv, to):
        ref = vall.at[src, rows(r), :]
        return remote(ref, ref, v_s, recv, cols=to)

    def arrived(sem, ref):
        pltpu.make_async_copy(ref, ref, sem).wait()

    def several(count):
        return vall.at[0, :count * BLOCK, :]

    def keep_split(src, r):
        high, low = split(vall[src, rows(r), :])
        vhl[src, rows(r), :WIDTH] = high
        vhl[src, rows(r), WIDTH:] = low

    def image(r):
        tiles = []
        for s in range(SLOTS):
            rel = lax.rem(col_index[r, s] - base, NBLK)
            tiles.append(win_hl[lax.min(rel, 3 * ROW_BLOCKS - 1)])
        quad = dot(cov_hl[r], jnp.concatenate(tiles, axis=0))
        vall[g, rows(r), :] = quarters(quad, BLOCK, WIDTH)

        @pl.when(goes_left(r))
        def _():
            xcopy(g, r, next_r.at[r], g_prev).start()

        @pl.when(goes_right(r))
        def _():
            xcopy(g, r, prev_r.at[r], g_next).start()

    for j in range(ROW_BLOCKS):
        r = turn_row(j)
        arrived(halo_r.at[j], win.at[0, pl.ds(0, BLOCK), :])
        split_window(far_side, r)
        image(r)
        keep_split(g, r)
        if j == 0:
            pl.semaphore_wait(word.at[0], 2)
            tell(word.at[2], next_z)
        if j == 3:
            pl.semaphore_wait(word.at[2], 2)
            tell(word.at[3], near_y)

    pl.semaphore_wait(word.at[3], 2)
    tell(word.at[4], near_y)

    def place(kind, block):
        for core in range(CORES):
            part = block[core * WIDTH // CORES:(core + 1) * WIDTH // CORES]
            tb[core, kind * TILES_G:(kind + 1) * TILES_G] = part.reshape(TILES_G, 8, WIDTH)

    def core_sum(kind):
        part = pl.ds(kind * TILES_G, TILES_G)
        send, recv = p1_s.at[kind], p1_r.at[kind]
        copy = remote(tb.at[1 - c, part], r1.at[part], send, recv, pts=sibling)
        return copy, part

    def scatter(y_to, far):
        to = y_to * ZS + lax.rem(z + far, ZS)
        return remote(s1.at[to], r2.at[here], p2_s, p2_r, pts=device(to))

    def scatter_rows(y_to):
        for far in NEAR_LAST[:-1]:
            scatter(y_to, far).start()

        @pl.when(y != y_to)
        def _():
            scatter(y_to, 0).start()

    def scatter_prev(z_to):
        return remote(s1.at[TILES_G + z_to], r3.at[here], p2_s, p3_r, cols=g_prev, pts=device(z_to))

    def sum_tile():
        arrived(p2_r, r2.at[pl.ds(1, PLANE - 1)])
        r2[here] = s1[here]
        gb[g, c, here] = jnp.sum(r2[...], axis=0)

        @pl.when(y == 0)
        def _():
            arrived(p3_r, r3)
            gb[g, c, here] += jnp.sum(r3[...], axis=0)

        ref = gb.at[g, c, here]
        for over in (2, 1, 3, 0):
            for far in NEAR_LAST:
                if over or far:
                    to = lax.rem(y + over, YS) * ZS + lax.rem(z + far, ZS)
                    remote(ref, ref, p4_s, p4_r.at[y], pts=device(to)).start()

    acc[...] = jnp.zeros_like(acc)
    acc2[...] = jnp.zeros_like(acc2)
    place(3, quarters(dot_t(vhl[g], vhl[g]), WIDTH, WIDTH))
    own_core, own_part = core_sum(3)
    own_core.start()

    for j in range(ROW_BLOCKS):
        r = turn_row(j)

        @pl.when(has_next(r))
        def _():
            arrived(next_r.at[r], several(1))
            keep_split(g_next, r)

        @pl.when(has_prev(r))
        def _():
            arrived(prev_r.at[r], several(1))
            keep_split(g_prev, r)

        @pl.when(between(r))
        def _():
            left = jnp.concatenate([vhl[g, rows(r), :], vhl[g_prev, rows(r), :]], axis=1)
            acc[...] += dot_t(left, vhl[g_next, rows(r), :])

        @pl.when((turn(r) == 3) & (r < HALF))
        def _():
            acc[:2 * WIDTH] += dot_t(vhl[g, rows(r), :], vhl[g_next, rows(r), :])

        @pl.when(prev_pair(r))
        def _():
            acc2[...] += dot_t(vhl[g_prev, rows(r), :], vhl[g, rows(r), :])

        if j == 2:
            own_core.wait_recv()
            s1[own_part] = tb[c, own_part] + r1[own_part]
            pl.semaphore_wait(word.at[4], 2)
            tell(word.at[5], near_x)
            scatter_rows(YS - 1)

    place(0, quarters(acc[:2 * WIDTH], WIDTH, WIDTH))
    place(1, quarters(acc2[...], WIDTH, WIDTH))
    place(2, quarters(acc[2 * WIDTH:], WIDTH, WIDTH))

    late = [core_sum(kind) for kind in (1, 0, 2)]
    for copy, _ in late:
        copy.start()
    pl.semaphore_wait(word.at[5], 2)
    for (copy, tiles_of), y_to in zip(late, (None, 0, 2)):
        copy.wait_recv()
        s1[tiles_of] = tb[c, tiles_of] + r1[tiles_of]
        if y_to is None:
            for far in NEAR_LAST:
                scatter_prev(lax.rem(z + far, ZS)).start()
        else:
            scatter_rows(y_to)

    for r in range(ROW_BLOCKS):
        @pl.when(jnp.logical_not(goes_left(r)))
        def _():
            xcopy(g, r, rest_r.at[0], g_prev).start()

        @pl.when(jnp.logical_not(goes_right(r)))
        def _():
            xcopy(g, r, rest_r.at[1], g_next).start()

        @pl.when(between(r))
        def _():
            xcopy(g_prev, r, rest_r.at[2], g_next).start()
            xcopy(g_next, r, rest_r.at[3], g_prev).start()

    @pl.when(y != 1)
    def _():
        sum_tile()

    pl.semaphore_wait(word.at[1], 2)

    def of_set(n):
        return pl.ds(n * TILES_G, TILES_G)

    def x_share(k, n):
        ref = gb.at[g, c, of_set(n)]
        return remote(ref, ref, p5_s, p5_r.at[GROUPS - k, n], cols=lax.rem(g + k, GROUPS))

    def core_share(k, n):
        ref = gb.at[lax.rem(g + k, GROUPS), c, of_set(n)]
        return remote(ref, ref, p6_s, p6_r.at[n], pts=sibling)

    for n in (3, 0, 2):
        @pl.when(y == n)
        def _():
            arrived(p4_r.at[n], gb.at[g, c, pl.ds(0, TILES_G - 1)])

        @pl.when(y != n)
        def _():
            arrived(p4_r.at[n], gb.at[g, c, pl.ds(0, TILES_G)])

        for k in (2, 1, 3):
            x_share(k, n).start()
        core_share(0, n).start()

    def pass_to_core(n):
        for k in (1, 3, 2):
            arrived(p5_r.at[k, n], gb.at[g, c, of_set(n)])
            core_share(k, n).start()

    def whole(n):
        arrived(p6_r.at[n], gb.at[:, 1 - c, of_set(n)])

    def part(a, kind):
        return jnp.concatenate(
            [gb[a, core, kind * TILES_G:(kind + 1) * TILES_G].reshape(WIDTH // CORES, WIDTH) for core in range(CORES)], axis=0
        )

    pass_to_core(3)
    pass_to_core(0)
    arrived(rest_r.at[0], several(3))
    arrived(rest_r.at[1], several(3))
    arrived(rest_r.at[2], several(4))
    arrived(rest_r.at[3], several(4))
    for r in range(ROW_BLOCKS):
        keep_split(g_opp, r)

        @pl.when(jnp.logical_not(has_next(r)))
        def _():
            keep_split(g_next, r)

        @pl.when(jnp.logical_not(has_prev(r)))
        def _():
            keep_split(g_prev, r)

    whole(3)
    diag = [part(a, 3) for a in range(GROUPS)]
    down = [lax.rsqrt(jnp.sum(d * eye, axis=1, keepdims=True)) for d in diag]
    across = [lax.rsqrt(jnp.sum(d * eye, axis=0, keepdims=True)) for d in diag]

    def put(a, h, block):
        block = block * down[a] * across[h]
        nat[a, h] = block - eye if a == h else block

    for a in range(GROUPS):
        put(a, a, diag[a])
    pass_to_core(2)
    whole(0)
    for a in range(GROUPS):
        h = (a + 1) % GROUPS
        block = part(a, 0)
        put(a, h, block)
        put(h, a, block.T)
    whole(2)
    for a in range(GROUPS // 2):
        h = a + GROUPS // 2
        block = part((a + 1) % GROUPS, 2) + part((a + 3) % GROUPS, 2).T
        put(a, h, block)
        put(h, a, block.T)

    side = COLS // 2
    first, second = slice(0, side), slice(side, COLS)
    parts = ((first, first), (first, second), (second, second))
    down_id = lax.broadcasted_iota(jnp.int32, (side, side), 0)
    across_id = lax.broadcasted_iota(jnp.int32, (side, side), 1)
    half_eye = jnp.where(down_id == across_id, 0.5, 0.0).astype(F32)
    upper = jnp.where(down_id < across_id, 1.0, 0.0).astype(F32) + half_eye
    w_h[second, first] = jnp.zeros((side, side), BF16)
    for t in range(GROUPS):
        for v in range(GROUPS):
            block = nat[order[t], order[v]]
            at = (slice(t * WIDTH, (t + 1) * WIDTH), slice(v * WIDTH, (v + 1) * WIDTH))
            high, low = split(block)
            e0_h[at] = high
            e0_l[at] = low
            e0[at] = block
    for m, n in parts:
        block = e0[m, n] if m != n else upper * e0[m, n]
        w_h[m, n] = (-block).astype(BF16)

    def newton(w_h, next_h, fine):
        for m, n in parts:
            depth = first if n == first else slice(0, COLS)
            prod = dot(e0_h[m, depth], w_h[depth, n])
            if fine:
                prod += dot(e0_l[m, depth], w_h[depth, n])
            value = (e0[m, n] + w_h[m, n].astype(F32)) + prod
            b[m, n] = value
            high, low = split(value)
            b_h[m, n] = high
            if fine:
                b_l[m, n] = low
        for m, n in parts:
            depth = first if m == first else slice(0, COLS)
            prod = dot_t(w_h[depth, m], b_h[depth, n])
            if fine:
                prod += dot_t(w_h[depth, m], b_l[depth, n])
            value = b[m, n] + prod
            if m == n:
                value = upper * value + half_eye * w_h[m, n].astype(F32)
            if fine:
                for k in range(2):
                    u_by[(2 if n == second else 0) + k, m] = value[:, k * WIDTH:(k + 1) * WIDTH]
                res[...] += jnp.sum((value * value).reshape(side // 8, 8, side), axis=0)
            else:
                u[m, n] = value
                u_h[m, n] = value.astype(BF16)
        if fine:
            return
        next_h[second, first] = jnp.zeros((side, side), BF16)
        for m, n in parts:
            depth = slice(m.start, n.stop)
            value = (w_h[m, n].astype(F32) - u[m, n]) - dot(w_h[m, depth], u_h[depth, n])
            high = value.astype(BF16)
            next_h[m, n] = high
            for k in range(2):
                w_by[(2 if n == second else 0) + k, m] = high[:, k * WIDTH:(k + 1) * WIDTH]

    res[...] = jnp.zeros_like(res)
    for k in range(2):
        u_by[k, second] = jnp.zeros((side, WIDTH), F32)
        w_by[k, second] = jnp.zeros((side, WIDTH), BF16)
    newton(w_h, w2_h, False)
    newton(w2_h, None, True)
    small[0, 0] = jnp.where(jnp.sum(res[...]) < TOLERANCE, 1, 0).astype(jnp.int32)

    rank = jnp.int32(0)
    for t in range(1, GROUPS):
        rank += jnp.where(order[t] == g, t, 0)
    rank = lax.min(rank, GROUPS - 1)
    step = u_by[rank]
    inverse = (w_by[rank].astype(F32) - step) - dot(w2_h[...], step.astype(BF16))
    for t in range(GROUPS):
        inv[t] = inverse[t * WIDTH:(t + 1) * WIDTH]
    for a in range(GROUPS):
        rows_a = slice(a * WIDTH, (a + 1) * WIDTH)
        same = jnp.where(g == a, 1.0, 0.0).astype(F32)
        high, low = split(down[a] * (inv[ranks[a]] + same * eye))
        x_hl[rows_a, :WIDTH] = high
        x_hl[rows_a, WIDTH:] = low

    for k in range(ROW_BLOCKS // 2):
        rows_k = slice(k * 2 * BLOCK, (k + 1) * 2 * BLOCK)
        high = jnp.concatenate([vhl[h, rows_k, :WIDTH] for h in range(GROUPS)], axis=1)
        low = jnp.concatenate([vhl[h, rows_k, WIDTH:] for h in range(GROUPS)], axis=1)
        q = dot(jnp.concatenate([high, low], axis=0), x_hl[...])
        out[rows_k, :] = quarters(q, 2 * BLOCK, WIDTH)

    arrived(halo_s, win.at[0])
    to_near.wait_send()
    arrived(v_s, vall.at[:3])
    own_core.wait_send()
    for copy, _ in late:
        copy.wait_send()
    arrived(p2_s, s1.at[pl.ds(0, TILES - 1)])

    @pl.when(y == 1)
    def _():
        arrived(p2_s, s1.at[pl.ds(0, 1)])

    @pl.when(y != 1)
    def _():
        arrived(p4_s, r2.at[pl.ds(0, PLANE - 1)])

    arrived(p5_s, gb.at[:3, 0, pl.ds(0, TILES - TILES_G)])
    arrived(p6_s, gb.at[:, 0, pl.ds(0, TILES - TILES_G)])


def fast(start, cov_blocks, col_index, order):
    dma = pltpu.SemaphoreType.DMA
    square = (COLS, COLS)
    hbm = pl.BlockSpec(memory_space=pl.ANY)
    smem = pl.BlockSpec(memory_space=pltpu.SMEM)
    return pl.pallas_call(
        kernel,
        out_shape=(
            pltpu.VMEM((ROWS, WIDTH), F32),
            pltpu.SMEM((1, 1), jnp.int32),
        ),
        in_specs=[hbm, hbm, hbm, hbm],
        out_specs=(pl.BlockSpec(memory_space=pltpu.VMEM), smem),
        scratch_shapes=[
            pltpu.SMEM((ROW_BLOCKS, SLOTS), jnp.int32),
            pltpu.SMEM((GROUPS,), jnp.int32),
            pltpu.VMEM((3, ROWS, WIDTH), F32),
            pltpu.VMEM((3 * ROW_BLOCKS, BLOCK, 2 * WIDTH), BF16),
            pltpu.VMEM((ROW_BLOCKS, SLOTS, BLOCK, BLOCK), F32),
            pltpu.VMEM((ROW_BLOCKS, 2 * BLOCK, SLOTS * BLOCK), BF16),
            pltpu.VMEM((GROUPS, ROWS, WIDTH), F32),
            pltpu.VMEM((GROUPS, ROWS, 2 * WIDTH), BF16),
            pltpu.VMEM((4 * WIDTH, 2 * WIDTH), F32),
            pltpu.VMEM((2 * WIDTH, 2 * WIDTH), F32),
            pltpu.VMEM((CORES, TILES, 8, WIDTH), F32),
            pltpu.VMEM((TILES, 8, WIDTH), F32),
            pltpu.VMEM((TILES, 8, WIDTH), F32),
            pltpu.VMEM((PLANE, 8, WIDTH), F32),
            pltpu.VMEM((PLANE, 8, WIDTH), F32),
            pltpu.VMEM((GROUPS, CORES, TILES, 8, WIDTH), F32),
            pltpu.VMEM((GROUPS, GROUPS, WIDTH, WIDTH), F32),
            pltpu.VMEM(square, F32),
            pltpu.VMEM(square, F32),
            pltpu.VMEM(square, F32),
            pltpu.VMEM(square, BF16),
            pltpu.VMEM(square, BF16),
            pltpu.VMEM(square, BF16),
            pltpu.VMEM(square, BF16),
            pltpu.VMEM(square, BF16),
            pltpu.VMEM(square, BF16),
            pltpu.VMEM(square, BF16),
            pltpu.VMEM((GROUPS, COLS, WIDTH), BF16),
            pltpu.VMEM((GROUPS, COLS, WIDTH), F32),
            pltpu.VMEM((GROUPS, WIDTH, WIDTH), F32),
            pltpu.VMEM((COLS, 2 * WIDTH), BF16),
            pltpu.VMEM((8, COLS // 2), F32),
            pltpu.SemaphoreType.REGULAR((6,)),
            dma((2,)),
            dma, dma,
            dma, dma((ROW_BLOCKS,)), dma, dma,
            dma, dma((ROW_BLOCKS,)), dma((ROW_BLOCKS,)), dma((4,)),
            dma((KINDS,)), dma((KINDS,)),
            dma, dma, dma,
            dma, dma((KINDS,)),
            dma, dma((GROUPS, KINDS)),
            dma, dma((KINDS,)),
        ],
        compiler_params=pltpu.CompilerParams(
            collective_id=0, has_side_effects=True, vmem_limit_bytes=56 * 1024 * 1024
        ),
    )(start, cov_blocks, col_index, order)


def body(start, cov_blocks, col_index, order):
    result, small = fast(start, cov_blocks, col_index, order)
    return lax.cond(
        small[0, 0] == 1,
        lambda: result,
        lambda: careful(start, cov_blocks, col_index, order),
    )


def solution(mesh):
    placed = (P("pts", "cols"), P("pts", None, None, None), P("pts", None), P())
    return jax.shard_map(
        body, mesh=mesh, in_specs=placed, out_specs=P("pts", "cols"), check_vma=False
    )
```

```python
import jax
import jax.numpy as jnp
from jax import lax
from jax.experimental import pallas as pl
from jax.experimental.pallas import tpu as pltpu
from jax.sharding import PartitionSpec as P

MESH = pl.DeviceIdType.MESH
F32 = jnp.float32
BF16 = jnp.bfloat16
GROUPS = 4
WIDTH = 128
BLOCK = 128
ROW_BLOCKS = 8
SLOTS = 8
NBLK = 512
YS, ZS, CORES = 4, 8, 2
COLS = GROUPS * WIDTH
ROWS = ROW_BLOCKS * BLOCK
HALF = ROW_BLOCKS // 2
PLANE = YS * ZS
TILES_G = WIDTH // CORES // 8
KINDS = 4
TILES = KINDS * TILES_G
NEAR_LAST = (4, 3, 5, 2, 6, 1, 7, 0)
TOLERANCE = 4e-4


def total(value, axis):
    distance = 1
    while distance < lax.axis_size(axis):
        pairs = [(i, i ^ distance) for i in range(lax.axis_size(axis))]
        value = value + lax.ppermute(value, axis, pairs)
        distance *= 2
    return value


def broadcast(value, axis, source):
    kept = jnp.where(lax.axis_index(axis) == source, value, 0).astype(value.dtype)
    return total(kept, axis)


def with_halo(cells, axis, width):
    count = lax.axis_size(axis)
    head = lax.slice_in_dim(cells, 0, width, axis=0)
    tail = lax.slice_in_dim(cells, cells.shape[0] - width, cells.shape[0], axis=0)
    return jnp.concatenate(
        [
            lax.ppermute(tail, axis, [(i, (i + 1) % count) for i in range(count)]),
            cells,
            lax.ppermute(head, axis, [((i + 1) % count, i) for i in range(count)]),
        ],
        axis=0,
    )


def inner(left, right):
    return lax.dot_general(
        left,
        right,
        (((0,), (0,)), ((), ())),
        precision=lax.Precision.HIGHEST,
        preferred_element_type=F32,
    )


def careful(start, cov_blocks, col_index, order):
    rows, group_size = start.shape
    blocks_dev = cov_blocks.shape[0]
    block = cov_blocks.shape[2]
    total_blocks = blocks_dev * lax.axis_size("pts")
    groups = lax.axis_size("cols")
    mine = lax.axis_index("cols")
    positions = jnp.arange(groups, dtype=jnp.int32)
    rank = jnp.sum(jnp.where(order == mine, positions, 0))
    first_block = lax.axis_index("pts") * blocks_dev - blocks_dev
    relative = jnp.mod(col_index - first_block, total_blocks)
    tiles = with_halo(start, "pts", rows).reshape(3 * blocks_dev, block, group_size)[relative]
    local = jnp.einsum(
        "rsab,rsbk->rak", cov_blocks, tiles, precision=lax.Precision.HIGHEST
    ).reshape(rows, group_size)

    def step(t, local):
        owner = order[t]
        gram = total(inner(local, local), "pts")
        lower = jnp.linalg.cholesky(gram)
        candidate = lax.linalg.triangular_solve(
            lower, local, left_side=False, lower=True, transpose_a=True
        )
        ortho = broadcast(candidate, "cols", owner)
        coef = total(inner(ortho, local), "pts")
        updated = local - jnp.dot(
            ortho, coef, precision=lax.Precision.HIGHEST, preferred_element_type=F32
        )
        return jnp.where(rank > t, updated, jnp.where(mine == owner, ortho, local))

    return lax.fori_loop(0, groups, step, local)


def split(x):
    high = x.astype(BF16)
    return high, (x - high.astype(F32)).astype(BF16)


def quarters(q, m, n):
    return (q[:m, :n] + q[m:, n:]) + (q[:m, n:] + q[m:, :n])


def dot(a, b):
    return jnp.dot(a, b, preferred_element_type=F32)


def dot_t(a, b):
    return lax.dot_general(a, b, (((0,), (0,)), ((), ())), preferred_element_type=F32)


def kernel(
    start, cov, col_in, order_in, out, small,
    col_index, order,
    win, win_hl, covv, cov_hl, vall, vhl, acc, acc2, tb, r1, s1, r2, r3, gb,
    nat, e0, b, u, e0_h, e0_l, w_h, w2_h, b_h, b_l, u_h, w_by, u_by, inv, x_hl, res,
    word, i_sem, c_sem, l_sem,
    halo_s, halo_r, n_s, n_r, v_s, next_r, prev_r, rest_r,
    p1_s, p1_r, p2_s, p2_r, p3_r, p4_s, p4_r, p5_s, p5_r, p6_s, p6_r,
):
    p = lax.axis_index("pts")
    g = lax.axis_index("cols")
    npts = YS * ZS * CORES
    c = lax.rem(p, CORES)
    z = lax.rem(lax.div(p, CORES), ZS)
    y = lax.div(p, CORES * ZS)
    before, after = lax.rem(p + npts - 1, npts), lax.rem(p + 1, npts)
    sibling = p + 1 - 2 * c
    g_next, g_prev, g_opp = (lax.rem(g + k, GROUPS) for k in (1, 3, 2))

    here = y * ZS + z

    def peer(k):
        y_to, z_to = lax.rem(y + lax.div(k, ZS), YS), lax.rem(z + lax.rem(k, ZS), ZS)
        return y_to * ZS + z_to

    def device(chip):
        return chip * CORES + c

    def remote(src, dst, send, recv, **where):
        return pltpu.make_async_remote_copy(
            src_ref=src, dst_ref=dst, send_sem=send, recv_sem=recv,
            device_id=where, device_id_type=MESH,
        )

    barrier = pltpu.get_barrier_semaphore()
    near_x = [dict(cols=h) for h in (g_next, g_prev)]
    near_z = [dict(pts=device(peer(k))) for k in (1, ZS - 1)]
    near_y = [dict(pts=device(peer(k))) for k in (ZS, (YS - 1) * ZS)]
    next_z = [dict(pts=device(peer(k))) for k in (2, ZS - 2)]
    neighbours = [dict(pts=before), dict(pts=after)] + near_x + near_z + near_y

    def tell(sem, devices):
        for one in devices:
            pl.semaphore_signal(sem, inc=1, device_id=one, device_id_type=MESH)

    tell(barrier, neighbours)

    cov_copy = pltpu.make_async_copy(cov, covv, c_sem)
    own_copy = pltpu.make_async_copy(start, win.at[1], l_sem)
    own_copy.start()
    col_copy = pltpu.make_async_copy(col_in, col_index, i_sem.at[0])
    col_copy.start()
    order_copy = pltpu.make_async_copy(order_in, order, i_sem.at[1])
    order_copy.start()

    cov_copy.start()

    pl.semaphore_wait(barrier, len(neighbours))
    tell(word.at[0], near_z)
    tell(word.at[1], near_x)

    def turn_row(j):
        return ROW_BLOCKS - 1 - j + c * (2 * j - ROW_BLOCKS + 1)

    def rows(r):
        return pl.ds(pl.multiple_of(r * BLOCK, BLOCK), BLOCK)

    far_side, near_side = 2 * c, 2 - 2 * c
    far_device = before + c * (after - before)

    def to_far(j):
        block = rows(ROW_BLOCKS - 1 - turn_row(j))
        return remote(start.at[block, :], win.at[near_side, block, :], halo_s, halo_r.at[j], pts=far_device)

    to_near = remote(start, win.at[far_side], n_s, n_r, pts=sibling)
    to_far(0).start()
    to_near.start()
    for j in range(1, ROW_BLOCKS):
        to_far(j).start()

    col_copy.wait()
    order_copy.wait()
    ranks = []
    for a in range(GROUPS):
        rank = jnp.int32(0)
        for t in range(1, GROUPS):
            rank += jnp.where(order[t] == a, t, 0)
        ranks.append(lax.min(rank, GROUPS - 1))
    row_id = lax.broadcasted_iota(jnp.int32, (WIDTH, WIDTH), 0)
    col_id = lax.broadcasted_iota(jnp.int32, (WIDTH, WIDTH), 1)
    eye = (row_id == col_id).astype(F32)

    cov_copy.wait()

    def split_cov(r, carry):
        for s in range(SLOTS):
            high, low = split(covv[r, s])
            cov_hl[r, :BLOCK, s * BLOCK:(s + 1) * BLOCK] = high
            cov_hl[r, BLOCK:, s * BLOCK:(s + 1) * BLOCK] = low
        return carry

    lax.fori_loop(0, ROW_BLOCKS, split_cov, 0)

    def split_window(side, k):
        high, low = split(win[side, rows(k), :])
        win_hl[side * ROW_BLOCKS + k, :, :WIDTH] = high
        win_hl[side * ROW_BLOCKS + k, :, WIDTH:] = low

    def split_own(k, carry):
        split_window(1, k)
        return carry

    def split_near(k, carry):
        split_window(near_side, k)
        return carry

    own_copy.wait()
    lax.fori_loop(0, ROW_BLOCKS, split_own, 0)
    to_near.wait_recv()
    lax.fori_loop(0, ROW_BLOCKS, split_near, 0)

    base = p * ROW_BLOCKS - ROW_BLOCKS - NBLK

    def turn(r):
        return lax.rem(g + GROUPS - lax.rem(r, GROUPS), GROUPS)

    def goes_left(r):
        t = turn(r)
        return (t >= 2) | ((t == 0) & (r < HALF))

    def goes_right(r):
        t = turn(r)
        return (t <= 1) | ((t == 3) & (r >= HALF))

    def between(r):
        t = turn(r)
        return (t == 1) | (t == 2)

    def has_next(r):
        t = turn(r)
        return (t == 1) | (t == 2) | ((t == 3) & (r < HALF))

    def has_prev(r):
        t = turn(r)
        return (t == 1) | (t == 2) | ((t == 0) & (r >= HALF))

    def prev_pair(r):
        t = turn(r)
        return (t == 1) | ((t == 0) & (r >= HALF))

    def xcopy(src, r, recv, to):
        ref = vall.at[src, rows(r), :]
        return remote(ref, ref, v_s, recv, cols=to)

    def arrived(sem, ref):
        pltpu.make_async_copy(ref, ref, sem).wait()

    def several(count):
        return vall.at[0, :count * BLOCK, :]

    def keep_split(src, r):
        high, low = split(vall[src, rows(r), :])
        vhl[src, rows(r), :WIDTH] = high
        vhl[src, rows(r), WIDTH:] = low

    def image(r):
        tiles = []
        for s in range(SLOTS):
            rel = lax.rem(col_index[r, s] - base, NBLK)
            tiles.append(win_hl[lax.min(rel, 3 * ROW_BLOCKS - 1)])
        quad = dot(cov_hl[r], jnp.concatenate(tiles, axis=0))
        vall[g, rows(r), :] = quarters(quad, BLOCK, WIDTH)

        @pl.when(goes_left(r))
        def _():
            xcopy(g, r, next_r.at[r], g_prev).start()

        @pl.when(goes_right(r))
        def _():
            xcopy(g, r, prev_r.at[r], g_next).start()

    for j in range(ROW_BLOCKS):
        r = turn_row(j)
        arrived(halo_r.at[j], win.at[0, pl.ds(0, BLOCK), :])
        split_window(far_side, r)
        image(r)
        if j == 0:
            pl.semaphore_wait(word.at[0], 2)
            tell(word.at[2], next_z)
        if j == 3:
            pl.semaphore_wait(word.at[2], 2)
            tell(word.at[3], near_y)

    pl.semaphore_wait(word.at[3], 2)
    tell(word.at[4], near_y)

    def place(kind, block):
        for core in range(CORES):
            part = block[core * WIDTH // CORES:(core + 1) * WIDTH // CORES]
            tb[core, kind * TILES_G:(kind + 1) * TILES_G] = part.reshape(TILES_G, 8, WIDTH)

    def core_sum(kind):
        part = pl.ds(kind * TILES_G, TILES_G)
        send, recv = p1_s, p1_r.at[kind]
        copy = remote(tb.at[1 - c, part], r1.at[part], send, recv, pts=sibling)
        return copy, part

    def scatter(y_to, far):
        to = y_to * ZS + lax.rem(z + far, ZS)
        return remote(s1.at[to], r2.at[here], p2_s, p2_r, pts=device(to))

    def scatter_rows(y_to):
        for far in NEAR_LAST[:-1]:
            scatter(y_to, far).start()

        @pl.when(y != y_to)
        def _():
            scatter(y_to, 0).start()

    def scatter_prev(z_to):
        return remote(s1.at[TILES_G + z_to], r3.at[here], p2_s, p3_r, cols=g_prev, pts=device(z_to))

    def sum_tile():
        arrived(p2_r, r2.at[pl.ds(1, PLANE - 1)])
        r2[here] = s1[here]
        gb[g, c, here] = jnp.sum(r2[...], axis=0)

        @pl.when(y == 0)
        def _():
            arrived(p3_r, r3)
            gb[g, c, here] += jnp.sum(r3[...], axis=0)

        ref = gb.at[g, c, here]
        for over in (2, 1, 3, 0):
            for far in NEAR_LAST:
                if over or far:
                    to = lax.rem(y + over, YS) * ZS + lax.rem(z + far, ZS)
                    remote(ref, ref, p4_s, p4_r.at[y], pts=device(to)).start()

    acc[...] = jnp.zeros_like(acc)
    acc2[...] = jnp.zeros_like(acc2)
    for r in range(ROW_BLOCKS):
        keep_split(g, r)
    place(3, quarters(dot_t(vhl[g], vhl[g]), WIDTH, WIDTH))
    own_core, own_part = core_sum(3)
    own_core.start()

    for j in range(ROW_BLOCKS):
        r = turn_row(j)

        @pl.when(has_next(r))
        def _():
            arrived(next_r.at[r], several(1))
            keep_split(g_next, r)

        @pl.when(has_prev(r))
        def _():
            arrived(prev_r.at[r], several(1))
            keep_split(g_prev, r)

        @pl.when(between(r))
        def _():
            left = jnp.concatenate([vhl[g, rows(r), :], vhl[g_prev, rows(r), :]], axis=1)
            acc[...] += dot_t(left, vhl[g_next, rows(r), :])

        @pl.when((turn(r) == 3) & (r < HALF))
        def _():
            acc[:2 * WIDTH] += dot_t(vhl[g, rows(r), :], vhl[g_next, rows(r), :])

        @pl.when(prev_pair(r))
        def _():
            acc2[...] += dot_t(vhl[g_prev, rows(r), :], vhl[g, rows(r), :])

        if j == 2:
            own_core.wait_recv()
            s1[own_part] = tb[c, own_part] + r1[own_part]
            pl.semaphore_wait(word.at[4], 2)
            tell(word.at[5], near_x)
            scatter_rows(YS - 1)

    place(0, quarters(acc[:2 * WIDTH], WIDTH, WIDTH))
    place(1, quarters(acc2[...], WIDTH, WIDTH))
    place(2, quarters(acc[2 * WIDTH:], WIDTH, WIDTH))

    late = [core_sum(kind) for kind in (1, 0, 2)]
    for copy, _ in late:
        copy.start()
    pl.semaphore_wait(word.at[5], 2)
    for (copy, tiles_of), y_to in zip(late, (None, 0, 2)):
        copy.wait_recv()
        s1[tiles_of] = tb[c, tiles_of] + r1[tiles_of]
        if y_to is None:
            for far in NEAR_LAST:
                scatter_prev(lax.rem(z + far, ZS)).start()
        else:
            scatter_rows(y_to)

    for r in range(ROW_BLOCKS):
        @pl.when(jnp.logical_not(goes_left(r)))
        def _():
            xcopy(g, r, rest_r.at[0], g_prev).start()

        @pl.when(jnp.logical_not(goes_right(r)))
        def _():
            xcopy(g, r, rest_r.at[1], g_next).start()

        @pl.when(between(r))
        def _():
            xcopy(g_prev, r, rest_r.at[2], g_next).start()
            xcopy(g_next, r, rest_r.at[3], g_prev).start()

    @pl.when(y != 1)
    def _():
        sum_tile()

    pl.semaphore_wait(word.at[1], 2)

    def of_set(n):
        return pl.ds(n * TILES_G, TILES_G)

    def x_share(k, n):
        ref = gb.at[g, c, of_set(n)]
        return remote(ref, ref, p5_s, p5_r.at[GROUPS - 1 - k, {3: 0, 0: 1, 2: 2}[n]], cols=lax.rem(g + k, GROUPS))

    def core_share(k, n):
        ref = gb.at[lax.rem(g + k, GROUPS), c, of_set(n)]
        return remote(ref, ref, p6_s, p6_r.at[n], pts=sibling)

    for n in (3, 0, 2):
        @pl.when(y == n)
        def _():
            arrived(p4_r.at[n], gb.at[g, c, pl.ds(0, TILES_G - 1)])

        @pl.when(y != n)
        def _():
            arrived(p4_r.at[n], gb.at[g, c, pl.ds(0, TILES_G)])

        for k in (2, 1, 3):
            x_share(k, n).start()
        core_share(0, n).start()

    def pass_to_core(n):
        for k in (1, 3, 2):
            arrived(p5_r.at[k - 1, {3: 0, 0: 1, 2: 2}[n]], gb.at[g, c, of_set(n)])
            core_share(k, n).start()

    def whole(n):
        arrived(p6_r.at[n], gb.at[:, 1 - c, of_set(n)])

    def part(a, kind):
        return jnp.concatenate(
            [gb[a, core, kind * TILES_G:(kind + 1) * TILES_G].reshape(WIDTH // CORES, WIDTH) for core in range(CORES)], axis=0
        )

    pass_to_core(3)
    pass_to_core(0)
    arrived(rest_r.at[0], several(3))
    arrived(rest_r.at[1], several(3))
    arrived(rest_r.at[2], several(4))
    arrived(rest_r.at[3], several(4))
    for r in range(ROW_BLOCKS):
        keep_split(g_opp, r)

        @pl.when(jnp.logical_not(has_next(r)))
        def _():
            keep_split(g_next, r)

        @pl.when(jnp.logical_not(has_prev(r)))
        def _():
            keep_split(g_prev, r)

    whole(3)
    diag = [part(a, 3) for a in range(GROUPS)]
    down = [lax.rsqrt(jnp.sum(d * eye, axis=1, keepdims=True)) for d in diag]
    across = [lax.rsqrt(jnp.sum(d * eye, axis=0, keepdims=True)) for d in diag]

    def put(a, h, block):
        block = block * down[a] * across[h]
        nat[a, h] = block - eye if a == h else block

    for a in range(GROUPS):
        put(a, a, diag[a])
    pass_to_core(2)
    whole(0)
    for a in range(GROUPS):
        h = (a + 1) % GROUPS
        block = part(a, 0)
        put(a, h, block)
        put(h, a, block.T)
    whole(2)
    for a in range(GROUPS // 2):
        h = a + GROUPS // 2
        block = part((a + 1) % GROUPS, 2) + part((a + 3) % GROUPS, 2).T
        put(a, h, block)
        put(h, a, block.T)

    side = COLS // 2
    first, second = slice(0, side), slice(side, COLS)
    parts = ((first, first), (first, second), (second, second))
    down_id = lax.broadcasted_iota(jnp.int32, (side, side), 0)
    across_id = lax.broadcasted_iota(jnp.int32, (side, side), 1)
    half_eye = jnp.where(down_id == across_id, 0.5, 0.0).astype(F32)
    upper = jnp.where(down_id < across_id, 1.0, 0.0).astype(F32) + half_eye
    w_h[second, first] = jnp.zeros((side, side), BF16)
    for t in range(GROUPS):
        for v in range(GROUPS):
            block = nat[order[t], order[v]]
            at = (slice(t * WIDTH, (t + 1) * WIDTH), slice(v * WIDTH, (v + 1) * WIDTH))
            high, low = split(block)
            e0_h[at] = high
            e0_l[at] = low
            e0[at] = block
    for m, n in parts:
        block = e0[m, n] if m != n else upper * e0[m, n]
        w_h[m, n] = (-block).astype(BF16)

    def newton(w_h, next_h, fine):
        for m, n in parts:
            depth = first if n == first else slice(0, COLS)
            prod = dot(e0_h[m, depth], w_h[depth, n])
            if fine:
                prod += dot(e0_l[m, depth], w_h[depth, n])
            value = (e0[m, n] + w_h[m, n].astype(F32)) + prod
            b[m, n] = value
            high, low = split(value)
            b_h[m, n] = high
            if fine:
                b_l[m, n] = low
        for m, n in parts:
            depth = first if m == first else slice(0, COLS)
            prod = dot_t(w_h[depth, m], b_h[depth, n])
            if fine:
                prod += dot_t(w_h[depth, m], b_l[depth, n])
            value = b[m, n] + prod
            if m == n:
                value = upper * value + half_eye * w_h[m, n].astype(F32)
            if fine:
                for k in range(2):
                    u_by[(2 if n == second else 0) + k, m] = value[:, k * WIDTH:(k + 1) * WIDTH]
                res[...] += jnp.sum((value * value).reshape(side // 8, 8, side), axis=0)
            else:
                u[m, n] = value
                u_h[m, n] = value.astype(BF16)
        if fine:
            return
        next_h[second, first] = jnp.zeros((side, side), BF16)
        for m, n in parts:
            depth = slice(m.start, n.stop)
            value = (w_h[m, n].astype(F32) - u[m, n]) - dot(w_h[m, depth], u_h[depth, n])
            high = value.astype(BF16)
            next_h[m, n] = high
            for k in range(2):
                w_by[(2 if n == second else 0) + k, m] = high[:, k * WIDTH:(k + 1) * WIDTH]

    res[...] = jnp.zeros_like(res)
    for k in range(2):
        u_by[k, second] = jnp.zeros((side, WIDTH), F32)
        w_by[k, second] = jnp.zeros((side, WIDTH), BF16)
    newton(w_h, w2_h, False)
    newton(w2_h, None, True)
    small[0, 0] = jnp.where(jnp.sum(res[...]) < TOLERANCE, 1, 0).astype(jnp.int32)

    rank = jnp.int32(0)
    for t in range(1, GROUPS):
        rank += jnp.where(order[t] == g, t, 0)
    rank = lax.min(rank, GROUPS - 1)
    step = u_by[rank]
    inverse = (w_by[rank].astype(F32) - step) - dot(w2_h[...], step.astype(BF16))
    for t in range(GROUPS):
        inv[t] = inverse[t * WIDTH:(t + 1) * WIDTH]
    for a in range(GROUPS):
        rows_a = slice(a * WIDTH, (a + 1) * WIDTH)
        same = jnp.where(g == a, 1.0, 0.0).astype(F32)
        high, low = split(down[a] * (inv[ranks[a]] + same * eye))
        x_hl[rows_a, :WIDTH] = high
        x_hl[rows_a, WIDTH:] = low

    for k in range(ROW_BLOCKS // 2):
        rows_k = slice(k * 2 * BLOCK, (k + 1) * 2 * BLOCK)
        high = jnp.concatenate([vhl[h, rows_k, :WIDTH] for h in range(GROUPS)], axis=1)
        low = jnp.concatenate([vhl[h, rows_k, WIDTH:] for h in range(GROUPS)], axis=1)
        q = dot(jnp.concatenate([high, low], axis=0), x_hl[...])
        out[rows_k, :] = quarters(q, 2 * BLOCK, WIDTH)

    arrived(halo_s, win.at[0])
    to_near.wait_send()
    arrived(v_s, vall.at[:3])
    arrived(p1_s, tb.at[0])
    arrived(p2_s, s1.at[pl.ds(0, TILES - 1)])

    @pl.when(y == 1)
    def _():
        arrived(p2_s, s1.at[pl.ds(0, 1)])

    @pl.when(y != 1)
    def _():
        arrived(p4_s, r2.at[pl.ds(0, PLANE - 1)])

    arrived(p5_s, gb.at[:3, 0, pl.ds(0, TILES - TILES_G)])
    arrived(p6_s, gb.at[:, 0, pl.ds(0, TILES - TILES_G)])


def fast(start, cov_blocks, col_index, order):
    dma = pltpu.SemaphoreType.DMA
    square = (COLS, COLS)
    hbm = pl.BlockSpec(memory_space=pl.ANY)
    smem = pl.BlockSpec(memory_space=pltpu.SMEM)
    return pl.pallas_call(
        kernel,
        out_shape=(
            pltpu.VMEM((ROWS, WIDTH), F32),
            pltpu.SMEM((1, 1), jnp.int32),
        ),
        in_specs=[hbm, hbm, hbm, hbm],
        out_specs=(pl.BlockSpec(memory_space=pltpu.VMEM), smem),
        scratch_shapes=[
            pltpu.SMEM((ROW_BLOCKS, SLOTS), jnp.int32),
            pltpu.SMEM((GROUPS,), jnp.int32),
            pltpu.VMEM((3, ROWS, WIDTH), F32),
            pltpu.VMEM((3 * ROW_BLOCKS, BLOCK, 2 * WIDTH), BF16),
            pltpu.VMEM((ROW_BLOCKS, SLOTS, BLOCK, BLOCK), F32),
            pltpu.VMEM((ROW_BLOCKS, 2 * BLOCK, SLOTS * BLOCK), BF16),
            pltpu.VMEM((GROUPS, ROWS, WIDTH), F32),
            pltpu.VMEM((GROUPS, ROWS, 2 * WIDTH), BF16),
            pltpu.VMEM((4 * WIDTH, 2 * WIDTH), F32),
            pltpu.VMEM((2 * WIDTH, 2 * WIDTH), F32),
            pltpu.VMEM((CORES, TILES, 8, WIDTH), F32),
            pltpu.VMEM((TILES, 8, WIDTH), F32),
            pltpu.VMEM((TILES, 8, WIDTH), F32),
            pltpu.VMEM((PLANE, 8, WIDTH), F32),
            pltpu.VMEM((PLANE, 8, WIDTH), F32),
            pltpu.VMEM((GROUPS, CORES, TILES, 8, WIDTH), F32),
            pltpu.VMEM((GROUPS, GROUPS, WIDTH, WIDTH), F32),
            pltpu.VMEM(square, F32),
            pltpu.VMEM(square, F32),
            pltpu.VMEM(square, F32),
            pltpu.VMEM(square, BF16),
            pltpu.VMEM(square, BF16),
            pltpu.VMEM(square, BF16),
            pltpu.VMEM(square, BF16),
            pltpu.VMEM(square, BF16),
            pltpu.VMEM(square, BF16),
            pltpu.VMEM(square, BF16),
            pltpu.VMEM((GROUPS, COLS, WIDTH), BF16),
            pltpu.VMEM((GROUPS, COLS, WIDTH), F32),
            pltpu.VMEM((GROUPS, WIDTH, WIDTH), F32),
            pltpu.VMEM((COLS, 2 * WIDTH), BF16),
            pltpu.VMEM((8, COLS // 2), F32),
            pltpu.SemaphoreType.REGULAR((6,)),
            dma((2,)),
            dma, dma,
            dma, dma((ROW_BLOCKS,)), dma, dma,
            dma, dma((ROW_BLOCKS,)), dma((ROW_BLOCKS,)), dma((4,)),
            dma, dma((KINDS,)),
            dma, dma, dma,
            dma, dma((KINDS,)),
            dma, dma((GROUPS - 1, KINDS - 1)),
            dma, dma((KINDS,)),
        ],
        compiler_params=pltpu.CompilerParams(
            collective_id=0, has_side_effects=True, vmem_limit_bytes=56 * 1024 * 1024
        ),
    )(start, cov_blocks, col_index, order)


def body(start, cov_blocks, col_index, order):
    result, small = fast(start, cov_blocks, col_index, order)
    return lax.cond(
        small[0, 0] == 1,
        lambda: result,
        lambda: careful(start, cov_blocks, col_index, order),
    )


def solution(mesh):
    placed = (P("pts", "cols"), P("pts", None, None, None), P("pts", None), P())
    return jax.shard_map(
        body, mesh=mesh, in_specs=placed, out_specs=P("pts", "cols"), check_vma=False
    )
```

```python
import jax
import jax.numpy as jnp
from jax import lax
from jax.experimental import pallas as pl
from jax.experimental.pallas import tpu as pltpu
from jax.sharding import PartitionSpec as P

MESH = pl.DeviceIdType.MESH
F32 = jnp.float32
BF16 = jnp.bfloat16
GROUPS = 4
WIDTH = 128
BLOCK = 128
ROW_BLOCKS = 8
SLOTS = 8
NBLK = 512
YS, ZS, CORES = 4, 8, 2
COLS = GROUPS * WIDTH
ROWS = ROW_BLOCKS * BLOCK
HALF = ROW_BLOCKS // 2
PLANE = YS * ZS
TILES_G = WIDTH // CORES // 8
KINDS = 4
TILES = KINDS * TILES_G
NEAR_LAST = (4, 3, 5, 2, 6, 1, 7, 0)
TOLERANCE = 4e-4


def total(value, axis):
    distance = 1
    while distance < lax.axis_size(axis):
        pairs = [(i, i ^ distance) for i in range(lax.axis_size(axis))]
        value = value + lax.ppermute(value, axis, pairs)
        distance *= 2
    return value


def broadcast(value, axis, source):
    kept = jnp.where(lax.axis_index(axis) == source, value, 0).astype(value.dtype)
    return total(kept, axis)


def with_halo(cells, axis, width):
    count = lax.axis_size(axis)
    head = lax.slice_in_dim(cells, 0, width, axis=0)
    tail = lax.slice_in_dim(cells, cells.shape[0] - width, cells.shape[0], axis=0)
    return jnp.concatenate(
        [
            lax.ppermute(tail, axis, [(i, (i + 1) % count) for i in range(count)]),
            cells,
            lax.ppermute(head, axis, [((i + 1) % count, i) for i in range(count)]),
        ],
        axis=0,
    )


def inner(left, right):
    return lax.dot_general(
        left,
        right,
        (((0,), (0,)), ((), ())),
        precision=lax.Precision.HIGHEST,
        preferred_element_type=F32,
    )


def careful(start, cov_blocks, col_index, order):
    rows, group_size = start.shape
    blocks_dev = cov_blocks.shape[0]
    block = cov_blocks.shape[2]
    total_blocks = blocks_dev * lax.axis_size("pts")
    groups = lax.axis_size("cols")
    mine = lax.axis_index("cols")
    positions = jnp.arange(groups, dtype=jnp.int32)
    rank = jnp.sum(jnp.where(order == mine, positions, 0))
    first_block = lax.axis_index("pts") * blocks_dev - blocks_dev
    relative = jnp.mod(col_index - first_block, total_blocks)
    tiles = with_halo(start, "pts", rows).reshape(3 * blocks_dev, block, group_size)[relative]
    local = jnp.einsum(
        "rsab,rsbk->rak", cov_blocks, tiles, precision=lax.Precision.HIGHEST
    ).reshape(rows, group_size)

    def step(t, local):
        owner = order[t]
        gram = total(inner(local, local), "pts")
        lower = jnp.linalg.cholesky(gram)
        candidate = lax.linalg.triangular_solve(
            lower, local, left_side=False, lower=True, transpose_a=True
        )
        ortho = broadcast(candidate, "cols", owner)
        coef = total(inner(ortho, local), "pts")
        updated = local - jnp.dot(
            ortho, coef, precision=lax.Precision.HIGHEST, preferred_element_type=F32
        )
        return jnp.where(rank > t, updated, jnp.where(mine == owner, ortho, local))

    return lax.fori_loop(0, groups, step, local)


def split(x):
    high = x.astype(BF16)
    return high, (x - high.astype(F32)).astype(BF16)


def quarters(q, m, n):
    return (q[:m, :n] + q[m:, n:]) + (q[:m, n:] + q[m:, :n])


def dot(a, b):
    return jnp.dot(a, b, preferred_element_type=F32)


def dot_t(a, b):
    return lax.dot_general(a, b, (((0,), (0,)), ((), ())), preferred_element_type=F32)


def kernel(
    start, cov, col_in, order_in, out, small,
    col_index, order,
    win, win_hl, covv, cov_hl, vall, vhl, acc, acc2, tb, r1, s1, r2, r3, gb,
    nat, e0, b, u, e0_h, e0_l, w_h, w2_h, b_h, b_l, u_h, w_by, u_by, inv, x_hl, res,
    word, i_sem, c_sem, l_sem,
    halo_s, halo_r, n_s, n_r, v_s, next_r, prev_r, rest_r,
    p1_s, p1_r, p2_s, p2_r, p3_r, p4_s, p4_r, p5_s, p5_r, p6_s, p6_r,
):
    p = lax.axis_index("pts")
    g = lax.axis_index("cols")
    npts = YS * ZS * CORES
    c = lax.rem(p, CORES)
    z = lax.rem(lax.div(p, CORES), ZS)
    y = lax.div(p, CORES * ZS)
    before, after = lax.rem(p + npts - 1, npts), lax.rem(p + 1, npts)
    sibling = p + 1 - 2 * c
    g_next, g_prev, g_opp = (lax.rem(g + k, GROUPS) for k in (1, 3, 2))

    here = y * ZS + z

    def peer(k):
        y_to, z_to = lax.rem(y + lax.div(k, ZS), YS), lax.rem(z + lax.rem(k, ZS), ZS)
        return y_to * ZS + z_to

    def device(chip):
        return chip * CORES + c

    def remote(src, dst, send, recv, **where):
        return pltpu.make_async_remote_copy(
            src_ref=src, dst_ref=dst, send_sem=send, recv_sem=recv,
            device_id=where, device_id_type=MESH,
        )

    barrier = pltpu.get_barrier_semaphore()
    near_x = [dict(cols=h) for h in (g_next, g_prev)]
    near_z = [dict(pts=device(peer(k))) for k in (1, ZS - 1)]
    near_y = [dict(pts=device(peer(k))) for k in (ZS, (YS - 1) * ZS)]
    next_z = [dict(pts=device(peer(k))) for k in (2, ZS - 2)]
    neighbours = [dict(pts=before), dict(pts=after)] + near_x + near_z + near_y

    def tell(sem, devices):
        for one in devices:
            pl.semaphore_signal(sem, inc=1, device_id=one, device_id_type=MESH)

    tell(barrier, neighbours)

    cov_copy = pltpu.make_async_copy(cov, covv, c_sem)
    own_copy = pltpu.make_async_copy(start, win.at[1], l_sem)
    own_copy.start()
    col_copy = pltpu.make_async_copy(col_in, col_index, i_sem.at[0])
    col_copy.start()
    order_copy = pltpu.make_async_copy(order_in, order, i_sem.at[1])
    order_copy.start()

    pl.semaphore_wait(barrier, len(neighbours))
    tell(word.at[0], near_z)
    tell(word.at[1], near_x)

    def turn_row(j):
        return ROW_BLOCKS - 1 - j + c * (2 * j - ROW_BLOCKS + 1)

    def rows(r):
        return pl.ds(pl.multiple_of(r * BLOCK, BLOCK), BLOCK)

    far_side, near_side = 2 * c, 2 - 2 * c
    far_device = before + c * (after - before)

    def to_far(j):
        block = rows(ROW_BLOCKS - 1 - turn_row(j))
        return remote(start.at[block, :], win.at[near_side, block, :], halo_s, halo_r.at[j], pts=far_device)

    to_near = remote(start, win.at[far_side], n_s, n_r, pts=sibling)
    to_far(0).start()
    to_near.start()
    for j in range(1, ROW_BLOCKS):
        to_far(j).start()
    cov_copy.start()

    col_copy.wait()
    order_copy.wait()
    ranks = []
    for a in range(GROUPS):
        rank = jnp.int32(0)
        for t in range(1, GROUPS):
            rank += jnp.where(order[t] == a, t, 0)
        ranks.append(lax.min(rank, GROUPS - 1))
    row_id = lax.broadcasted_iota(jnp.int32, (WIDTH, WIDTH), 0)
    col_id = lax.broadcasted_iota(jnp.int32, (WIDTH, WIDTH), 1)
    eye = (row_id == col_id).astype(F32)

    cov_copy.wait()

    def split_cov(r, carry):
        for s in range(SLOTS):
            high, low = split(covv[r, s])
            cov_hl[r, :BLOCK, s * BLOCK:(s + 1) * BLOCK] = high
            cov_hl[r, BLOCK:, s * BLOCK:(s + 1) * BLOCK] = low
        return carry

    lax.fori_loop(0, ROW_BLOCKS, split_cov, 0)

    def split_window(side, k):
        high, low = split(win[side, rows(k), :])
        win_hl[side * ROW_BLOCKS + k, :, :WIDTH] = high
        win_hl[side * ROW_BLOCKS + k, :, WIDTH:] = low

    def split_own(k, carry):
        split_window(1, k)
        return carry

    def split_near(k, carry):
        split_window(near_side, k)
        return carry

    own_copy.wait()
    lax.fori_loop(0, ROW_BLOCKS, split_own, 0)
    to_near.wait_recv()
    lax.fori_loop(0, ROW_BLOCKS, split_near, 0)

    base = p * ROW_BLOCKS - ROW_BLOCKS - NBLK

    def turn(r):
        return lax.rem(g + GROUPS - lax.rem(r, GROUPS), GROUPS)

    def goes_left(r):
        t = turn(r)
        return (t >= 2) | ((t == 0) & (r < HALF))

    def goes_right(r):
        t = turn(r)
        return (t <= 1) | ((t == 3) & (r >= HALF))

    def between(r):
        t = turn(r)
        return (t == 1) | (t == 2)

    def has_next(r):
        t = turn(r)
        return (t == 1) | (t == 2) | ((t == 3) & (r < HALF))

    def has_prev(r):
        t = turn(r)
        return (t == 1) | (t == 2) | ((t == 0) & (r >= HALF))

    def prev_pair(r):
        t = turn(r)
        return (t == 1) | ((t == 0) & (r >= HALF))

    def xcopy(src, r, recv, to):
        ref = vall.at[src, rows(r), :]
        return remote(ref, ref, v_s, recv, cols=to)

    def arrived(sem, ref):
        pltpu.make_async_copy(ref, ref, sem).wait()

    def several(count):
        return vall.at[0, :count * BLOCK, :]

    def keep_split(src, r):
        high, low = split(vall[src, rows(r), :])
        vhl[src, rows(r), :WIDTH] = high
        vhl[src, rows(r), WIDTH:] = low

    def image(r):
        tiles = []
        for s in range(SLOTS):
            rel = lax.rem(col_index[r, s] - base, NBLK)
            tiles.append(win_hl[lax.min(rel, 3 * ROW_BLOCKS - 1)])
        quad = dot(cov_hl[r], jnp.concatenate(tiles, axis=0))
        vall[g, rows(r), :] = quarters(quad, BLOCK, WIDTH)

        @pl.when(goes_left(r))
        def _():
            xcopy(g, r, next_r.at[r], g_prev).start()

        @pl.when(goes_right(r))
        def _():
            xcopy(g, r, prev_r.at[r], g_next).start()

    for j in range(ROW_BLOCKS):
        r = turn_row(j)
        arrived(halo_r.at[j], win.at[0, pl.ds(0, BLOCK), :])
        split_window(far_side, r)
        image(r)
        if j == 0:
            pl.semaphore_wait(word.at[0], 2)
            tell(word.at[2], next_z)
        if j == 3:
            pl.semaphore_wait(word.at[2], 2)
            tell(word.at[3], near_y)

    pl.semaphore_wait(word.at[3], 2)
    tell(word.at[4], near_y)

    def place(kind, block):
        for core in range(CORES):
            part = block[core * WIDTH // CORES:(core + 1) * WIDTH // CORES]
            tb[core, kind * TILES_G:(kind + 1) * TILES_G] = part.reshape(TILES_G, 8, WIDTH)

    def core_sum(kind):
        part = pl.ds(kind * TILES_G, TILES_G)
        send, recv = p1_s, p1_r.at[kind]
        copy = remote(tb.at[1 - c, part], r1.at[part], send, recv, pts=sibling)
        return copy, part

    def scatter(y_to, far):
        to = y_to * ZS + lax.rem(z + far, ZS)
        return remote(s1.at[to], r2.at[here], p2_s, p2_r, pts=device(to))

    def scatter_rows(y_to):
        for far in NEAR_LAST[:-1]:
            scatter(y_to, far).start()

        @pl.when(y != y_to)
        def _():
            scatter(y_to, 0).start()

    def scatter_prev(z_to):
        return remote(s1.at[TILES_G + z_to], r3.at[here], p2_s, p3_r, cols=g_prev, pts=device(z_to))

    def sum_tile():
        arrived(p2_r, r2.at[pl.ds(1, PLANE - 1)])
        r2[here] = s1[here]
        gb[g, c, here] = jnp.sum(r2[...], axis=0)

        @pl.when(y == 0)
        def _():
            arrived(p3_r, r3)
            gb[g, c, here] += jnp.sum(r3[...], axis=0)

        ref = gb.at[g, c, here]
        for over in (2, 1, 3, 0):
            for far in NEAR_LAST:
                if over or far:
                    to = lax.rem(y + over, YS) * ZS + lax.rem(z + far, ZS)
                    remote(ref, ref, p4_s, p4_r.at[y], pts=device(to)).start()

    acc[...] = jnp.zeros_like(acc)
    acc2[...] = jnp.zeros_like(acc2)
    for r in range(ROW_BLOCKS):
        keep_split(g, r)
    place(3, quarters(dot_t(vhl[g], vhl[g]), WIDTH, WIDTH))
    own_core, own_part = core_sum(3)
    own_core.start()

    for j in range(ROW_BLOCKS):
        r = turn_row(j)

        @pl.when(has_next(r))
        def _():
            arrived(next_r.at[r], several(1))
            keep_split(g_next, r)

        @pl.when(has_prev(r))
        def _():
            arrived(prev_r.at[r], several(1))
            keep_split(g_prev, r)

        @pl.when(between(r))
        def _():
            left = jnp.concatenate([vhl[g, rows(r), :], vhl[g_prev, rows(r), :]], axis=1)
            acc[...] += dot_t(left, vhl[g_next, rows(r), :])

        @pl.when((turn(r) == 3) & (r < HALF))
        def _():
            acc[:2 * WIDTH] += dot_t(vhl[g, rows(r), :], vhl[g_next, rows(r), :])

        @pl.when(prev_pair(r))
        def _():
            acc2[...] += dot_t(vhl[g_prev, rows(r), :], vhl[g, rows(r), :])

        if j == 2:
            own_core.wait_recv()
            s1[own_part] = tb[c, own_part] + r1[own_part]
            pl.semaphore_wait(word.at[4], 2)
            tell(word.at[5], near_x)
            scatter_rows(YS - 1)

    place(0, quarters(acc[:2 * WIDTH], WIDTH, WIDTH))
    place(1, quarters(acc2[...], WIDTH, WIDTH))
    place(2, quarters(acc[2 * WIDTH:], WIDTH, WIDTH))

    late = [core_sum(kind) for kind in (1, 0, 2)]
    for copy, _ in late:
        copy.start()
    pl.semaphore_wait(word.at[5], 2)
    for (copy, tiles_of), y_to in zip(late, (None, 0, 2)):
        copy.wait_recv()
        s1[tiles_of] = tb[c, tiles_of] + r1[tiles_of]
        if y_to is None:
            for far in NEAR_LAST:
                scatter_prev(lax.rem(z + far, ZS)).start()
        else:
            scatter_rows(y_to)

    for r in range(ROW_BLOCKS):
        @pl.when(jnp.logical_not(goes_left(r)))
        def _():
            xcopy(g, r, rest_r.at[0], g_prev).start()

        @pl.when(jnp.logical_not(goes_right(r)))
        def _():
            xcopy(g, r, rest_r.at[1], g_next).start()

        @pl.when(between(r))
        def _():
            xcopy(g_prev, r, rest_r.at[2], g_next).start()
            xcopy(g_next, r, rest_r.at[3], g_prev).start()

    @pl.when(y != 1)
    def _():
        sum_tile()

    pl.semaphore_wait(word.at[1], 2)

    def of_set(n):
        return pl.ds(n * TILES_G, TILES_G)

    def x_share(k, n):
        ref = gb.at[g, c, of_set(n)]
        return remote(ref, ref, p5_s, p5_r.at[GROUPS - 1 - k, {3: 0, 0: 1, 2: 2}[n]], cols=lax.rem(g + k, GROUPS))

    def core_share(k, n):
        ref = gb.at[lax.rem(g + k, GROUPS), c, of_set(n)]
        return remote(ref, ref, p6_s, p6_r.at[n], pts=sibling)

    for n in (3, 0, 2):
        @pl.when(y == n)
        def _():
            arrived(p4_r.at[n], gb.at[g, c, pl.ds(0, TILES_G - 1)])

        @pl.when(y != n)
        def _():
            arrived(p4_r.at[n], gb.at[g, c, pl.ds(0, TILES_G)])

        for k in (2, 1, 3):
            x_share(k, n).start()
        core_share(0, n).start()

    def pass_to_core(n):
        for k in (1, 3, 2):
            arrived(p5_r.at[k - 1, {3: 0, 0: 1, 2: 2}[n]], gb.at[g, c, of_set(n)])
            core_share(k, n).start()

    def whole(n):
        arrived(p6_r.at[n], gb.at[:, 1 - c, of_set(n)])

    def part(a, kind):
        return jnp.concatenate(
            [gb[a, core, kind * TILES_G:(kind + 1) * TILES_G].reshape(WIDTH // CORES, WIDTH) for core in range(CORES)], axis=0
        )

    pass_to_core(3)
    pass_to_core(0)
    arrived(rest_r.at[0], several(3))
    arrived(rest_r.at[1], several(3))
    arrived(rest_r.at[2], several(4))
    arrived(rest_r.at[3], several(4))
    for r in range(ROW_BLOCKS):
        keep_split(g_opp, r)

        @pl.when(jnp.logical_not(has_next(r)))
        def _():
            keep_split(g_next, r)

        @pl.when(jnp.logical_not(has_prev(r)))
        def _():
            keep_split(g_prev, r)

    whole(3)
    diag = [part(a, 3) for a in range(GROUPS)]
    down = [lax.rsqrt(jnp.sum(d * eye, axis=1, keepdims=True)) for d in diag]
    across = [lax.rsqrt(jnp.sum(d * eye, axis=0, keepdims=True)) for d in diag]

    def put(a, h, block):
        block = block * down[a] * across[h]
        nat[a, h] = block - eye if a == h else block

    for a in range(GROUPS):
        put(a, a, diag[a])
    pass_to_core(2)
    whole(0)
    for a in range(GROUPS):
        h = (a + 1) % GROUPS
        block = part(a, 0)
        put(a, h, block)
        put(h, a, block.T)
    whole(2)
    for a in range(GROUPS // 2):
        h = a + GROUPS // 2
        block = part((a + 1) % GROUPS, 2) + part((a + 3) % GROUPS, 2).T
        put(a, h, block)
        put(h, a, block.T)

    side = COLS // 2
    first, second = slice(0, side), slice(side, COLS)
    parts = ((first, first), (first, second), (second, second))
    down_id = lax.broadcasted_iota(jnp.int32, (side, side), 0)
    across_id = lax.broadcasted_iota(jnp.int32, (side, side), 1)
    half_eye = jnp.where(down_id == across_id, 0.5, 0.0).astype(F32)
    upper = jnp.where(down_id < across_id, 1.0, 0.0).astype(F32) + half_eye
    w_h[second, first] = jnp.zeros((side, side), BF16)
    for t in range(GROUPS):
        for v in range(GROUPS):
            block = nat[order[t], order[v]]
            at = (slice(t * WIDTH, (t + 1) * WIDTH), slice(v * WIDTH, (v + 1) * WIDTH))
            high, low = split(block)
            e0_h[at] = high
            e0_l[at] = low
            e0[at] = block
    for m, n in parts:
        block = e0[m, n] if m != n else upper * e0[m, n]
        w_h[m, n] = (-block).astype(BF16)

    def newton(w_h, next_h, fine):
        for m, n in parts:
            depth = first if n == first else slice(0, COLS)
            prod = dot(e0_h[m, depth], w_h[depth, n])
            if fine:
                prod += dot(e0_l[m, depth], w_h[depth, n])
            value = (e0[m, n] + w_h[m, n].astype(F32)) + prod
            b[m, n] = value
            high, low = split(value)
            b_h[m, n] = high
            if fine:
                b_l[m, n] = low
        for m, n in parts:
            depth = first if m == first else slice(0, COLS)
            prod = dot_t(w_h[depth, m], b_h[depth, n])
            if fine:
                prod += dot_t(w_h[depth, m], b_l[depth, n])
            value = b[m, n] + prod
            if m == n:
                value = upper * value + half_eye * w_h[m, n].astype(F32)
            if fine:
                for k in range(2):
                    u_by[(2 if n == second else 0) + k, m] = value[:, k * WIDTH:(k + 1) * WIDTH]
                res[...] += jnp.sum((value * value).reshape(side // 8, 8, side), axis=0)
            else:
                u[m, n] = value
                u_h[m, n] = value.astype(BF16)
        if fine:
            return
        next_h[second, first] = jnp.zeros((side, side), BF16)
        for m, n in parts:
            depth = slice(m.start, n.stop)
            value = (w_h[m, n].astype(F32) - u[m, n]) - dot(w_h[m, depth], u_h[depth, n])
            high = value.astype(BF16)
            next_h[m, n] = high
            for k in range(2):
                w_by[(2 if n == second else 0) + k, m] = high[:, k * WIDTH:(k + 1) * WIDTH]

    res[...] = jnp.zeros_like(res)
    for k in range(2):
        u_by[k, second] = jnp.zeros((side, WIDTH), F32)
        w_by[k, second] = jnp.zeros((side, WIDTH), BF16)
    newton(w_h, w2_h, False)
    newton(w2_h, None, True)
    small[0, 0] = jnp.where(jnp.sum(res[...]) < TOLERANCE, 1, 0).astype(jnp.int32)

    rank = jnp.int32(0)
    for t in range(1, GROUPS):
        rank += jnp.where(order[t] == g, t, 0)
    rank = lax.min(rank, GROUPS - 1)
    step = u_by[rank]
    inverse = (w_by[rank].astype(F32) - step) - dot(w2_h[...], step.astype(BF16))
    for t in range(GROUPS):
        inv[t] = inverse[t * WIDTH:(t + 1) * WIDTH]
    for a in range(GROUPS):
        rows_a = slice(a * WIDTH, (a + 1) * WIDTH)
        same = jnp.where(g == a, 1.0, 0.0).astype(F32)
        high, low = split(down[a] * (inv[ranks[a]] + same * eye))
        x_hl[rows_a, :WIDTH] = high
        x_hl[rows_a, WIDTH:] = low

    for k in range(ROW_BLOCKS // 2):
        rows_k = slice(k * 2 * BLOCK, (k + 1) * 2 * BLOCK)
        high = jnp.concatenate([vhl[h, rows_k, :WIDTH] for h in range(GROUPS)], axis=1)
        low = jnp.concatenate([vhl[h, rows_k, WIDTH:] for h in range(GROUPS)], axis=1)
        q = dot(jnp.concatenate([high, low], axis=0), x_hl[...])
        out[rows_k, :] = quarters(q, 2 * BLOCK, WIDTH)

    arrived(halo_s, win.at[0])
    to_near.wait_send()
    arrived(v_s, vall.at[:3])
    arrived(p1_s, tb.at[0])
    arrived(p2_s, s1.at[pl.ds(0, TILES - 1)])

    @pl.when(y == 1)
    def _():
        arrived(p2_s, s1.at[pl.ds(0, 1)])

    @pl.when(y != 1)
    def _():
        arrived(p4_s, r2.at[pl.ds(0, PLANE - 1)])

    arrived(p5_s, gb.at[:3, 0, pl.ds(0, TILES - TILES_G)])
    arrived(p6_s, gb.at[:, 0, pl.ds(0, TILES - TILES_G)])


def fast(start, cov_blocks, col_index, order):
    dma = pltpu.SemaphoreType.DMA
    square = (COLS, COLS)
    hbm = pl.BlockSpec(memory_space=pl.ANY)
    smem = pl.BlockSpec(memory_space=pltpu.SMEM)
    return pl.pallas_call(
        kernel,
        out_shape=(
            pltpu.VMEM((ROWS, WIDTH), F32),
            pltpu.SMEM((1, 1), jnp.int32),
        ),
        in_specs=[hbm, hbm, hbm, hbm],
        out_specs=(pl.BlockSpec(memory_space=pltpu.VMEM), smem),
        scratch_shapes=[
            pltpu.SMEM((ROW_BLOCKS, SLOTS), jnp.int32),
            pltpu.SMEM((GROUPS,), jnp.int32),
            pltpu.VMEM((3, ROWS, WIDTH), F32),
            pltpu.VMEM((3 * ROW_BLOCKS, BLOCK, 2 * WIDTH), BF16),
            pltpu.VMEM((ROW_BLOCKS, SLOTS, BLOCK, BLOCK), F32),
            pltpu.VMEM((ROW_BLOCKS, 2 * BLOCK, SLOTS * BLOCK), BF16),
            pltpu.VMEM((GROUPS, ROWS, WIDTH), F32),
            pltpu.VMEM((GROUPS, ROWS, 2 * WIDTH), BF16),
            pltpu.VMEM((4 * WIDTH, 2 * WIDTH), F32),
            pltpu.VMEM((2 * WIDTH, 2 * WIDTH), F32),
            pltpu.VMEM((CORES, TILES, 8, WIDTH), F32),
            pltpu.VMEM((TILES, 8, WIDTH), F32),
            pltpu.VMEM((TILES, 8, WIDTH), F32),
            pltpu.VMEM((PLANE, 8, WIDTH), F32),
            pltpu.VMEM((PLANE, 8, WIDTH), F32),
            pltpu.VMEM((GROUPS, CORES, TILES, 8, WIDTH), F32),
            pltpu.VMEM((GROUPS, GROUPS, WIDTH, WIDTH), F32),
            pltpu.VMEM(square, F32),
            pltpu.VMEM(square, F32),
            pltpu.VMEM(square, F32),
            pltpu.VMEM(square, BF16),
            pltpu.VMEM(square, BF16),
            pltpu.VMEM(square, BF16),
            pltpu.VMEM(square, BF16),
            pltpu.VMEM(square, BF16),
            pltpu.VMEM(square, BF16),
            pltpu.VMEM(square, BF16),
            pltpu.VMEM((GROUPS, COLS, WIDTH), BF16),
            pltpu.VMEM((GROUPS, COLS, WIDTH), F32),
            pltpu.VMEM((GROUPS, WIDTH, WIDTH), F32),
            pltpu.VMEM((COLS, 2 * WIDTH), BF16),
            pltpu.VMEM((8, COLS // 2), F32),
            pltpu.SemaphoreType.REGULAR((6,)),
            dma((2,)),
            dma, dma,
            dma, dma((ROW_BLOCKS,)), dma, dma,
            dma, dma((ROW_BLOCKS,)), dma((ROW_BLOCKS,)), dma((4,)),
            dma, dma((KINDS,)),
            dma, dma, dma,
            dma, dma((KINDS,)),
            dma, dma((GROUPS - 1, KINDS - 1)),
            dma, dma((KINDS,)),
        ],
        compiler_params=pltpu.CompilerParams(
            collective_id=0, has_side_effects=True, vmem_limit_bytes=56 * 1024 * 1024
        ),
    )(start, cov_blocks, col_index, order)


def body(start, cov_blocks, col_index, order):
    result, small = fast(start, cov_blocks, col_index, order)
    return lax.cond(
        small[0, 0] == 1,
        lambda: result,
        lambda: careful(start, cov_blocks, col_index, order),
    )


def solution(mesh):
    placed = (P("pts", "cols"), P("pts", None, None, None), P("pts", None), P())
    return jax.shard_map(
        body, mesh=mesh, in_specs=placed, out_specs=P("pts", "cols"), check_vma=False
    )
```
